32 devices in a mesh: seq: 16 (over z, y, x), head: 2 (over core).
Axes of the slice: x: 2, y: 2, z: 4, core: 2. Of those that a mesh axis runs over, the one named last changes fastest.
Arguments:
- tokens: bfloat16 [4096, 2048], P('seq'), may hold values from -6 to 6
- cotangent: bfloat16 [4096, 2048], P('seq'), may hold values from -6 to 6
- g1: bfloat16 [2048], P('seq'), may hold values from 0.5 to 1.5
- w_q: bfloat16 [2048, 1024], P('seq', 'head'), may hold values from -0.125 to 0.125
- w_k: bfloat16 [2048, 256], P('seq', 'head'), may hold values from -0.125 to 0.125
- w_v: bfloat16 [2048, 256], P('seq', 'head'), may hold values from -0.125 to 0.125
- w_o: bfloat16 [1024, 2048], P('head', 'seq'), may hold values from -3 to 3
- w_z: bfloat16 [2048, 3072], P('seq', 'head'), may hold values from -0.125 to 0.125
- w_x: bfloat16 [2048, 3072], P('seq', 'head'), may hold values from -0.125 to 0.125
- w_bc: bfloat16 [2048, 512], P('seq'), may hold values from -0.125 to 0.125
- w_dt: bfloat16 [2048, 48], P('seq', 'head'), may hold values from -0.125 to 0.125
- conv_bc: bfloat16 [4, 512], P(None, 'seq'), may hold values from -3 to 3
- conv_bc_bias: bfloat16 [512], P('seq'), may hold values from -3 to 3
- w_out: bfloat16 [3072, 2048], P('head', 'seq'), may hold values from -0.013671875 to 0.013671875
- g2: bfloat16 [2048], P('seq'), may hold values from 0.5 to 1.5
- w_gate: bfloat16 [2048, 4096], P('seq', 'head'), may hold values from -0.125 to 0.125
- w_up: bfloat16 [2048, 4096], P('seq', 'head'), may hold values from -0.125 to 0.125
- w_down: bfloat16 [4096, 2048], P('head', 'seq'), may hold values from -0.09375 to 0.09375
- conv_x: bfloat16 [4, 3072], P(None, 'head'), may hold values from -3 to 3
- conv_x_bias: bfloat16 [3072], P('head'), may hold values from -3 to 3
- dt_bias: bfloat16 [48], P('head'), may hold values from -8 to -3
- a_log: bfloat16 [48], P('head'), may hold values from -2 to 2
- d_skip: bfloat16 [48], P('head'), may hold values from 0.5 to 1.5
Outputs:
- output: bfloat16 [4096, 2048], P('seq')
- grad_tokens: float32 [4096, 2048], P('seq')
- grad_g1: float32 [2048], P('seq')
- grad_w_q: float32 [2048, 1024], P('seq', 'head')
- grad_w_k: float32 [2048, 256], P('seq', 'head')
- grad_w_v: float32 [2048, 256], P('seq', 'head')
- grad_w_o: float32 [1024, 2048], P('head', 'seq')
- grad_w_z: float32 [2048, 3072], P('seq', 'head')
- grad_w_x: float32 [2048, 3072], P('seq', 'head')
- grad_w_bc: float32 [2048, 512], P('seq')
- grad_w_dt: float32 [2048, 48], P('seq', 'head')
- grad_conv_bc: float32 [4, 512], P(None, 'seq')
- grad_conv_bc_bias: float32 [512], P('seq')
- grad_w_out: float32 [3072, 2048], P('head', 'seq')
- grad_g2: float32 [2048], P('seq')
- grad_w_gate: float32 [2048, 4096], P('seq', 'head')
- grad_w_up: float32 [2048, 4096], P('seq', 'head')
- grad_w_down: float32 [4096, 2048], P('head', 'seq')
- grad_conv_x: float32 [4, 3072], P(None, 'head')
- grad_conv_x_bias: float32 [3072], P('head')
- grad_dt_bias: float32 [48], P('head')
- grad_a_log: float32 [48], P('head')
- grad_d_skip: float32 [48], P('head')
The draws below stay inside these ranges and needn't reach their ends.
All inputs are finite; a program needn't handle non-finite values.
Results may differ from the reference program's by a relative error of at most 0.017.
Values may be sent and summed in bfloat16 or wider, within the bound.
No kernel may reach another device: no remote copies, remote signals or barrier semaphores. Data moves between devices by JAX's collectives and lax.ppermute only.
A program may use at most 320 MiB of HBM per device.

```python
import math
import jax
import jax.numpy as jnp
from jax import lax

D = 2048
FF = 4096
Q_HEADS = 8
KV_HEADS = 2
HEAD_DIM = 128
SSM_HEADS = 48
SSM_DIM = 64
STATE = 256
CONV = 4
TOK_DEV = 256
TOKENS = 4096
INNER = 3072


def with_spikes(values, stream_key, source, target, blocks, factor):
    owner, partner = [(jnp.arange(values.shape[dim]) // (values.shape[dim] // blocks)).reshape([-1 if axis == dim else 1 for axis in range(values.ndim)]) for dim in (source, target)]
    chosen = jax.random.permutation(stream_key, blocks)[partner]
    strong = (owner == chosen) | (owner == (partner + blocks // 2) % blocks)
    return jnp.where(strong, factor * values, values)


def block_scale(stream_key, extent, split, least, top_value):
    def one(axis_at, blocks):
        steps = jax.random.uniform(jax.random.fold_in(jax.random.fold_in(stream_key, 6), axis_at), (blocks,), jnp.float32, least / len(split), top_value / len(split))
        return jnp.repeat(jnp.exp(steps), extent[axis_at] // blocks).reshape((-1,) + (1,) * (len(extent) - axis_at - 1))

    factor_of = one(*split[0])
    for cut in split[1:]:
        factor_of = factor_of * one(*cut)
    return factor_of


def normal_values(rng, extent, width, limit, cuts=(), kind=jnp.bfloat16):
    factor_of = block_scale(rng, extent, cuts, -0.22, 0.18) if cuts else 1.0
    array = jax.random.normal(rng, extent, jnp.float32) * width * factor_of
    return jnp.minimum(jnp.maximum(array, -limit), limit).astype(kind)


def bell_draw_with(rng, dims, deviation, reach, split, heavy, kind=jnp.bfloat16):
    values = deviation * jax.random.normal(rng, dims, jnp.float32)
    if split:
        values = values * block_scale(rng, dims, split, -0.22, 0.18)
    return jnp.clip(with_spikes(values, jax.random.fold_in(rng, 3), *heavy), -reach, reach).astype(kind)


def setup_inputs(seed: int = 0) -> dict:
    splits = jax.random.split(jax.random.key(seed), 24)
    return {
        "tokens": bell_draw_with(splits[0], (TOKENS, D), 1.0, 6.0, ((0, 16),), (0, 1, 16, 2.0)),
        "cotangent": bell_draw_with(splits[1], (TOKENS, D), 1.0, 6.0, ((0, 16),), (0, 1, 16, 2.0)),
        "g1": jnp.clip(1.0 + 0.1 * jax.random.normal(splits[2], (D,), jnp.float32), 0.5, 1.5).astype(jnp.bfloat16),
        "w_q": normal_values(splits[3], (D, Q_HEADS * HEAD_DIM), D ** -0.5, 0.125, ((0, 16), (1, 2))),
        "w_k": normal_values(splits[4], (D, KV_HEADS * HEAD_DIM), D ** -0.5, 0.125, ((0, 16), (1, 2))),
        "w_v": normal_values(splits[5], (D, KV_HEADS * HEAD_DIM), D ** -0.5, 0.125, ((0, 16), (1, 2))),
        "w_o": normal_values(splits[6], (Q_HEADS * HEAD_DIM, D), 4 ** -0.5, 3.0, ((0, 2), (1, 16))),
        "w_z": normal_values(splits[7], (D, INNER), D ** -0.5, 0.125, ((0, 16), (1, 2))),
        "w_x": normal_values(splits[8], (D, INNER), D ** -0.5, 0.125, ((0, 16), (1, 2))),
        "w_bc": normal_values(splits[9], (D, 2 * STATE), D ** -0.5, 0.125, ((0, 16),)),
        "w_dt": normal_values(splits[10], (D, SSM_HEADS), D ** -0.5, 0.125, ((0, 16), (1, 2))),
        "conv_bc": normal_values(splits[11], (CONV, 2 * STATE), CONV ** -0.5, 3.0, ((1, 16),)),
        "conv_bc_bias": normal_values(splits[12], (2 * STATE,), 0.5, 3.0, ((0, 16),)),
        "w_out": normal_values(splits[13], (INNER, D), (64 * INNER) ** -0.5, 0.013671875, ((0, 2), (1, 16))),
        "g2": jnp.clip(1.0 + 0.1 * jax.random.normal(splits[14], (D,), jnp.float32), 0.5, 1.5).astype(jnp.bfloat16),
        "w_gate": normal_values(splits[15], (D, FF), D ** -0.5, 0.125, ((0, 16), (1, 2))),
        "w_up": normal_values(splits[16], (D, FF), D ** -0.5, 0.125, ((0, 16), (1, 2))),
        "w_down": normal_values(splits[17], (FF, D), FF ** -0.5, 0.09375, ((0, 2), (1, 16))),
        "conv_x": normal_values(splits[18], (CONV, INNER), CONV ** -0.5, 3.0, ((1, 2),)),
        "conv_x_bias": normal_values(splits[19], (INNER,), 0.5, 3.0, ((0, 2),)),
        "dt_bias": jnp.clip(-8.0 + 5.0 * jax.random.uniform(splits[20], (SSM_HEADS,), jnp.float32) ** block_scale(splits[20], (SSM_HEADS,), ((0, 2),), -0.2, 0.2), -8.0, -3.0).astype(jnp.bfloat16),
        "a_log": jnp.clip(jax.random.uniform(splits[21], (SSM_HEADS,), jnp.float32, -2.0, 2.0) * block_scale(splits[21], (SSM_HEADS,), ((0, 2),), -0.4, 0.0), -2.0, 2.0).astype(jnp.bfloat16),
        "d_skip": jnp.clip(0.5 + 1.0 * jax.random.uniform(splits[22], (SSM_HEADS,), jnp.float32) ** block_scale(splits[22], (SSM_HEADS,), ((0, 2),), -0.2, 0.2), 0.5, 1.5).astype(jnp.bfloat16),
    }


EPS = 1e-05
ROPE_BASE = 100000000000.0
MASKED = -1e+30
HIGHEST = lax.Precision.HIGHEST

@jax.custom_vjp
def low(v):
    return lax.optimization_barrier(v.astype(jnp.bfloat16)).astype(jnp.float32)

@jax.custom_vjp
def low_back(v):
    return v

def low_keep(v):
    return (low(v), None)

def low_pass(kept, grad):
    return (grad,)

def back_keep(v):
    return (v, None)

def back_low(kept, grad):
    return (low(grad),)
low.defvjp(low_keep, low_pass)
low_back.defvjp(back_keep, back_low)

def matmul_high(left, right):
    return jnp.dot(left, right, precision=HIGHEST)

def normalize(values, gain):
    factor = lax.rsqrt(lax.optimization_barrier(jnp.mean(values * values, -1, keepdims=True)) + EPS)
    return values * factor * gain

def rotate(values, positions, sign):
    half = values.shape[-1] // 2
    freqs = ROPE_BASE ** (-jnp.arange(half, dtype=jnp.float32) / half)
    angle = sign * positions.astype(jnp.float32)[:, None] * freqs[None, :]
    cosine = jnp.cos(angle)[:, None, :]
    sine = jnp.sin(angle)[:, None, :]
    first = values[..., :half]
    second = values[..., half:]
    return jnp.concatenate([first * cosine - second * sine, second * cosine + first * sine], -1)

def causal_conv(inputs, weight, bias):
    length = inputs.shape[0]
    padded = jnp.concatenate([jnp.zeros((CONV - 1, inputs.shape[1]), jnp.float32), inputs], 0)
    total = bias[None, :]
    for tap in range(CONV):
        total = total + weight[tap][None, :] * padded[tap:tap + length]
    return total

def span_state(xc, bmat, dt, logs):
    cum = jnp.cumsum(logs, 0)
    tail = jnp.exp(cum[-1][None, :] - cum) * dt
    local = jnp.einsum('sh,shp,sn->hpn', tail, xc, bmat, precision=HIGHEST)
    return (local, jnp.exp(cum[-1]))

def span_output(xc, bmat, cmat, dt, logs, state_in, d_skip):
    length = xc.shape[0]
    cum = jnp.cumsum(logs, 0)
    diff = cum[:, None, :] - cum[None, :, :]
    order = jnp.arange(length)
    causal = (order[:, None] >= order[None, :])[:, :, None]
    decay = jnp.exp(jnp.where(causal, diff, MASKED))
    inner = matmul_high(cmat, bmat.T)
    mixing = decay * inner[:, :, None] * dt[None, :, :]
    within = jnp.einsum('tsh,shp->thp', mixing, xc, precision=HIGHEST)
    carried = jnp.exp(cum)[:, :, None] * jnp.einsum('tn,hpn->thp', cmat, state_in, precision=HIGHEST)
    return within + carried + d_skip[None, :, None] * xc

def attention(queries, keys, values):
    length = queries.shape[0]
    group = queries.shape[1] // keys.shape[1]
    block = math.gcd(length, 512)
    count = length // block
    grouped = queries.reshape(count, block, keys.shape[1], group, HEAD_DIM)
    key_pos = jnp.arange(length)

    @jax.checkpoint
    def one_block(item):
        query_block, start = item
        scores = jnp.einsum('qgrd,kgd->grqk', query_block, keys, precision=HIGHEST) * HEAD_DIM ** (-0.5)
        scores = low_back(scores)
        query_pos = start + jnp.arange(block)
        scores = jnp.where(key_pos[None, :] <= query_pos[:, None], scores, MASKED)
        probs = low(jax.nn.softmax(scores, axis=-1))
        return jnp.einsum('grqk,kgd->qgrd', probs, values, precision=HIGHEST)
    starts = jnp.arange(count) * block
    result = lax.map(one_block, (grouped, starts))
    return result.reshape(length, -1)

def mamba(z_proj, x_proj, bc_proj, dt_proj, conv_x, conv_x_bias, conv_bc, conv_bc_bias, dt_bias, a_log, d_skip):
    length = x_proj.shape[0]
    xc = jax.nn.silu(causal_conv(x_proj, conv_x, conv_x_bias))
    bc = jax.nn.silu(causal_conv(bc_proj, conv_bc, conv_bc_bias))
    dt = jax.nn.softplus(dt_proj + dt_bias[None, :])
    logs = -dt * jnp.exp(a_log)[None, :]
    blocks = length // TOK_DEV
    pieces = (xc.reshape(blocks, TOK_DEV, SSM_HEADS, SSM_DIM), bc[:, :STATE].reshape(blocks, TOK_DEV, STATE), bc[:, STATE:].reshape(blocks, TOK_DEV, STATE), dt.reshape(blocks, TOK_DEV, SSM_HEADS), logs.reshape(blocks, TOK_DEV, SSM_HEADS))

    @jax.checkpoint
    def step(state, piece):
        xblk, bblk, cblk, dtblk, logblk = piece
        local, decay_total = span_state(xblk, bblk, dtblk, logblk)
        outputs = span_output(xblk, bblk, cblk, dtblk, logblk, state, d_skip)
        return (decay_total[:, None, None] * state + local, outputs)
    start_state = jnp.zeros((SSM_HEADS, SSM_DIM, STATE), jnp.float32)
    _, outputs = lax.scan(step, start_state, pieces)
    return outputs.reshape(length, INNER) * jax.nn.silu(z_proj)

def forward(tokens, g1, w_q, w_k, w_v, w_o, w_z, w_x, w_bc, w_dt, conv_bc, conv_bc_bias, w_out, g2, w_gate, w_up, w_down, conv_x, conv_x_bias, dt_bias, a_log, d_skip):
    length = tokens.shape[0]
    positions = jnp.arange(length)
    n1 = low(normalize(tokens, g1))
    q_proj = low_back(matmul_high(n1, w_q))
    k_proj = low_back(matmul_high(n1, w_k))
    values = low(low_back(matmul_high(n1, w_v))).reshape(length, KV_HEADS, HEAD_DIM)
    queries = low(rotate(q_proj.reshape(length, Q_HEADS, HEAD_DIM), positions, 1.0))
    keys = low(rotate(k_proj.reshape(length, KV_HEADS, HEAD_DIM), positions, 1.0))
    attended = low(low_back(attention(queries, keys, values)))
    z_proj = low_back(matmul_high(n1, w_z))
    x_proj = low_back(matmul_high(n1, w_x))
    bc_proj = low_back(matmul_high(n1, w_bc))
    dt_proj = low_back(matmul_high(n1, w_dt))
    gated = mamba(z_proj, x_proj, bc_proj, dt_proj, conv_x, conv_x_bias, conv_bc, conv_bc_bias, dt_bias, a_log, d_skip)
    gated = low(low_back(gated))
    mixed = low_back(matmul_high(attended, w_o) + matmul_high(gated, w_out))
    hidden = tokens + mixed
    n2 = low(normalize(hidden, g2))
    gate = low_back(matmul_high(n2, w_gate))
    up = low_back(matmul_high(n2, w_up))
    act = low(jax.nn.silu(gate) * up)
    return hidden + matmul_high(act, w_down)

def reference(tokens, cotangent, g1, w_q, w_k, w_v, w_o, w_z, w_x, w_bc, w_dt, conv_bc, conv_bc_bias, w_out, g2, w_gate, w_up, w_down, conv_x, conv_x_bias, dt_bias, a_log, d_skip):
    params = [p.astype(jnp.float32) for p in (g1, w_q, w_k, w_v, w_o, w_z, w_x, w_bc, w_dt, conv_bc, conv_bc_bias, w_out, g2, w_gate, w_up, w_down, conv_x, conv_x_bias, dt_bias, a_log, d_skip)]
    result, back = jax.vjp(forward, tokens.astype(jnp.float32), *params)
    grads = back(cotangent.astype(jnp.float32))
    return (result.astype(jnp.bfloat16), grads[0], grads[1], grads[2], grads[3], grads[4], grads[5], grads[6], grads[7], grads[8], grads[9], grads[10], grads[11], grads[12], grads[13], grads[14], grads[15], grads[16], grads[17], grads[18], grads[19], grads[20], grads[21])
```

```python
import math

import jax
import jax.numpy as jnp
from jax import lax
from jax.sharding import Mesh, PartitionSpec as P

HEAD_DIM = 128
STATE = 256
CONV = 4
EPS = 1e-05
ROPE_BASE = 100000000000.0
MASKED = -1e30
HIGHEST = lax.Precision.HIGHEST
F32 = jnp.float32
B16 = jnp.bfloat16


def after(x, *earlier):
    return lax.optimization_barrier((x, earlier))[0]


def swap_cores(x):
    return lax.ppermute(x, "head", [(0, 1), (1, 0)])


def trade_near(x):
    return lax.all_to_all(x, "near", 0, 0, tiled=True)


def gather_near(x):
    return trade_near(jnp.broadcast_to(x, (lax.axis_size("near"), *x.shape)))


def both_halves(mine, other, dim):
    first = lax.axis_index("head") == 0
    return jnp.concatenate([jnp.where(first, mine, other), jnp.where(first, other, mine)], dim)


def gather_tokens(x):
    half = x.shape[1] // 2
    mine = lax.dynamic_slice_in_dim(x, lax.axis_index("head") * half, half, 1)
    rows = gather_near(mine).reshape(-1, half)
    return both_halves(rows, swap_cores(rows), 1)


def scatter_tokens(partial):
    near = lax.axis_size("near")
    half = partial.shape[1] // 2
    core = lax.axis_index("head")
    give = lax.dynamic_slice_in_dim(partial, (1 - core) * half, half, 1).astype(B16)
    keep = lax.dynamic_slice_in_dim(partial, core * half, half, 1)
    mine = (keep + swap_cores(give).astype(F32)).astype(B16)
    parts = trade_near(mine.reshape(near, -1, half))
    total = jnp.sum(parts.astype(F32), 0)
    return both_halves(total, swap_cores(total), 1)


def ring_route(axis):
    count = lax.axis_size(axis)
    return [(i, (i + 1) % count) for i in range(count)]


def ring_gather(x):
    count, place = lax.axis_size("group"), lax.axis_index("group")
    held = jnp.zeros((count, *x.shape), x.dtype)
    held = lax.dynamic_update_index_in_dim(held, x, place, 0)
    for turn in range(1, count):
        x = lax.ppermute(x, "group", ring_route("group"))
        held = lax.dynamic_update_index_in_dim(held, x, (place - turn) % count, 0)
    return held


def ring_sum(parts):
    count, place = lax.axis_size("group"), lax.axis_index("group")

    def part(turn):
        return lax.dynamic_index_in_dim(parts, (place - 1 - turn) % count, 0, False)

    moving = part(0)
    for turn in range(1, count):
        moving = lax.ppermute(moving, "group", ring_route("group"))
        moving = moving.astype(F32) + part(turn).astype(F32)
        if turn < count - 1:
            moving = moving.astype(B16)
    return moving


def step_group(x, distance):
    count = lax.axis_size("group")
    route = [(i, i + distance) for i in range(count) if 0 <= i + distance < count]
    return lax.ppermute(x, "group", route)


def dot(left, right, dims=((1,), (0,))):
    return lax.dot_general(left, right, (dims, ((), ())), preferred_element_type=F32)


def dot_nt(left, right):
    return dot(left, right, ((1,), (1,)))


def dot_tn(left, right):
    return dot(left, right, ((0,), (0,)))


def exact(spec, *operands):
    return jnp.einsum(spec, *operands, precision=HIGHEST)


def normalize(values, gain):
    factor = lax.rsqrt(jnp.mean(values * values, -1, keepdims=True) + EPS)
    unit = values * factor
    return unit * gain, unit, factor


def norm_back(grad_out, unit, factor, gain):
    grad_unit = grad_out * gain[None, :]
    grad_in = factor * (grad_unit - unit * jnp.mean(grad_unit * unit, -1, keepdims=True))
    return grad_in, jnp.sum(grad_out * unit, 0)


def rope_angles(positions, first, count, half):
    index = first + jnp.arange(count, dtype=F32)
    freqs = ROPE_BASE ** (-index / half)
    return positions.astype(F32), freqs


def rotate_pair(first, second, cosine, sine):
    return first * cosine - second * sine, second * cosine + first * sine


def conv(inputs, edge, weight, bias, dim):
    length = inputs.shape[dim]
    padded = jnp.concatenate([edge, inputs], dim)
    total = bias
    for tap in range(CONV):
        total = total + weight[tap] * lax.slice_in_dim(padded, tap, tap + length, axis=dim)
    return total


def conv_back(grad, grad_edge, inputs, edge, weight, dim):
    length = inputs.shape[dim]
    padded = jnp.concatenate([edge, inputs], dim)
    late = jnp.concatenate([grad, grad_edge], dim)
    total = 0.0
    taps = []
    for tap in range(CONV):
        back = CONV - 1 - tap
        total = total + weight[tap] * lax.slice_in_dim(late, back, back + length, axis=dim)
        taps.append(jnp.sum(grad * lax.slice_in_dim(padded, tap, tap + length, axis=dim), dim))
    return total, jnp.stack(taps), jnp.sum(grad, dim)


def silu_slope(v):
    s = jax.nn.sigmoid(v)
    return s * (1.0 + v * (1.0 - s))


def attention_scores(queries, keys_t, first):
    scores = dot(queries, keys_t) * HEAD_DIM**-0.5
    rows = first + lax.broadcasted_iota(jnp.int32, scores.shape, 0)
    return jnp.where(lax.broadcasted_iota(jnp.int32, scores.shape, 1) <= rows, scores, MASKED)


def attend(queries, keys_t, values_t, first):
    scores = attention_scores(queries, keys_t, first)
    top = jnp.max(scores, 1, keepdims=True)
    probs = jnp.exp(scores - top)
    mass = jnp.sum(probs, 1, keepdims=True)
    out = dot_nt((probs / mass).astype(B16), values_t)
    return out, top + jnp.log(mass)


def attend_back(queries, keys_t, values_t, first, grad, lse, delta):
    probs = jnp.exp(attention_scores(queries, keys_t, first) - lse)
    grad_probs = dot(grad, values_t)
    grad_scores = (probs * (grad_probs - delta)).astype(B16)
    grad_q = dot_nt(grad_scores, keys_t) * HEAD_DIM**-0.5
    grad_kt = dot_tn(queries, grad_scores) * HEAD_DIM**-0.5
    grad_vt = dot_tn(grad, probs.astype(B16))
    return grad_q, grad_kt, grad_vt


def decay_matrix(cum):
    length = cum.shape[-1]
    order = jnp.arange(length)
    causal = order[:, None] >= order[None, :]
    return jnp.exp(jnp.where(causal, cum[..., :, None] - cum[..., None, :], MASKED))


def scan_forward(scaled, bmat, cmat, cum):
    decay = decay_matrix(cum)
    inner = exact("ctn,csn->cts", cmat, bmat)
    within = exact("chts,cshp->cthp", decay * inner[:, None], scaled)
    tail = jnp.exp(cum[..., -1:] - cum)
    added = exact("cshp,csn->chpn", scaled * tail.transpose(0, 2, 1)[..., None], bmat)
    state = jnp.zeros_like(added[0])
    states = []
    for c in range(added.shape[0]):
        states.append(state)
        state = jnp.exp(cum[c, :, -1])[:, None, None] * state + added[c]
    states = jnp.stack(states)
    carried = exact("ctn,chpn->cthp", cmat, states) * jnp.exp(cum).transpose(0, 2, 1)[..., None]
    return within + carried, states, state


def scan_backward(scaled, bmat, cmat, cum, states, state_out, grad, grad_state):
    decay = decay_matrix(cum)
    inner = exact("ctn,csn->cts", cmat, bmat)
    tail = jnp.exp(cum[..., -1:] - cum).transpose(0, 2, 1)[..., None]
    faded = grad * jnp.exp(cum).transpose(0, 2, 1)[..., None]
    grad_scaled = exact("chts,cthp->cshp", decay * inner[:, None], grad)
    grad_inner = jnp.sum(exact("cthp,cshp->chts", grad, scaled) * decay, 1)
    read = exact("cthp,ctn->chpn", faded, cmat)
    count = grad.shape[0]
    grad_states = [None] * count
    grad_last = [None] * count
    following = [*(states[c] for c in range(1, count)), state_out]
    for c in reversed(range(count)):
        grad_states[c] = grad_state
        grad_last[c] = jnp.sum(following[c] * grad_state, (1, 2))
        grad_state = jnp.exp(cum[c, :, -1])[:, None, None] * grad_state + read[c]
    grad_states = jnp.stack(grad_states)
    grad_scaled = grad_scaled + tail * exact("csn,chpn->cshp", bmat, grad_states)
    grad_c = exact("cts,csn->ctn", grad_inner, bmat) + exact("cthp,chpn->ctn", faded, states)
    grad_b = exact("cts,ctn->csn", grad_inner, cmat) + exact(
        "cshp,chpn->csn", scaled * tail, grad_states
    )
    return grad_scaled, grad_b, grad_c, jnp.stack(grad_last)


def per_device(
    tokens,
    cotangent,
    g1,
    w_q,
    w_k,
    w_v,
    w_o,
    w_z,
    w_x,
    w_bc,
    w_dt,
    conv_bc,
    conv_bc_bias,
    w_out,
    g2,
    w_gate,
    w_up,
    w_down,
    conv_x,
    conv_x_bias,
    dt_bias,
    a_log,
    d_skip,
):
    near, groups = lax.axis_size("near"), lax.axis_size("group")
    here, group, core = (lax.axis_index(a) for a in ("near", "group", "head"))
    rows, width = tokens.shape
    span = near * rows
    piece = w_q.shape[0]
    first_position = group * span

    def columns(w):
        return w.reshape(w.shape[0], near, -1).transpose(1, 0, 2)

    def share(x, dim):
        size = x.shape[dim] // near
        return lax.dynamic_slice_in_dim(x, here * size, size, dim)

    smalls = jnp.concatenate([g1, g2, conv_bc.reshape(-1), conv_bc_bias])
    devices = near * groups
    smalls = lax.all_to_all(
        jnp.broadcast_to(smalls, (devices, smalls.shape[0])), ("group", "near"), 0, 0, tiled=True
    ).astype(F32)
    gain1 = smalls[:, :piece].reshape(-1)
    gain2 = smalls[:, piece : 2 * piece].reshape(-1)
    taps_bc = smalls[:, 2 * piece : -conv_bc_bias.shape[0]].reshape(devices, CONV, -1)
    taps_bc = taps_bc.transpose(1, 0, 2).reshape(CONV, 2, near, -1)
    taps_bc = taps_bc[:, core, here][:, :, None]
    bias_bc = smalls[:, -conv_bc_bias.shape[0] :].reshape(2, near, -1)[core, here][:, None]

    key_cols = HEAD_DIM // near
    half_cols = key_cols // 2
    state_cols = STATE // near
    k_cols = w_k.reshape(piece, 2, near, half_cols).transpose(2, 0, 1, 3)
    w_bc_mine = lax.dynamic_slice_in_dim(w_bc, core * STATE, STATE, 1)
    small_cols = [k_cols.reshape(near, piece, key_cols), columns(w_v), columns(w_bc_mine)]
    pack1 = trade_near(jnp.concatenate([columns(w_q), *small_cols, columns(w_x)], 2))
    dt_heads = w_dt.shape[1] // near
    pack_dt = jnp.pad(w_dt.T.reshape(near, dt_heads, piece), ((0, 0), (0, -dt_heads % 8), (0, 0)))
    pack_dt = trade_near(pack_dt).transpose(1, 0, 2).reshape(-1, near * piece)
    all_tokens = gather_tokens(tokens)
    full1 = ring_gather(pack1.reshape(near * piece, -1))
    full_dt = ring_gather(pack_dt)
    pack2 = trade_near(after(columns(w_z), pack1)).reshape(near * piece, -1)
    full_z = ring_gather(after(pack2, full1))
    pack3 = jnp.concatenate([w_o.reshape(near, -1, piece), w_out.reshape(near, -1, piece)], 1)
    pack3 = trade_near(after(pack3, pack2))
    full3 = ring_gather(after(pack3, full_z))
    pack4 = trade_near(after(jnp.concatenate([columns(w_gate), columns(w_up)], 2), pack3))
    full4 = ring_gather(after(pack4.reshape(near * piece, -1), full3))
    pack5 = trade_near(after(w_down.reshape(near, -1, piece), pack4))
    full5 = ring_gather(after(pack5, full4))
    all_cotangent = gather_tokens(after(cotangent, pack5))

    wq_cols = w_q.shape[1] // near
    full1 = full1.reshape(width, -1)
    full_q, full_kvbc, full_x = jnp.split(full1, [wq_cols, wq_cols + 2 * key_cols + state_cols], 1)
    full_dt = full_dt.transpose(1, 0, 2).reshape(-1, width)[:dt_heads]
    full_z = full_z.reshape(width, -1)
    full3 = full3.transpose(2, 0, 1, 3).reshape(-1, width)
    o_rows = w_o.shape[0] // near
    full_o, full_out = full3[:o_rows], full3[o_rows:]
    full4 = full4.reshape(width, -1)
    ff = full4.shape[1] // 2
    full_gate, full_up = full4[:, :ff], full4[:, ff:]
    full_down = full5.transpose(2, 0, 1, 3).reshape(-1, width)

    n1 = normalize(all_tokens.astype(F32), gain1)[0].astype(B16)
    positions = (first_position + jnp.arange(span)).astype(F32)
    half = HEAD_DIM // 2
    freqs = ROPE_BASE ** (-jnp.arange(half, dtype=F32) / half)
    angle = positions[:, None] * freqs[None, :]
    cos_q, sin_q = jnp.cos(angle), jnp.sin(angle)
    cos_k, sin_k = (share(x, 1).T for x in (cos_q, sin_q))

    q_proj = dot(n1, full_q)
    queries = jnp.concatenate(rotate_pair(q_proj[:, :half], q_proj[:, half:], cos_q, sin_q), 1)
    queries = queries.astype(B16)
    kvbc = dot(full_kvbc, n1, ((0,), (1,)))
    k_first, k_second = rotate_pair(kvbc[:half_cols], kvbc[half_cols:key_cols], cos_k, sin_k)
    kv = jnp.concatenate([k_first, k_second, kvbc[key_cols : 2 * key_cols]], 0).astype(B16)
    kv = gather_near(ring_gather(kv))
    keys_t = kv[:, :, :key_cols].reshape(near, groups, 2, half_cols, span)
    keys_t = keys_t.transpose(2, 0, 3, 1, 4).reshape(HEAD_DIM, -1)
    values_t = kv[:, :, key_cols:].transpose(0, 2, 1, 3).reshape(HEAD_DIM, -1)

    bc_proj = kvbc[2 * key_cols :]
    bc_edge = step_group(bc_proj[:, span - CONV + 1 :], 1)
    bc_pre = conv(bc_proj, bc_edge, taps_bc, bias_bc, 1)
    bc_mine = gather_near(jax.nn.silu(bc_pre).astype(B16)).reshape(STATE, span)
    bc_other = swap_cores(bc_mine)
    bc_both = both_halves(bc_mine, bc_other, 0).astype(F32)
    bmat = bc_both[:STATE].reshape(STATE, near, rows).transpose(1, 2, 0)
    cmat = bc_both[STATE:].reshape(STATE, near, rows).transpose(1, 2, 0)

    x_proj = dot(n1, full_x)
    x_edge = step_group(x_proj[span - CONV + 1 :], 1)
    taps_x = share(conv_x, 1).astype(F32)[:, None, :]
    bias_x = share(conv_x_bias, 0).astype(F32)[None, :]
    x_pre = conv(x_proj, x_edge, taps_x, bias_x, 0)
    xc = jax.nn.silu(x_pre)
    inner_cols = xc.shape[1]
    channels = inner_cols // dt_heads
    dt_pre = dot_nt(full_dt, n1) + share(dt_bias, 0).astype(F32)[:, None]
    dt = jax.nn.softplus(dt_pre)
    decay_rate = jnp.exp(share(a_log, 0).astype(F32))[:, None]
    logs = -dt * decay_rate
    skip = share(d_skip, 0).astype(F32)
    chunked = logs.reshape(dt_heads, near, rows).transpose(1, 0, 2)
    triangle = jnp.tril(jnp.ones((rows, rows), F32))
    cum = exact("chs,ts->cht", chunked, triangle)
    xh = xc.reshape(near, rows, dt_heads, channels)
    dt_col = dt.reshape(dt_heads, near, rows).transpose(1, 2, 0)[..., None]
    scaled = xh * dt_col

    outputs, states, state_out = scan_forward(scaled, bmat, cmat, cum)
    chunk_total = cum[..., -1]
    before = jnp.cumsum(chunk_total, 0) - chunk_total
    group_total = jnp.sum(chunk_total, 0)
    all_states = ring_gather(state_out.astype(B16))
    all_totals = ring_gather(jnp.pad(group_total, (0, -dt_heads % 8)))[:, :dt_heads]

    attended32, lse = attend(queries, keys_t, values_t, first_position)
    attended = attended32.astype(B16)

    entering = jnp.zeros_like(state_out)
    for turn in range(groups - 1):
        passed = jnp.exp(all_totals[turn])[:, None, None] * entering + all_states[turn].astype(F32)
        entering = jnp.where(turn < group, passed, entering)
    fade = jnp.exp(cum + before[..., None]).transpose(0, 2, 1)[..., None]
    outputs = outputs + fade * exact("ctn,hpn->cthp", cmat, entering)
    states = states + jnp.exp(before)[:, :, None, None] * entering
    state_out = state_out + jnp.exp(group_total)[:, None, None] * entering
    y = outputs + skip[:, None] * xh
    z_proj = dot(n1, full_z)
    gated = (y.reshape(span, -1) * jax.nn.silu(z_proj)).astype(B16)

    mixed = scatter_tokens(dot(attended, full_o) + dot(gated, full_out))
    hidden = tokens.astype(F32) + mixed
    normed2, unit2, factor2 = normalize(hidden, gain2)
    n2 = gather_tokens(normed2.astype(B16))
    gate, up = dot(n2, full_gate), dot(n2, full_up)
    sigma = jax.nn.sigmoid(gate)
    act = (gate * sigma * up).astype(B16)
    grad_act = dot_nt(all_cotangent, full_down)
    grad_gate = (grad_act * up * sigma * (1.0 + gate * (1.0 - sigma))).astype(B16)
    grad_up = (grad_act * gate * sigma).astype(B16)
    grad_n2 = scatter_tokens(dot_nt(grad_gate, full_gate) + dot_nt(grad_up, full_up))

    def rows_home(grad):
        parts = ring_sum(grad.astype(B16).reshape(groups, near * piece, -1))
        parts = trade_near(parts.astype(B16).reshape(near, piece, -1))
        return parts

    def joined(parts):
        return parts.transpose(1, 0, 2).reshape(piece, -1).astype(F32)

    def cols_home(grad):
        parts = grad.astype(B16).reshape(-1, groups, near * piece).transpose(1, 0, 2)
        parts = ring_sum(parts).astype(B16)
        parts = trade_near(parts.reshape(-1, near, piece).transpose(1, 0, 2))
        return parts.reshape(-1, piece).astype(F32)

    feed = scatter_tokens(dot(act, full_down))
    output = (hidden + feed).astype(B16)
    sum_wgate = joined(rows_home(dot_tn(n2, grad_gate)))
    sum_wup = joined(rows_home(dot_tn(n2, grad_up)))
    sum_wdown = cols_home(dot_tn(act, all_cotangent))

    grad_norm2, grad_g2 = norm_back(grad_n2, unit2, factor2, gain2)
    grad_hidden = cotangent.astype(F32) + grad_norm2
    grad_mixed = gather_tokens(grad_hidden.astype(B16))

    grad_attended = dot_nt(grad_mixed, full_o).astype(B16)
    grad_gated = dot_nt(grad_mixed, full_out).astype(B16).astype(F32)

    sig_z = jax.nn.sigmoid(z_proj)
    grad_y = grad_gated * z_proj * sig_z
    grad_z = (grad_gated * y.reshape(span, -1) * sig_z * (1.0 + z_proj * (1.0 - sig_z))).astype(B16)
    grad_y = grad_y.reshape(near, rows, dt_heads, channels)
    read = exact("cthp,ctn->hpn", grad_y * fade, cmat)
    all_reads = ring_gather(read.astype(B16))

    delta = jnp.sum(grad_attended.astype(F32) * attended32, 1, keepdims=True)
    grad_q, grad_kt, grad_vt = attend_back(
        queries, keys_t, values_t, first_position, grad_attended, lse, delta
    )
    k_parts = grad_kt.astype(B16).reshape(2, near, half_cols, -1).transpose(1, 0, 2, 3)
    v_parts = grad_vt.astype(B16).reshape(near, key_cols, -1)
    kv_parts = jnp.concatenate([k_parts.reshape(near, key_cols, -1), v_parts], 1)
    kv_parts = jnp.sum(trade_near(kv_parts).astype(F32), 0).astype(B16)
    kv_parts = kv_parts.reshape(-1, groups, span).transpose(1, 0, 2)
    kv_parts = lax.all_to_all(kv_parts, "group", 0, 0, tiled=True)
    grad_kv = jnp.sum(kv_parts.astype(F32), 0)
    gk_first, gk_second = rotate_pair(
        grad_kv[:half_cols], grad_kv[half_cols:key_cols], cos_k, -sin_k
    )
    grad_q = jnp.concatenate(rotate_pair(grad_q[:, :half], grad_q[:, half:], cos_q, -sin_q), 1)
    grad_q = grad_q.astype(B16)

    leaving = jnp.zeros_like(entering)
    for turn in reversed(range(1, groups)):
        passed = jnp.exp(all_totals[turn])[:, None, None] * leaving + all_reads[turn].astype(F32)
        leaving = jnp.where(turn > group, passed, leaving)
    grad_scaled, grad_b, grad_c, grad_last = scan_backward(
        scaled, bmat, cmat, cum, states, state_out, grad_y, leaving
    )
    grad_bc = jnp.stack([grad_b, grad_c]).transpose(0, 3, 1, 2).reshape(2, STATE, span).astype(B16)
    kept = lax.dynamic_index_in_dim(grad_bc, core, 0, False)
    given = lax.dynamic_index_in_dim(grad_bc, 1 - core, 0, False)
    kept = (kept.astype(F32) + swap_cores(given).astype(F32)).astype(B16)
    grad_bc = jnp.sum(trade_near(kept.reshape(near, -1, span)).astype(F32), 0)

    grad_cum = jnp.sum(grad_y * outputs - grad_scaled * scaled, -1).transpose(0, 2, 1)
    grad_cum = grad_cum.at[..., -1].add(grad_last)
    grad_logs = exact("cht,ts->chs", grad_cum, triangle)
    grad_logs = grad_logs.transpose(1, 0, 2).reshape(dt_heads, span)
    grad_dt = jnp.sum(grad_scaled * xh, -1).transpose(2, 0, 1).reshape(dt_heads, span)
    grad_dt = grad_dt - grad_logs * decay_rate
    grad_dt_pre = grad_dt * jax.nn.sigmoid(dt_pre)
    grad_dt_low = grad_dt_pre.astype(B16)
    grad_xc = grad_scaled * dt_col + skip[:, None] * grad_y
    grad_skip = jnp.sum(grad_y * xh, (0, 1, 3))
    grad_alog = jnp.sum(grad_logs * logs, 1)
    grad_dtbias = jnp.sum(grad_dt_pre, 1)

    grad_xpre = grad_xc.reshape(span, -1) * silu_slope(x_pre)
    grad_bcpre = grad_bc * silu_slope(bc_pre)
    next_x = step_group(grad_xpre[: CONV - 1], -1)
    next_bc = step_group(grad_bcpre[:, : CONV - 1], -1)
    grad_x, grad_tapx, grad_biasx = conv_back(grad_xpre, next_x, x_proj, x_edge, taps_x, 0)
    grad_bcp, grad_tapbc, grad_biasbc = conv_back(
        grad_bcpre, next_bc, bc_proj, bc_edge, taps_bc, 1
    )
    grad_x = grad_x.astype(B16)
    grad_kvbc = jnp.concatenate([gk_first, gk_second, grad_kv[key_cols:], grad_bcp], 0).astype(B16)

    partial1 = (
        dot_nt(grad_q, full_q)
        + dot(grad_kvbc, full_kvbc, ((0,), (1,)))
        + dot_nt(grad_z, full_z)
        + dot_nt(grad_x, full_x)
        + dot_tn(grad_dt_low, full_dt)
    )
    grad_n1 = scatter_tokens(partial1)
    _, unit1, factor1 = normalize(tokens.astype(F32), gain1)
    grad_norm1, grad_g1 = norm_back(grad_n1, unit1, factor1, gain1)
    grad_tokens = grad_hidden + grad_norm1

    grad3 = jnp.concatenate([dot_tn(attended, grad_mixed), dot_tn(gated, grad_mixed)], 0)
    home3 = grad3.astype(B16).reshape(-1, groups, near * piece).transpose(1, 0, 2)
    home3 = ring_sum(home3).astype(B16)
    home3 = trade_near(home3.reshape(-1, near, piece).transpose(1, 0, 2)).astype(F32)
    sum_wo = home3[:, :o_rows].reshape(-1, piece)
    sum_wout = home3[:, o_rows:].reshape(-1, piece)
    sum_wz = joined(rows_home(dot_tn(n1, grad_z)))
    grad_kvbc_w = dot(n1, grad_kvbc, ((0,), (1,)))
    home1 = rows_home(jnp.concatenate([dot_tn(n1, grad_q), grad_kvbc_w], 1))
    at = [wq_cols, wq_cols + key_cols, wq_cols + 2 * key_cols]
    home_q, home_k, home_v, home_bc = jnp.split(home1, at, 2)
    sum_wq, sum_wv = joined(home_q), joined(home_v)
    sum_wk = home_k.reshape(near, piece, 2, half_cols).transpose(1, 2, 0, 3)
    sum_wk = sum_wk.reshape(piece, -1).astype(F32)
    bc_mine = joined(home_bc).astype(B16)
    sum_wbc = both_halves(bc_mine, swap_cores(bc_mine), 1).astype(F32)
    sum_wx = joined(rows_home(dot_tn(n1, grad_x)))
    grad_wdt = dot(grad_dt_low, n1)
    dt_parts = jnp.pad(grad_wdt.astype(B16), ((0, -dt_heads % 8), (0, 0)))
    dt_parts = ring_sum(dt_parts.reshape(-1, groups, near * piece).transpose(1, 0, 2)).astype(B16)
    dt_parts = trade_near(dt_parts.reshape(-1, near, piece).transpose(1, 0, 2))
    sum_wdt = dt_parts[:, :dt_heads].reshape(-1, piece).T.astype(F32)

    grads_bc = jnp.concatenate([grad_tapbc.reshape(-1), grad_biasbc])
    other_bc = swap_cores(grads_bc)
    mine = [grad_g1, grad_g2, grad_tapx.reshape(-1), grad_biasx, grad_dtbias, grad_alog, grad_skip]
    mine = [*mine, both_halves(grads_bc, other_bc, 0)]
    ends, at = [], 0
    for g in mine[:-1]:
        at += g.shape[0]
        ends.append(at)
    packed = jnp.concatenate(mine)
    packed = lax.all_to_all(
        jnp.broadcast_to(packed, (devices, packed.shape[0])), ("group", "near"), 0, 0, tiled=True
    )
    every = jnp.split(packed, ends, 1)
    place = group * near + here

    def own(x):
        return lax.dynamic_slice_in_dim(jnp.sum(x, 0), place * piece, piece, 0)

    def by_near(x):
        return jnp.sum(x.reshape(groups, near, -1), 0)

    sum_g1, sum_g2 = own(every[0]), own(every[1])
    sum_convx = by_near(every[2]).reshape(near, CONV, -1).transpose(1, 0, 2).reshape(CONV, -1)
    sum_convxb, sum_dtbias, sum_alog, sum_dskip = (by_near(x).reshape(-1) for x in every[3:7])
    sum_bc = by_near(every[7]).reshape(near, 2, CONV + 1, -1).transpose(2, 1, 0, 3)
    sum_bc = sum_bc.reshape(CONV + 1, -1)
    bc_cols = conv_bc.shape[1]
    sum_bc = lax.dynamic_slice_in_dim(sum_bc, place * bc_cols, bc_cols, 1)
    return (
        output,
        grad_tokens,
        sum_g1,
        sum_wq,
        sum_wk,
        sum_wv,
        sum_wo,
        sum_wz,
        sum_wx,
        sum_wbc,
        sum_wdt,
        sum_bc[:CONV],
        sum_bc[CONV],
        sum_wout,
        sum_g2,
        sum_wgate,
        sum_wup,
        sum_wdown,
        sum_convx,
        sum_convxb,
        sum_dtbias,
        sum_alog,
        sum_dskip,
    )


def solution(mesh):
    seq, cores = mesh.shape["seq"], mesh.shape["head"]
    near = math.gcd(seq, 4)
    split = Mesh(mesh.devices.reshape(seq // near, near, cores), ("group", "near", "head"))
    seq = ("group", "near")
    row_split = P(seq, "head")
    col_split = P("head", seq)
    weights = (
        P(seq),
        row_split,
        row_split,
        row_split,
        col_split,
        row_split,
        row_split,
        P(seq, None),
        row_split,
        P(None, seq),
        P(seq),
        col_split,
        P(seq),
        row_split,
        row_split,
        col_split,
        P(None, "head"),
        P("head"),
        P("head"),
        P("head"),
        P("head"),
    )
    tokens = P(seq, None)
    return jax.shard_map(
        per_device,
        mesh=split,
        in_specs=(tokens, tokens, *weights),
        out_specs=(tokens, tokens, *weights),
        check_vma=False,
    )
```

```python
import functools
import math

import jax
import jax.numpy as jnp
from jax import lax
from jax.experimental import pallas as pl
from jax.experimental.pallas import tpu as pltpu
from jax.sharding import Mesh, PartitionSpec as P

HEAD_DIM = 128
STATE = 256
CONV = 4
EPS = 1e-05
ROPE_BASE = 100000000000.0
MASKED = -1e30
HIGHEST = lax.Precision.HIGHEST
F32 = jnp.float32
B16 = jnp.bfloat16
ATTEND_ROWS = 256
ATTEND_KEYS = 512
VMEM_LIMIT = 40 << 20


def after(x, *earlier):
    return lax.optimization_barrier((x, earlier))[0]


def swap_cores(x):
    return lax.ppermute(x, "head", [(0, 1), (1, 0)])


def to_near(x, k):
    return lax.ppermute(x, "near", [(i, i ^ k) for i in range(lax.axis_size("near"))])


def around(x, distance):
    count = lax.axis_size("group")
    return lax.ppermute(x, "group", [(i, (i + distance) % count) for i in range(count)])


def step_group(x, distance):
    count = lax.axis_size("group")
    route = [(i, i + distance) for i in range(count) if 0 <= i + distance < count]
    return lax.ppermute(x, "group", route)


def place_kernel(index, *refs):
    *blocks, out = refs
    for k, block in enumerate(blocks):
        out[index[k]] = block[...]


def placed(index, blocks):
    shape = jax.ShapeDtypeStruct((len(blocks), *blocks[0].shape), blocks[0].dtype)
    return whole_call(place_kernel, shape, [], 0, jnp.stack(index).astype(jnp.int32), *blocks)


def near_places():
    here = lax.axis_index("near")
    return [here ^ k for k in range(lax.axis_size("near"))]


def sent_near(x):
    blocks = [lax.dynamic_index_in_dim(x, at, 0, False) for at in near_places()]
    return [to_near(b, k) if k else b for k, b in enumerate(blocks)]


def trade_near(x):
    return placed(near_places(), sent_near(x))


def added(blocks):
    total = blocks[0].astype(F32)
    for block in blocks[1:]:
        total = total + block.astype(F32)
    return total


def gather_near(x):
    places = near_places()
    return placed(places, [x] + [to_near(x, k) for k in range(1, len(places))])


def gather_groups(x):
    count, group = lax.axis_size("group"), lax.axis_index("group")
    places = [(group - r) % count for r in range(count)]
    return placed(places, [x] + [around(x, r) for r in range(1, count)])


def trade_all(x):
    return lax.all_to_all(x, ("group", "near"), 0, 0, tiled=True)


def both_halves(mine, other, dim):
    first = lax.axis_index("head") == 0
    return jnp.concatenate([jnp.where(first, mine, other), jnp.where(first, other, mine)], dim)


def own_half(x):
    half = x.shape[0] // 2
    return lax.dynamic_slice_in_dim(x, lax.axis_index("head") * half, half, 0)


def tokens_kernel(gained, index, *refs):
    *refs, out = refs
    gain = refs.pop()[...] if gained else None
    count = len(refs) // 2
    for k in range(count):
        for side in range(2):
            value = refs[k + side * count][...]
            if gained:
                value = value.astype(F32)
                power = jnp.mean(value * value, 1, keepdims=True)
                value = (value * lax.rsqrt(power + EPS) * gain).astype(B16)
            out[index[k], index[count + side]] = value


def sent_tokens(mine):
    got = [mine] + [to_near(mine, k) for k in range(1, lax.axis_size("near"))]
    return [*got, *map(swap_cores, got)]


def placed_tokens(parts, gain=None):
    core, places = lax.axis_index("head"), near_places()
    rows, width = parts[0].shape
    index = jnp.stack([*places, core, 1 - core]).astype(jnp.int32)
    operands = [index, *parts]
    if gain is not None:
        operands.append(gain[None, :])
    shape = jax.ShapeDtypeStruct((len(places), 2, rows, width), parts[0].dtype)
    kernel = functools.partial(tokens_kernel, gain is not None)
    return whole_call(kernel, shape, [], 8 * shape.size, *operands).reshape(-1, width)


def gather_tokens(mine):
    return placed_tokens(sent_tokens(mine))


def dots_kernel(turned, core, *refs):
    *refs, give, keep = refs
    pairs = len(turned)
    for out, side in (give, 1 - core[0]), (keep, core[0]):
        lefts = []
        for left in refs[:pairs]:
            blocks = [left[j, side] for j in range(left.shape[0])]
            lefts.append(jnp.concatenate(blocks, 0))
        width = out.shape[1]
        tile = min(width, 512)
        for n in range(width // tile):
            cols = slice(n * tile, (n + 1) * tile)
            total = None
            for left, right, turn in zip(lefts, refs[pairs:], turned):
                part = dot_nt(left, right[cols]) if turn else dot(left, right[:, cols])
                total = part if total is None else total + part
            out[:, cols] = total.astype(B16)


def summed_dots(width, *pairs):
    lefts, rights, specs, turned, work = [], [], [], [], 0
    near = lax.axis_size("near")
    for left, right in pairs:
        span, depth = left.shape
        lefts.append(left.reshape(near, 2, span // near // 2, depth))
        turned.append(isinstance(right, tuple))
        array, at = right if turned[-1] else (right, 0)
        shape = (width, depth) if turned[-1] else array.shape
        specs.append(pl.BlockSpec(shape, lambda i, at=at: (0, at)))
        rights.append(array)
        work += 2 * span * width * depth
    smem = pl.BlockSpec(memory_space=pltpu.SMEM)
    wholes = [pl.BlockSpec(a.shape, lambda i: (0, 0, 0, 0)) for a in lefts]
    shape = (lefts[0].shape[0] * lefts[0].shape[2], width)
    return pl.pallas_call(
        functools.partial(dots_kernel, turned),
        grid=(1,),
        in_specs=[smem, *wholes, *specs],
        out_specs=[pl.BlockSpec(shape, lambda i: (0, 0))] * 2,
        out_shape=[jax.ShapeDtypeStruct(shape, B16)] * 2,
        cost_estimate=pl.CostEstimate(flops=work, bytes_accessed=4 << 20, transcendentals=0),
        compiler_params=pltpu.CompilerParams(vmem_limit_bytes=VMEM_LIMIT),
    )(lax.axis_index("head").astype(jnp.int32).reshape(1), *lefts, *rights)


def grads_kernel(count, *refs):
    *refs, out = refs
    at = 0
    for left, right in zip(refs[:count], refs[count:]):
        cols = slice(at, at + right.shape[1])
        out[:, cols] = dot_tn(left[...], right[...]).astype(B16)
        at = cols.stop


def joined_grads(*pairs):
    lefts, rights = zip(*pairs)
    span, width = lefts[0].shape
    total = sum(r.shape[1] for r in rights)
    tile = min(width, 512)
    return pl.pallas_call(
        functools.partial(grads_kernel, len(pairs)),
        grid=(width // tile,),
        in_specs=[pl.BlockSpec((span, tile), lambda i: (0, i))] * len(pairs)
        + [pl.BlockSpec(r.shape, lambda i: (0, 0)) for r in rights],
        out_specs=pl.BlockSpec((tile, total), lambda i: (i, 0)),
        out_shape=jax.ShapeDtypeStruct((width, total), B16),
        cost_estimate=pl.CostEstimate(
            flops=2 * span * width * total, bytes_accessed=16 << 20, transcendentals=0
        ),
        compiler_params=pltpu.CompilerParams(vmem_limit_bytes=VMEM_LIMIT),
    )(*lefts, *rights)


def meet_kernel(index, keep, got, *outs):
    rows = outs[0].shape[0]
    for k, out in enumerate(outs):
        part = pl.ds(pl.multiple_of(index[k] * rows, rows), rows)
        out[...] = (keep[part].astype(F32) + got[part].astype(F32)).astype(B16)


def partial_tokens(width, pairs):
    return met_tokens(*summed_dots(width, *pairs))


def met_tokens(give, keep):
    places = near_places()
    got = swap_cores(give)
    rows, width = keep.shape[0] // len(places), keep.shape[1]
    shapes = [jax.ShapeDtypeStruct((rows, width), B16)] * len(places)
    index = jnp.stack(places).astype(jnp.int32)
    return whole_call(meet_kernel, shapes, [], 2 * keep.size, index, keep, got)


def scatter_tokens(blocks, alongside=None):
    blocks = [to_near(b, k) if k else b for k, b in enumerate(blocks)]
    if alongside is not None:
        blocks, alongside = lax.optimization_barrier((blocks, alongside))
    return added(blocks), alongside


def dot(left, right, dims=((1,), (0,))):
    return lax.dot_general(left, right, (dims, ((), ())), preferred_element_type=F32)


def dot_nt(left, right):
    return dot(left, right, ((1,), (1,)))


def dot_tn(left, right):
    return dot(left, right, ((0,), (0,)))


def dot_exact(left, right, dims=((1,), (0,))):
    return lax.dot_general(
        left, right, (dims, ((), ())), precision=HIGHEST, preferred_element_type=F32
    )


def normalize(values, gain):
    factor = lax.rsqrt(jnp.mean(values * values, -1, keepdims=True) + EPS)
    unit = values * factor
    return unit * gain, unit, factor


def norm_back(grad_out, unit, factor, gain):
    grad_unit = grad_out * gain[None, :]
    grad_in = factor * (grad_unit - unit * jnp.mean(grad_unit * unit, -1, keepdims=True))
    return grad_in, jnp.sum(grad_out * unit, 0)


def rotate_pair(first, second, cosine, sine):
    return first * cosine - second * sine, second * cosine + first * sine


def conv(inputs, edge, weight, bias, dim):
    length = inputs.shape[dim]
    padded = jnp.concatenate([edge, inputs], dim)
    total = bias
    for tap in range(CONV):
        total = total + weight[tap] * lax.slice_in_dim(padded, tap, tap + length, axis=dim)
    return total


def conv_back(grad, grad_edge, inputs, edge, weight, dim):
    length = inputs.shape[dim]
    padded = jnp.concatenate([edge, inputs], dim)
    late = jnp.concatenate([grad, grad_edge], dim)
    total = 0.0
    taps = []
    for tap in range(CONV):
        back = CONV - 1 - tap
        total = total + weight[tap] * lax.slice_in_dim(late, back, back + length, axis=dim)
        taps.append(jnp.sum(grad * lax.slice_in_dim(padded, tap, tap + length, axis=dim), dim))
    return total, jnp.stack(taps), jnp.sum(grad, dim)


def silu_slope(v):
    s = jax.nn.sigmoid(v)
    return s * (1.0 + v * (1.0 - s))


def row_block(i):
    return slice(i * ATTEND_ROWS, (i + 1) * ATTEND_ROWS)


def attend_kernel(index, q, *refs):
    *parts, out, lse, k_t, v_t, total, top, mass = refs
    span = q.shape[0]
    wide = min(ATTEND_KEYS, span)
    keys = HEAD_DIM // len(parts)
    half = keys // 2

    @pl.loop(0, index[0] + 1)
    def _(r):
        for k, part in enumerate(parts):
            at = pl.multiple_of(index[k + 1] * half, half)
            k_t[r, pl.ds(at, half)] = part[r, :half]
            k_t[r, pl.ds(at + HEAD_DIM // 2, half)] = part[r, half:keys]
            at = pl.multiple_of(index[k + 1] * keys, keys)
            v_t[r, pl.ds(at, keys)] = part[r, keys:]

    @pl.loop(index[0] + 1, k_t.shape[0])
    def _(r):
        k_t[r] = jnp.zeros(k_t.shape[1:], B16)
        v_t[r] = jnp.zeros(v_t.shape[1:], B16)

    def meet(i, keys_t, values_t, first):
        scores = dot(q[row_block(i)], keys_t) * HEAD_DIM**-0.5
        if first:
            rows = i * ATTEND_ROWS + lax.broadcasted_iota(jnp.int32, scores.shape, 0)
            cols = lax.broadcasted_iota(jnp.int32, scores.shape, 1)
            scores = jnp.where(cols <= rows, scores, MASKED)
        peak = jnp.max(scores, 1, keepdims=True)
        if not first:
            old = top[row_block(i)]
            peak = jnp.maximum(old, peak)
            fade = jnp.exp(old - peak)
        probs = jnp.exp(scores - peak)
        weight = jnp.sum(probs, 1, keepdims=True)
        read = dot_nt(probs.astype(B16), values_t)
        if not first:
            weight = weight + fade * mass[row_block(i)]
            read = read + fade * total[row_block(i)]
        top[row_block(i)] = peak
        mass[row_block(i)] = weight
        total[row_block(i)] = read

    for i in range(span // ATTEND_ROWS):
        keys = (i + 1) * ATTEND_ROWS
        meet(i, k_t[0, :, :keys], v_t[0, :, :keys], True)

    @pl.loop(1, index[0] + 1)
    def _(r):
        for j in range(span // wide):
            keys_t = k_t[r, :, j * wide : (j + 1) * wide]
            values_t = v_t[r, :, j * wide : (j + 1) * wide]
            for i in range(span // ATTEND_ROWS):
                meet(i, keys_t, values_t, False)

    out[...] = total[...] / mass[...]
    lse[...] = top[...] + jnp.log(mass[...])


def whole_call(kernel, out_shape, scratch, cost, *operands):
    vmem = pl.BlockSpec(memory_space=pltpu.VMEM)
    smem = pl.BlockSpec(memory_space=pltpu.SMEM)
    return pl.pallas_call(
        kernel,
        out_shape=out_shape,
        in_specs=[smem] + [vmem] * (len(operands) - 1),
        out_specs=jax.tree.map(lambda _: vmem, out_shape),
        scratch_shapes=scratch,
        cost_estimate=pl.CostEstimate(flops=cost, bytes_accessed=4 << 20, transcendentals=0),
        compiler_params=pltpu.CompilerParams(vmem_limit_bytes=VMEM_LIMIT),
    )(*operands)


def attend(index, queries, parts):
    span, groups = queries.shape[0], parts[0].shape[0]
    shape = jax.ShapeDtypeStruct
    turned = shape((groups, HEAD_DIM, span), B16)
    column = pltpu.VMEM((span, 1), F32)
    return whole_call(
        attend_kernel,
        (shape((span, HEAD_DIM), F32), shape((span, 1), F32), turned, turned),
        [pltpu.VMEM((span, HEAD_DIM), F32), column, column],
        2 * span * span * groups * HEAD_DIM,
        index,
        queries,
        *parts,
    )


def attend_back_kernel(index, q, q_t, d, d_t, k_t, v_t, lse, delta, grad_q, *refs):
    *outs, sum_k, sum_v = refs
    span = q.shape[0]
    keys = HEAD_DIM // len(outs)
    half = keys // 2
    wide = min(ATTEND_KEYS, span)
    blocks = span // ATTEND_ROWS

    def meet(i, keys_t, values_t, offset, total_q):
        part = row_block(i)
        scores = dot(q[part], keys_t) * HEAD_DIM**-0.5
        if offset is not None:
            rows = i * ATTEND_ROWS + lax.broadcasted_iota(jnp.int32, scores.shape, 0)
            cols = offset + lax.broadcasted_iota(jnp.int32, scores.shape, 1)
            scores = jnp.where(cols <= rows, scores, MASKED)
        probs = jnp.exp(scores - lse[part])
        grad_scores = (probs * (dot(d[part], values_t) - delta[part])).astype(B16)
        update = dot_nt(grad_scores, keys_t)
        grad_q[part] = update if total_q is None else grad_q[part] + update
        return dot(q_t[:, part], grad_scores), dot(d_t[:, part], probs.astype(B16))

    def store(r, cols, pair):
        sum_k[...] = (pair[0] * HEAD_DIM**-0.5).astype(B16)
        sum_v[...] = pair[1].astype(B16)
        for k, out in enumerate(outs):
            at = pl.multiple_of(index[k + 1] * half, half)
            out[r, :half, cols] = sum_k[pl.ds(at, half)]
            out[r, half:keys, cols] = sum_k[pl.ds(at + HEAD_DIM // 2, half)]
            at = pl.multiple_of(index[k + 1] * keys, keys)
            out[r, keys:, cols] = sum_v[pl.ds(at, keys)]

    for j in range(span // wide):
        cols = slice(j * wide, (j + 1) * wide)
        pair = None
        for i in range(j * wide // ATTEND_ROWS, blocks):
            more = meet(i, k_t[0, :, cols], v_t[0, :, cols], j * wide, None if j == 0 else True)
            pair = more if pair is None else (pair[0] + more[0], pair[1] + more[1])
        store(0, cols, pair)

    @pl.loop(1, index[0] + 1)
    def _(r):
        for j in range(span // wide):
            cols = slice(j * wide, (j + 1) * wide)
            pair = None
            for i in range(blocks):
                more = meet(i, k_t[r, :, cols], v_t[r, :, cols], None, True)
                pair = more if pair is None else (pair[0] + more[0], pair[1] + more[1])
            store(r, cols, pair)

    @pl.loop(index[0] + 1, k_t.shape[0])
    def _(r):
        for out in outs:
            out[r] = jnp.zeros(out.shape[1:], B16)


def attend_back(index, queries, keys_t, values_t, grad, lse, delta):
    span, groups = queries.shape[0], keys_t.shape[0]
    near = lax.axis_size("near")
    shape = jax.ShapeDtypeStruct
    part = shape((groups, 2 * HEAD_DIM // near, span), B16)
    wide = pltpu.VMEM((HEAD_DIM, min(ATTEND_KEYS, span)), B16)
    grad_q, *parts = whole_call(
        attend_back_kernel,
        (shape(queries.shape, F32), *[part] * near),
        [wide, wide],
        5 * span * span * groups * HEAD_DIM,
        index,
        queries,
        queries.T,
        grad,
        grad.T,
        keys_t,
        values_t,
        lse,
        delta,
    )
    return grad_q, parts


def spread(per_head, of_head):
    return dot_exact(per_head, of_head, ((0,), (0,)))


def head_decay(cum, cum_t, h):
    length = cum.shape[0]
    rows = lax.broadcasted_iota(jnp.int32, (length, length), 0)
    cols = lax.broadcasted_iota(jnp.int32, (length, length), 1)
    gap = cum[:, h : h + 1] - cum_t[h : h + 1, :]
    return jnp.exp(jnp.where(cols <= rows, gap, MASKED))


def in_head(shape, h, channels):
    lane = lax.broadcasted_iota(jnp.int32, shape, 1)
    return (lane >= h * channels) & (lane < (h + 1) * channels)


def scan_kernel(heads, x, dt, cum, cum_t, b_t, c_t, of_head, y, states, last, state):
    @pl.when(pl.program_id(0) == 0)
    def _():
        state[...] = jnp.zeros_like(state)

    channels = x.shape[1] // heads
    per = HEAD_DIM // channels
    owner = of_head[...]
    cums, cums_t = cum[...], cum_t[...]
    scaled = x[...] * spread(dt[...], owner)
    inner = dot_tn(c_t[...], b_t[...])
    wide = spread(cums_t, owner)
    end = wide[-1:]
    states[0] = state[...]
    carried = dot_exact(c_t[...].astype(F32), state[...], ((0,), (0,))) * jnp.exp(wide)
    for at in range(heads // per):
        lanes = slice(at * HEAD_DIM, (at + 1) * HEAD_DIM)
        block = scaled[:, lanes]
        within = None
        for k in range(per):
            mixing = head_decay(cums, cums_t, at * per + k) * inner
            part = dot_exact(mixing, block)
            mine = in_head(part.shape, k, channels)
            within = part if within is None else jnp.where(mine, part, within)
        y[:, lanes] = within + carried[:, lanes]
    added = dot_exact(b_t[...].astype(F32), scaled * jnp.exp(end - wide))
    state[...] = jnp.exp(end) * state[...] + added
    last[...] = state[...]


def scan_forward(heads, x, dt, cum, cum_t, b_t, c_t, of_head, rows):
    span, inner = x.shape
    chunks = span // rows
    by_row = lambda width: pl.BlockSpec((rows, width), lambda c: (c, 0))
    by_col = lambda height: pl.BlockSpec((height, rows), lambda c: (0, c))
    whole = lambda a: pl.BlockSpec(a.shape, lambda c: (0,) * a.ndim)
    shape = jax.ShapeDtypeStruct
    return pl.pallas_call(
        functools.partial(scan_kernel, heads),
        grid=(chunks,),
        in_specs=[
            by_row(inner),
            by_col(dt.shape[0]),
            by_row(cum.shape[1]),
            by_col(dt.shape[0]),
            by_col(STATE),
            by_col(STATE),
            whole(of_head),
        ],
        out_specs=[
            by_row(inner),
            pl.BlockSpec((1, STATE, inner), lambda c: (c, 0, 0)),
            pl.BlockSpec((STATE, inner), lambda c: (0, 0)),
        ],
        out_shape=[
            shape((span, inner), F32),
            shape((chunks, STATE, inner), F32),
            shape((STATE, inner), F32),
        ],
        scratch_shapes=[pltpu.VMEM((STATE, inner), F32)],
        cost_estimate=pl.CostEstimate(
            flops=60 * span * rows * inner, bytes_accessed=8 << 20, transcendentals=0
        ),
        compiler_params=pltpu.CompilerParams(vmem_limit_bytes=VMEM_LIMIT),
    )(x, dt, cum, cum_t, b_t, c_t, of_head)


def scan_back_kernel(
    heads,
    x,
    dt,
    cum,
    cum_t,
    b_t,
    c_t,
    of_head,
    skip,
    state_in,
    state_out,
    y,
    grad,
    leaving,
    grad_x,
    grad_bt,
    grad_ct,
    grad_logs,
    grad_dt,
    grad_skip,
    grad_state,
):
    @pl.when(pl.program_id(0) == 0)
    def _():
        grad_state[...] = leaving[...]
        grad_skip[...] = jnp.zeros_like(grad_skip)

    channels = x.shape[1] // heads
    per = HEAD_DIM // channels
    owner = of_head[...]
    cums, cums_t = cum[...], cum_t[...]
    times = spread(dt[...], owner)
    values = x[...]
    scaled = values * times
    inner = dot_tn(c_t[...], b_t[...])
    wide = spread(cums_t, owner)
    end = wide[-1:]
    tail = jnp.exp(end - wide)
    back = grad[...]
    faded = back * jnp.exp(wide)
    b32, c32 = b_t[...].astype(F32), c_t[...].astype(F32)
    to_state = grad_state[...]
    grad_inner = jnp.zeros_like(inner)
    within = []
    for at in range(heads // per):
        lanes = slice(at * HEAD_DIM, (at + 1) * HEAD_DIM)
        total = None
        for k in range(per):
            decay = head_decay(cums, cums_t, at * per + k)
            part = dot_exact(decay * inner, back[:, lanes], ((0,), (0,)))
            mine = in_head(part.shape, k, channels)
            total = part if total is None else jnp.where(mine, part, total)
            only = jnp.where(mine, back[:, lanes], 0.0)
            grad_inner += dot_exact(only, scaled[:, lanes], ((1,), (1,))) * decay
        within.append(total)
    grad_scaled = jnp.concatenate(within, 1)
    grad_scaled += tail * dot_exact(b32, to_state, ((0,), (0,)))
    grad_ct[...] = (
        dot_exact(b32, grad_inner, ((1,), (1,))) + dot_exact(state_in[0], faded, ((1,), (1,)))
    ).astype(B16)
    grad_bt[...] = (
        dot_exact(c32, grad_inner) + dot_exact(to_state, scaled * tail, ((1,), (1,)))
    ).astype(B16)
    grad_x[...] = grad_scaled * times + skip[...] * back
    grad_skip[...] += jnp.sum(back * values, 0, keepdims=True)
    at_end = jnp.sum(state_out[0] * to_state, 0, keepdims=True)
    change = back * y[...] - grad_scaled * scaled
    rows = lax.broadcasted_iota(jnp.int32, change.shape, 0)
    change = change + jnp.where(rows == change.shape[0] - 1, at_end, 0.0)
    per_head = dot_exact(owner, change, ((1,), (1,)))
    length = change.shape[0]
    later = lax.broadcasted_iota(jnp.int32, (length, length), 0) >= lax.broadcasted_iota(
        jnp.int32, (length, length), 1
    )
    grad_logs[...] = dot_exact(per_head, later.astype(F32))
    grad_dt[...] = dot_exact(owner, grad_scaled * values, ((1,), (1,)))
    grad_state[...] = jnp.exp(end) * to_state + dot_exact(c32, faded)


def scan_backward(
    heads, x, dt, cum, cum_t, b_t, c_t, of_head, skip, states, y, grad, leaving, rows
):
    span, inner = x.shape
    chunks = span // rows
    last = chunks - 1
    by_row = lambda width: pl.BlockSpec((rows, width), lambda c: (last - c, 0))
    by_col = lambda height: pl.BlockSpec((height, rows), lambda c: (0, last - c))
    whole = lambda a: pl.BlockSpec(a.shape, lambda c: (0,) * a.ndim)
    at_state = lambda more: pl.BlockSpec((1, STATE, inner), lambda c: (last - c + more, 0, 0))
    padded = dt.shape[0]
    shape = jax.ShapeDtypeStruct
    return pl.pallas_call(
        functools.partial(scan_back_kernel, heads),
        grid=(chunks,),
        in_specs=[
            by_row(inner),
            by_col(padded),
            by_row(cum.shape[1]),
            by_col(padded),
            by_col(STATE),
            by_col(STATE),
            whole(of_head),
            whole(skip),
            at_state(0),
            at_state(1),
            by_row(inner),
            by_row(inner),
            whole(leaving),
        ],
        out_specs=[
            by_row(inner),
            by_col(STATE),
            by_col(STATE),
            by_col(padded),
            by_col(padded),
            whole(skip),
        ],
        out_shape=[
            shape((span, inner), F32),
            shape((STATE, span), B16),
            shape((STATE, span), B16),
            shape((padded, span), F32),
            shape((padded, span), F32),
            shape(skip.shape, F32),
        ],
        scratch_shapes=[pltpu.VMEM((STATE, inner), F32)],
        cost_estimate=pl.CostEstimate(
            flops=120 * span * rows * inner, bytes_accessed=16 << 20, transcendentals=0
        ),
        compiler_params=pltpu.CompilerParams(vmem_limit_bytes=VMEM_LIMIT),
    )(x, dt, cum, cum_t, b_t, c_t, of_head, skip, states, states, y, grad, leaving)


def per_device(
    tokens,
    cotangent,
    g1,
    w_q,
    w_k,
    w_v,
    w_o,
    w_z,
    w_x,
    w_bc,
    w_dt,
    conv_bc,
    conv_bc_bias,
    w_out,
    g2,
    w_gate,
    w_up,
    w_down,
    conv_x,
    conv_x_bias,
    dt_bias,
    a_log,
    d_skip,
):
    near, groups = lax.axis_size("near"), lax.axis_size("group")
    here, group, core = (lax.axis_index(a) for a in ("near", "group", "head"))
    rows, width = tokens.shape
    span = near * rows
    piece = w_q.shape[0]

    def columns(w):
        return w.reshape(w.shape[0], near, -1).transpose(1, 0, 2)

    def share(x, dim):
        size = x.shape[dim] // near
        return lax.dynamic_slice_in_dim(x, here * size, size, dim)

    devices = near * groups
    key_cols = HEAD_DIM // near
    half_cols = key_cols // 2
    state_cols = STATE // near
    heads = w_dt.shape[1] // near
    padded = heads + -heads % 8
    k_cols = w_k.reshape(piece, 2, near, half_cols).transpose(2, 0, 1, 3)
    w_bc_mine = lax.dynamic_slice_in_dim(w_bc, core * STATE, STATE, 1)
    pack1 = [columns(w_x), k_cols.reshape(near, piece, key_cols), columns(w_v)]
    pack1 = jnp.concatenate([*pack1, columns(w_bc_mine)], 2)
    extra = jnp.concatenate([g1, g2, conv_bc.reshape(-1), conv_bc_bias])
    n_small, n_dt = extra.shape[0], heads * piece
    extra = jnp.broadcast_to(extra, (near, n_small))
    extra = jnp.concatenate([extra, w_dt.T.reshape(near, n_dt)], 1)
    extra = jnp.pad(extra, ((0, 0), (0, -extra.shape[1] % (8 * pack1.shape[2]))))
    pack1 = jnp.concatenate([pack1, extra.reshape(near, -1, pack1.shape[2])], 1)
    inner, q_cols, ff = w_z.shape[1] // near, w_q.shape[1] // near, w_gate.shape[1] // near
    pack1 = trade_near(pack1)
    full1 = gather_groups(pack1.reshape(-1, pack1.shape[2]))
    token_parts = sent_tokens(after(own_half(tokens), pack1))
    pack2 = [columns(w_z), columns(w_out.T), columns(w_q), columns(w_o.T)]
    sent2 = sent_near(after(jnp.concatenate(pack2, 2), *token_parts[:near]))
    pack3 = jnp.concatenate([columns(w_gate), columns(w_up), columns(w_down.T)], 2)
    sent3 = sent_near(after(pack3, *sent2))
    grad_parts = sent_tokens(after(own_half(cotangent), *sent3))
    pack2 = placed(near_places(), sent2).reshape(near * piece, -1)

    positions = (group * span + jnp.arange(span)).astype(F32)
    half = HEAD_DIM // 2
    freqs = ROPE_BASE ** (-jnp.arange(half, dtype=F32) / half)
    angle = positions[:, None] * freqs[None, :]
    cos_q, sin_q = jnp.cos(angle), jnp.sin(angle)
    cos_k, sin_k = (share(x, 1).T for x in (cos_q, sin_q))
    full1, cos_q, sin_q, cos_k, sin_k, pack2 = lax.optimization_barrier(
        (full1, cos_q, sin_q, cos_k, sin_k, pack2)
    )
    full2 = lax.all_gather(pack2, "group", axis=0, tiled=True)

    full1 = full1.reshape(devices, -1, full1.shape[2])
    extra = full1[:, piece:].reshape(devices, -1)
    full_dt = extra[:, n_small : n_small + n_dt].reshape(devices, heads, piece)
    full_dt = full_dt.transpose(1, 0, 2).reshape(heads, width)
    full_dt = jnp.pad(full_dt, ((0, padded - heads), (0, 0)))
    smalls = extra[:, :n_small].astype(F32)
    gain1 = smalls[:, :piece].reshape(-1)
    gain2 = smalls[:, piece : 2 * piece].reshape(-1)
    taps_bc = smalls[:, 2 * piece : -conv_bc_bias.shape[0]].reshape(devices, CONV, -1)
    taps_bc = taps_bc.transpose(1, 0, 2).reshape(CONV, 2, near, -1)
    taps_bc = taps_bc[:, core, here][:, :, None]
    bias_bc = smalls[:, -conv_bc_bias.shape[0] :].reshape(2, near, -1)[core, here][:, None]
    full1 = full1[:, :piece].reshape(width, -1)
    n1 = placed_tokens(token_parts, gain1)
    full_x, full_kvbc = full1[:, :inner], full1[:, inner:]
    full_z, full_out_t = full2[:, :inner], full2[:, inner : 2 * inner]
    full_q, full_o_t = full2[:, 2 * inner : 2 * inner + q_cols], full2[:, 2 * inner + q_cols :]

    kvbc = dot(full_kvbc, n1, ((0,), (1,)))
    k_first, k_second = rotate_pair(kvbc[:half_cols], kvbc[half_cols:key_cols], cos_k, sin_k)
    kv = jnp.concatenate([k_first, k_second, kvbc[key_cols : 2 * key_cols]], 0).astype(B16)
    kv_parts = [kv] + [step_group(kv, r) for r in range(1, groups)]
    sent3 = lax.optimization_barrier((sent3, n1))[0]
    pack3 = placed(near_places(), sent3).reshape(near * piece, -1)
    n1_x, pack3 = lax.optimization_barrier((n1, pack3, kv))[:2]
    full3 = lax.all_gather(pack3, "group", axis=0, tiled=True)
    full_gu, full_down_t = full3[:, : 2 * ff], full3[:, 2 * ff :]

    bc_proj = kvbc[2 * key_cols :]
    bc_edge = step_group(bc_proj[:, span - CONV + 1 :], 1)
    bc_pre = conv(bc_proj, bc_edge, taps_bc, bias_bc, 1)
    bc_mine = gather_near(jax.nn.silu(bc_pre).astype(B16)).reshape(STATE, span)
    bc_other = swap_cores(bc_mine)
    first = core == 0
    b_t, c_t = jnp.where(first, bc_mine, bc_other), jnp.where(first, bc_other, bc_mine)

    def by_head(x):
        return jnp.pad(share(x, 0).astype(F32), (0, padded - heads))[:, None]

    of_head = jnp.arange(inner)[None, :] // (inner // heads) == jnp.arange(padded)[:, None]
    of_head = of_head.astype(F32)
    dt_pre = dot_nt(full_dt, n1) + by_head(dt_bias)
    dt = jax.nn.softplus(dt_pre)
    decay_rate = jnp.exp(by_head(a_log))
    logs = -dt * decay_rate
    triangle = jnp.triu(jnp.ones((rows, rows), F32))
    cum_t = dot_exact(logs.reshape(padded * near, rows), triangle).reshape(padded, near, rows)
    chunk_total = cum_t[:, :, -1]
    before = jnp.cumsum(chunk_total, 1) - chunk_total
    group_total = jnp.sum(chunk_total, 1, keepdims=True)
    fade = jnp.exp(spread((cum_t + before[:, :, None]).reshape(padded, span), of_head))
    cum_t = cum_t.reshape(padded, span)
    cum = cum_t.T
    group_decay = jnp.exp(spread(group_total, of_head))

    x_proj = dot(n1_x, full_x)
    x_edge = step_group(x_proj[span - CONV + 1 :], 1)
    taps_x = share(conv_x, 1).astype(F32)[:, None, :]
    bias_x = share(conv_x_bias, 0).astype(F32)[None, :]
    skip = spread(by_head(d_skip), of_head)
    x_pre = conv(x_proj, x_edge, taps_x, bias_x, 0)
    xc = jax.nn.silu(x_pre)
    kv_parts = jnp.stack(kv_parts)
    xc = after(xc, kv_parts, *grad_parts)
    kv_parts = [to_near(kv_parts, k) if k else kv_parts for k in range(near)]
    outputs, states, state_out = scan_forward(heads, xc, dt, cum, cum_t, b_t, c_t, of_head, rows)

    def sent_states(state, direction):
        pad = jnp.broadcast_to(group_decay, (16, inner))
        sent = jnp.concatenate([state, pad], 0).astype(B16)
        return [step_group(sent, direction * r) for r in range(1, groups)]

    def chained(parts):
        total = jnp.zeros((STATE, inner), F32)
        for part in reversed(parts):
            part = part.astype(F32)
            total = part[STATE : STATE + 1] * total + part[:STATE]
        return total

    entering = sent_states(state_out, 1)
    q_proj = dot(n1, full_q)
    queries = jnp.concatenate(rotate_pair(q_proj[:, :half], q_proj[:, half:], cos_q, sin_q), 1)
    queries = queries.astype(B16)
    z_proj = dot(n1, full_z)
    index = jnp.stack([group, *near_places()]).astype(jnp.int32)
    attended32, lse, keys_t, values_t = attend(index, queries, kv_parts)
    attended = attended32.astype(B16)
    entering = chained(after(entering, attended, z_proj))

    outputs = outputs + fade * dot_tn(c_t, entering.astype(B16))
    y = outputs + skip * xc
    gated = (y * jax.nn.silu(z_proj)).astype(B16)

    at_q, o_rows = 2 * inner // q_cols, w_o.shape[0] // near
    pairs = [(gated, (full2, 1)), (attended, (full2, at_q + 1))]
    mixed, all_cotangent = scatter_tokens(partial_tokens(width, pairs), placed_tokens(grad_parts))
    my_tokens, my_cotangent = own_half(tokens).astype(F32), own_half(cotangent).astype(F32)
    hidden = my_tokens + mixed
    normed2, unit2, factor2 = normalize(hidden, gain2)
    n2 = gather_tokens(normed2.astype(B16))
    both = dot(n2, full_gu)
    gate, up = both[:, :ff], both[:, ff:]
    sigma = jax.nn.sigmoid(gate)
    act = (gate * sigma * up).astype(B16)
    grad_act = dot(all_cotangent, full_down_t)
    grad_gate = grad_act * up * sigma * (1.0 + gate * (1.0 - sigma))
    grad_gu = jnp.concatenate([grad_gate, grad_act * gate * sigma], 1).astype(B16)

    def sum_groups(grad):
        return lax.psum_scatter(grad, "group", scatter_dimension=0, tiled=True)

    def by_near_rows(own):
        return trade_near(own.reshape(near, piece, -1))

    def joined(parts):
        return parts.transpose(1, 0, 2).reshape(piece, -1).astype(F32)

    def joined_t(parts):
        return parts.transpose(0, 2, 1).reshape(-1, piece).astype(F32)

    partial2 = partial_tokens(width, [(grad_gu, (full3, 0))])
    grads3 = joined_grads((n2, grad_gu), (all_cotangent, act))
    grad_n2, (grads3, feed) = scatter_tokens(
        partial2, alongside=(grads3, summed_dots(width, (act, (full3, 2))))
    )
    home3 = sum_groups(grads3)

    grad_norm2, grad_g2 = norm_back(grad_n2, unit2, factor2, gain2)
    grad_hidden = my_cotangent + grad_norm2
    grad_mixed = gather_tokens(grad_hidden.astype(B16))

    grad_attended = dot(grad_mixed, full_o_t).astype(B16)
    grad_gated = dot(grad_mixed, full_out_t).astype(B16).astype(F32)

    sig_z = jax.nn.sigmoid(z_proj)
    grad_y = grad_gated * z_proj * sig_z
    grad_z = (grad_gated * y * sig_z * (1.0 + z_proj * (1.0 - sig_z))).astype(B16)
    read = sent_states(dot(c_t, (grad_y * fade).astype(B16)), -1)
    feed, _ = scatter_tokens(met_tokens(*after(feed, grad_mixed)))
    output = (hidden + feed).astype(B16)
    output = both_halves(output, swap_cores(output), 0)
    grad_attended = after(grad_attended, output, grad_y, grad_z)

    delta = jnp.sum(grad_attended.astype(F32) * attended32, 1, keepdims=True)
    grad_q, kv_parts = attend_back(
        index, queries, keys_t, values_t, grad_attended, lse, delta
    )
    kv_parts = added([to_near(p, k) if k else p for k, p in enumerate(kv_parts)])
    kv_sent = kv_parts.astype(B16)
    grad_kv = kv_parts[0]
    for r in range(1, groups):
        grad_kv = grad_kv + step_group(kv_sent[r], -r).astype(F32)
    gk_first, gk_second = rotate_pair(
        grad_kv[:half_cols], grad_kv[half_cols:key_cols], cos_k, -sin_k
    )
    grad_q = grad_q * HEAD_DIM**-0.5
    grad_q = jnp.concatenate(rotate_pair(grad_q[:, :half], grad_q[:, half:], cos_q, -sin_q), 1)
    grad_zq = jnp.concatenate([grad_z, grad_q.astype(B16)], 1)
    mixer_out = jnp.concatenate([gated, attended], 1)
    grads2 = joined_grads((grad_mixed, mixer_out), (n1, grad_zq))
    home2 = sum_groups(grads2)

    before_wide = jnp.exp(spread(before, of_head))
    states = jnp.concatenate([states, state_out[None]], 0)
    before_wide = jnp.concatenate([before_wide, group_decay], 0)
    states = states + before_wide[:, None, :] * entering
    grad_y = after(grad_y, kv_sent, grads2)
    leaving = chained(after(read, kv_sent))
    grad_xc, grad_bt, grad_ct, grad_logs, grad_dt, grad_skip = scan_backward(
        heads, xc, dt, cum, cum_t, b_t, c_t, of_head, skip, states, outputs, grad_y, leaving, rows
    )
    kept = jnp.where(first, grad_bt, grad_ct)
    given = swap_cores(jnp.where(first, grad_ct, grad_bt))
    kept = (kept.astype(F32) + given.astype(F32)).astype(B16)
    grad_bc = added(sent_near(kept.reshape(near, -1, span)))
    grad_dt = grad_dt - grad_logs * decay_rate
    grad_dt_pre = grad_dt * jax.nn.sigmoid(dt_pre)
    grad_dt_low = grad_dt_pre.astype(B16)
    grad_skip = dot_exact(of_head, grad_skip, ((1,), (1,)))[:heads, 0]
    grad_alog = jnp.sum(grad_logs * logs, 1)[:heads]
    grad_dtbias = jnp.sum(grad_dt_pre, 1)[:heads]

    grad_xpre = grad_xc * silu_slope(x_pre)
    grad_bcpre = grad_bc * silu_slope(bc_pre)
    next_x = step_group(grad_xpre[: CONV - 1], -1)
    next_bc = step_group(grad_bcpre[:, : CONV - 1], -1)
    grad_x, grad_tapx, grad_biasx = conv_back(grad_xpre, next_x, x_proj, x_edge, taps_x, 0)
    grad_bcp, grad_tapbc, grad_biasbc = conv_back(
        grad_bcpre, next_bc, bc_proj, bc_edge, taps_bc, 1
    )
    grad_kvbc = jnp.concatenate([gk_first, gk_second, grad_kv[key_cols:], grad_bcp], 0)
    grad_first = jnp.concatenate([grad_x.astype(B16), grad_kvbc.astype(B16).T], 1)

    home1 = dot_tn(n1, grad_first).astype(B16).reshape(devices, piece, -1)
    grad_wdt = dot(grad_dt_low, n1).astype(B16).reshape(padded, devices, piece)
    grad_wdt = grad_wdt.transpose(1, 0, 2).reshape(devices, -1)
    grad_wdt = jnp.pad(grad_wdt, ((0, 0), (0, -grad_wdt.shape[1] % home1.shape[2])))
    grad_wdt = grad_wdt.reshape(devices, -1, home1.shape[2])
    home1 = trade_all(jnp.concatenate([home1, grad_wdt], 1))

    home3 = home3.reshape(near, piece, -1)
    pairs = [
        (grad_zq[:, :inner], (full2, 0)),
        (grad_zq[:, inner:], (full2, at_q)),
        (grad_first, (full1, 0)),
        (grad_dt_low.T, full_dt),
    ]
    partial1 = partial_tokens(width, pairs)
    home3 = trade_near(after(home3, *partial1))
    outs3 = joined(home3[:, :, :ff]), joined(home3[:, :, ff : 2 * ff]), joined_t(home3[:, :, 2 * ff :])
    grad_n1, outs3 = scatter_tokens(partial1, alongside=outs3)
    sum_wgate, sum_wup, sum_wdown = outs3
    _, unit1, factor1 = normalize(my_tokens, gain1)
    grad_norm1, grad_g1 = norm_back(grad_n1, unit1, factor1, gain1)
    grad_tokens = grad_hidden + grad_norm1
    grad_tokens = both_halves(grad_tokens, swap_cores(grad_tokens), 0)

    home2 = trade_near(after(home2, grad_n1).reshape(near, piece, -1))
    at_o = inner + o_rows
    sum_wout, sum_wo = joined_t(home2[:, :, :inner]), joined_t(home2[:, :, inner:at_o])
    sum_wz, sum_wq = joined(home2[:, :, at_o : at_o + inner]), joined(home2[:, :, at_o + inner :])
    home1 = after(home1, grad_n1)
    home1 = jnp.sum(home1.reshape(groups, near, *home1.shape[1:]).astype(F32), 0)
    sum_wdt = home1[:, piece:].reshape(near, -1)[:, : heads * piece].reshape(-1, piece).T
    at = [inner, inner + key_cols, inner + 2 * key_cols]
    home_x, home_k, home_v, home_bc = jnp.split(home1[:, :piece], at, 2)
    sum_wx, sum_wv = joined(home_x), joined(home_v)
    sum_wk = home_k.reshape(near, piece, 2, half_cols).transpose(1, 2, 0, 3)
    sum_wk = sum_wk.reshape(piece, -1)
    bc_mine = joined(home_bc)
    sum_wbc = both_halves(bc_mine, swap_cores(bc_mine), 1)

    crossing = jnp.concatenate([grad_g1, grad_g2, grad_tapbc.reshape(-1), grad_biasbc])
    other = swap_cores(crossing)
    gains = 2 * width
    mine = [crossing[:width] + other[:width], crossing[width:gains] + other[width:gains]]
    mine = [*mine, grad_tapx.reshape(-1), grad_biasx, grad_dtbias, grad_alog, grad_skip]
    mine = [*mine, both_halves(crossing[gains:], other[gains:], 0)]
    ends, at = [], 0
    for g in mine[:-1]:
        at += g.shape[0]
        ends.append(at)
    packed = jnp.concatenate(mine)
    size = packed.shape[0]
    packed = jnp.pad(packed, (0, -size % 1024)).reshape(-1, HEAD_DIM)
    packed = trade_all(jnp.broadcast_to(packed, (devices, *packed.shape)))
    packed = packed.reshape(devices, -1)[:, :size]
    every = jnp.split(packed, ends, 1)
    place = group * near + here

    def own(x):
        return lax.dynamic_slice_in_dim(jnp.sum(x, 0), place * piece, piece, 0)

    def by_near(x):
        return jnp.sum(x.reshape(groups, near, -1), 0)

    sum_g1, sum_g2 = own(every[0]), own(every[1])
    sum_convx = by_near(every[2]).reshape(near, CONV, -1).transpose(1, 0, 2).reshape(CONV, -1)
    sum_convxb, sum_dtbias, sum_alog, sum_dskip = (by_near(x).reshape(-1) for x in every[3:7])
    sum_bc = by_near(every[7]).reshape(near, 2, CONV + 1, -1).transpose(2, 1, 0, 3)
    sum_bc = sum_bc.reshape(CONV + 1, -1)
    bc_cols = conv_bc.shape[1]
    sum_bc = lax.dynamic_slice_in_dim(sum_bc, place * bc_cols, bc_cols, 1)
    return (
        output,
        grad_tokens,
        sum_g1,
        sum_wq,
        sum_wk,
        sum_wv,
        sum_wo,
        sum_wz,
        sum_wx,
        sum_wbc,
        sum_wdt,
        sum_bc[:CONV],
        sum_bc[CONV],
        sum_wout,
        sum_g2,
        sum_wgate,
        sum_wup,
        sum_wdown,
        sum_convx,
        sum_convxb,
        sum_dtbias,
        sum_alog,
        sum_dskip,
    )


def solution(mesh):
    seq, cores = mesh.shape["seq"], mesh.shape["head"]
    near = math.gcd(seq, 4)
    split = Mesh(mesh.devices.reshape(seq // near, near, cores), ("group", "near", "head"))
    seq = ("group", "near")
    row_split = P(seq, "head")
    col_split = P("head", seq)
    weights = (
        P(seq),
        row_split,
        row_split,
        row_split,
        col_split,
        row_split,
        row_split,
        P(seq, None),
        row_split,
        P(None, seq),
        P(seq),
        col_split,
        P(seq),
        row_split,
        row_split,
        col_split,
        P(None, "head"),
        P("head"),
        P("head"),
        P("head"),
        P("head"),
    )
    tokens = P(seq, None)
    return jax.shard_map(
        per_device,
        mesh=split,
        in_specs=(tokens, tokens, *weights),
        out_specs=(tokens, tokens, *weights),
        check_vma=False,
    )
```

```python
import functools
import math

import jax
import jax.numpy as jnp
from jax import lax
from jax.experimental import pallas as pl
from jax.experimental.layout import Layout, with_layout_constraint
from jax.experimental.pallas import tpu as pltpu
from jax.sharding import Mesh, PartitionSpec as P

HEAD_DIM = 128
STATE = 256
CONV = 4
EPS = 1e-05
ROPE_BASE = 100000000000.0
MASKED = -1e30
HIGHEST = lax.Precision.HIGHEST
F32 = jnp.float32
B16 = jnp.bfloat16
ATTEND_ROWS = 256
ATTEND_KEYS = 512
VMEM_LIMIT = 40 << 20


def after(x, *earlier):
    return lax.optimization_barrier((x, earlier))[0]


def swap_cores(x):
    return lax.ppermute(x, "head", [(0, 1), (1, 0)])


def to_near(x, k):
    return lax.ppermute(x, "near", [(i, i ^ k) for i in range(lax.axis_size("near"))])


def around(x, distance):
    count = lax.axis_size("group")
    return lax.ppermute(x, "group", [(i, (i + distance) % count) for i in range(count)])


def step_group(x, distance):
    count = lax.axis_size("group")
    route = [(i, i + distance) for i in range(count) if 0 <= i + distance < count]
    return lax.ppermute(x, "group", route)


def place_kernel(count, index, *refs):
    for k, block in enumerate(refs[:count]):
        at = 0
        for out in refs[count:]:
            cols = slice(at, at + out.shape[-1])
            out[index[k]] = block[..., cols]
            at = cols.stop


def placed(index, blocks, widths=None):
    block = blocks[0]
    shapes = [
        jax.ShapeDtypeStruct((len(blocks), *block.shape[:-1], w), block.dtype)
        for w in widths or block.shape[-1:]
    ]
    kernel = functools.partial(place_kernel, len(blocks))
    out = whole_call(kernel, shapes, [], jnp.stack(index).astype(jnp.int32), *blocks)
    return out if widths else out[0]


def near_places():
    here = lax.axis_index("near")
    return [here ^ k for k in range(lax.axis_size("near"))]


def sent_near(x):
    blocks = [lax.dynamic_index_in_dim(x, at, 0, False) for at in near_places()]
    return [to_near(b, k) if k else b for k, b in enumerate(blocks)]


def trade_near(x):
    return placed(near_places(), sent_near(x))


def added(blocks):
    total = blocks[0].astype(F32)
    for block in blocks[1:]:
        total = total + block.astype(F32)
    return total


def gather_near(x):
    places = near_places()
    return placed(places, [x] + [to_near(x, k) for k in range(1, len(places))])


def trade_all(x):
    return lax.all_to_all(x, ("group", "near"), 0, 0, tiled=True)


def both_halves(mine, other, dim):
    first = lax.axis_index("head") == 0
    return jnp.concatenate([jnp.where(first, mine, other), jnp.where(first, other, mine)], dim)


def own_half(x):
    half = x.shape[0] // 2
    return lax.dynamic_slice_in_dim(x, lax.axis_index("head") * half, half, 0)


def tokens_kernel(gained, index, *refs):
    *refs, out = refs
    gain = refs.pop()[...] if gained else None
    count = len(refs) // 2
    for k in range(count):
        for side in range(2):
            value = refs[k + side * count][...]
            if gained:
                value = value.astype(F32)
                power = jnp.mean(value * value, 1, keepdims=True)
                value = (value * lax.rsqrt(power + EPS) * gain).astype(B16)
            out[index[k], index[count + side]] = value


def sent_tokens(mine):
    got = [mine] + [to_near(mine, k) for k in range(1, lax.axis_size("near"))]
    return [*got, *map(swap_cores, got)]


def placed_tokens(parts, gain=None):
    core, places = lax.axis_index("head"), near_places()
    rows, width = parts[0].shape
    index = jnp.stack([*places, core, 1 - core]).astype(jnp.int32)
    operands = [index, *parts]
    if gain is not None:
        operands.append(gain[None, :])
    shape = jax.ShapeDtypeStruct((len(places), 2, rows, width), parts[0].dtype)
    kernel = functools.partial(tokens_kernel, gain is not None)
    return whole_call(kernel, shape, [], *operands).reshape(-1, width)


def gather_tokens(mine):
    return placed_tokens(sent_tokens(mine))


def dots_kernel(turned, core, *refs):
    *refs, give, keep = refs
    pairs = len(turned)
    for out, side in (give, 1 - core[0]), (keep, core[0]):
        lefts = []
        for left in refs[:pairs]:
            blocks = [left[j, side] for j in range(left.shape[0])]
            lefts.append(jnp.concatenate(blocks, 0))
        width = out.shape[1]
        tile = min(width, 512)
        for n in range(width // tile):
            cols = slice(n * tile, (n + 1) * tile)
            total = None
            for left, right, turn in zip(lefts, refs[pairs:], turned):
                part = dot_nt(left, right[cols]) if turn else dot(left, right[:, cols])
                total = part if total is None else total + part
            out[:, cols] = total.astype(B16)


def summed_dots(width, *pairs):
    lefts, rights, specs, turned, work = [], [], [], [], 0
    near = lax.axis_size("near")
    for left, right in pairs:
        span, depth = left.shape
        lefts.append(left.reshape(near, 2, span // near // 2, depth))
        turned.append(isinstance(right, tuple))
        array, at = right if turned[-1] else (right, 0)
        shape = (width, depth) if turned[-1] else array.shape
        specs.append(pl.BlockSpec(shape, lambda i, at=at: (0, at)))
        rights.append(array)
        work += 2 * span * width * depth
    smem = pl.BlockSpec(memory_space=pltpu.SMEM)
    wholes = [pl.BlockSpec(a.shape, lambda i: (0, 0, 0, 0)) for a in lefts]
    shape = (lefts[0].shape[0] * lefts[0].shape[2], width)
    return pl.pallas_call(
        functools.partial(dots_kernel, turned),
        grid=(1,),
        in_specs=[smem, *wholes, *specs],
        out_specs=[pl.BlockSpec(shape, lambda i: (0, 0))] * 2,
        out_shape=[jax.ShapeDtypeStruct(shape, B16)] * 2,
        cost_estimate=pl.CostEstimate(flops=0, bytes_accessed=0, transcendentals=0),
        compiler_params=pltpu.CompilerParams(vmem_limit_bytes=VMEM_LIMIT),
    )(lax.axis_index("head").astype(jnp.int32).reshape(1), *lefts, *rights)


def grads_kernel(count, *refs):
    *refs, out = refs
    at = 0
    for left, right in zip(refs[:count], refs[count:]):
        cols = slice(at, at + right.shape[1])
        out[:, cols] = dot_tn(left[...], right[...]).astype(B16)
        at = cols.stop


def joined_grads(*pairs):
    lefts, rights = zip(*pairs)
    span, width = lefts[0].shape
    total = sum(r.shape[1] for r in rights)
    tile = min(width, 512)
    return pl.pallas_call(
        functools.partial(grads_kernel, len(pairs)),
        grid=(width // tile,),
        in_specs=[pl.BlockSpec((span, tile), lambda i: (0, i))] * len(pairs)
        + [pl.BlockSpec(r.shape, lambda i: (0, 0)) for r in rights],
        out_specs=pl.BlockSpec((tile, total), lambda i: (i, 0)),
        out_shape=jax.ShapeDtypeStruct((width, total), B16),
        cost_estimate=pl.CostEstimate(flops=0, bytes_accessed=0, transcendentals=0),
        compiler_params=pltpu.CompilerParams(vmem_limit_bytes=VMEM_LIMIT),
    )(*lefts, *rights)


def meet_kernel(index, keep, got, *outs):
    rows = outs[0].shape[0]
    for k, out in enumerate(outs):
        part = pl.ds(pl.multiple_of(index[k] * rows, rows), rows)
        out[...] = (keep[part].astype(F32) + got[part].astype(F32)).astype(B16)


def partial_tokens(width, pairs):
    return met_tokens(*summed_dots(width, *pairs))


def met_tokens(give, keep):
    places = near_places()
    got = swap_cores(give)
    rows, width = keep.shape[0] // len(places), keep.shape[1]
    shapes = [jax.ShapeDtypeStruct((rows, width), B16)] * len(places)
    index = jnp.stack(places).astype(jnp.int32)
    return whole_call(meet_kernel, shapes, [], index, keep, got)


def scatter_tokens(blocks, alongside=None):
    blocks = [to_near(b, k) if k else b for k, b in enumerate(blocks)]
    if alongside is not None:
        blocks, alongside = lax.optimization_barrier((blocks, alongside))
    return added(blocks), alongside


def dot(left, right, dims=((1,), (0,))):
    return lax.dot_general(left, right, (dims, ((), ())), preferred_element_type=F32)


def dot_nt(left, right):
    return dot(left, right, ((1,), (1,)))


def dot_tn(left, right):
    return dot(left, right, ((0,), (0,)))


def dot_exact(left, right, dims=((1,), (0,))):
    return lax.dot_general(
        left, right, (dims, ((), ())), precision=HIGHEST, preferred_element_type=F32
    )


def normalize(values, gain):
    factor = lax.rsqrt(jnp.mean(values * values, -1, keepdims=True) + EPS)
    unit = values * factor
    return unit * gain, unit, factor


def norm_back(grad_out, unit, factor, gain):
    grad_unit = grad_out * gain[None, :]
    grad_in = factor * (grad_unit - unit * jnp.mean(grad_unit * unit, -1, keepdims=True))
    return grad_in, jnp.sum(grad_out * unit, 0)


def rotate_pair(first, second, cosine, sine):
    return first * cosine - second * sine, second * cosine + first * sine


def conv(inputs, edge, weight, bias, dim):
    length = inputs.shape[dim]
    padded = jnp.concatenate([edge, inputs], dim)
    total = bias
    for tap in range(CONV):
        total = total + weight[tap] * lax.slice_in_dim(padded, tap, tap + length, axis=dim)
    return total


def conv_back(grad, grad_edge, inputs, edge, weight, dim):
    length = inputs.shape[dim]
    padded = jnp.concatenate([edge, inputs], dim)
    late = jnp.concatenate([grad, grad_edge], dim)
    total = 0.0
    taps = []
    for tap in range(CONV):
        back = CONV - 1 - tap
        total = total + weight[tap] * lax.slice_in_dim(late, back, back + length, axis=dim)
        taps.append(jnp.sum(grad * lax.slice_in_dim(padded, tap, tap + length, axis=dim), dim))
    return total, jnp.stack(taps), jnp.sum(grad, dim)


def silu_slope(v):
    s = jax.nn.sigmoid(v)
    return s * (1.0 + v * (1.0 - s))


def row_block(i):
    return slice(i * ATTEND_ROWS, (i + 1) * ATTEND_ROWS)


def attend_kernel(index, q, *refs):
    *parts, out, lse, k_t, v_t, total, top, mass = refs
    span = q.shape[0]
    wide = min(ATTEND_KEYS, span)
    keys = HEAD_DIM // len(parts)
    half = keys // 2

    @pl.loop(0, index[0] + 1)
    def _(r):
        for k, part in enumerate(parts):
            at = pl.multiple_of(index[k + 1] * half, half)
            own = pl.multiple_of(r * 2 * keys, 2 * keys)
            k_t[r, pl.ds(at, half)] = part[pl.ds(own, half)]
            k_t[r, pl.ds(at + HEAD_DIM // 2, half)] = part[pl.ds(own + half, half)]
            at = pl.multiple_of(index[k + 1] * keys, keys)
            v_t[r, pl.ds(at, keys)] = part[pl.ds(own + keys, keys)]

    @pl.loop(index[0] + 1, k_t.shape[0])
    def _(r):
        k_t[r] = jnp.zeros(k_t.shape[1:], B16)
        v_t[r] = jnp.zeros(v_t.shape[1:], B16)

    def meet(i, keys_t, values_t, first):
        scores = dot(q[row_block(i)], keys_t) * HEAD_DIM**-0.5
        if first:
            rows = i * ATTEND_ROWS + lax.broadcasted_iota(jnp.int32, scores.shape, 0)
            cols = lax.broadcasted_iota(jnp.int32, scores.shape, 1)
            scores = jnp.where(cols <= rows, scores, MASKED)
        peak = jnp.max(scores, 1, keepdims=True)
        if not first:
            old = top[row_block(i)]
            peak = jnp.maximum(old, peak)
            fade = jnp.exp(old - peak)
        probs = jnp.exp(scores - peak)
        weight = jnp.sum(probs, 1, keepdims=True)
        read = dot_nt(probs.astype(B16), values_t)
        if not first:
            weight = weight + fade * mass[row_block(i)]
            read = read + fade * total[row_block(i)]
        top[row_block(i)] = peak
        mass[row_block(i)] = weight
        total[row_block(i)] = read

    for i in range(span // ATTEND_ROWS):
        keys = (i + 1) * ATTEND_ROWS
        meet(i, k_t[0, :, :keys], v_t[0, :, :keys], True)

    @pl.loop(1, index[0] + 1)
    def _(r):
        for j in range(span // wide):
            keys_t = k_t[r, :, j * wide : (j + 1) * wide]
            values_t = v_t[r, :, j * wide : (j + 1) * wide]
            for i in range(span // ATTEND_ROWS):
                meet(i, keys_t, values_t, False)

    out[...] = total[...] / mass[...]
    lse[...] = top[...] + jnp.log(mass[...])


def whole_call(kernel, out_shape, scratch, index, *operands):
    def whole(array):
        return pl.BlockSpec(array.shape, lambda i: (0,) * len(array.shape))

    return pl.pallas_call(
        kernel,
        grid=(1,),
        out_shape=out_shape,
        in_specs=[pl.BlockSpec(memory_space=pltpu.SMEM), *map(whole, operands)],
        out_specs=jax.tree.map(whole, out_shape),
        scratch_shapes=scratch,
        cost_estimate=pl.CostEstimate(flops=0, bytes_accessed=0, transcendentals=0),
        compiler_params=pltpu.CompilerParams(vmem_limit_bytes=VMEM_LIMIT),
    )(index, *operands)


def attend(index, queries, parts):
    span, groups = queries.shape[0], lax.axis_size("group")
    shape = jax.ShapeDtypeStruct
    turned = shape((groups, HEAD_DIM, span), B16)
    column = pltpu.VMEM((span, 1), F32)
    return whole_call(
        attend_kernel,
        (shape((span, HEAD_DIM), F32), shape((span, 1), F32), turned, turned),
        [pltpu.VMEM((span, HEAD_DIM), F32), column, column],
        index,
        queries,
        *parts,
    )


def attend_back_kernel(index, q, q_t, d, d_t, k_t, v_t, lse, delta, grad_q, *refs):
    *outs, sum_k, sum_v = refs
    span = q.shape[0]
    keys = HEAD_DIM // len(outs)
    half = keys // 2
    wide = min(ATTEND_KEYS, span)
    blocks = span // ATTEND_ROWS

    def meet(i, keys_t, values_t, offset, total_q):
        part = row_block(i)
        scores = dot(q[part], keys_t) * HEAD_DIM**-0.5
        if offset is not None:
            rows = i * ATTEND_ROWS + lax.broadcasted_iota(jnp.int32, scores.shape, 0)
            cols = offset + lax.broadcasted_iota(jnp.int32, scores.shape, 1)
            scores = jnp.where(cols <= rows, scores, MASKED)
        probs = jnp.exp(scores - lse[part])
        grad_scores = (probs * (dot(d[part], values_t) - delta[part])).astype(B16)
        update = dot_nt(grad_scores, keys_t)
        grad_q[part] = update if total_q is None else grad_q[part] + update
        return dot(q_t[:, part], grad_scores), dot(d_t[:, part], probs.astype(B16))

    def store(r, cols, pair):
        sum_k[...] = (pair[0] * HEAD_DIM**-0.5).astype(B16)
        sum_v[...] = pair[1].astype(B16)
        for k, out in enumerate(outs):
            at = pl.multiple_of(index[k + 1] * half, half)
            own = r * 2 * keys if isinstance(r, int) else pl.multiple_of(r * 2 * keys, 2 * keys)
            out[pl.ds(own, half), cols] = sum_k[pl.ds(at, half)]
            out[pl.ds(own + half, half), cols] = sum_k[pl.ds(at + HEAD_DIM // 2, half)]
            at = pl.multiple_of(index[k + 1] * keys, keys)
            out[pl.ds(own + keys, keys), cols] = sum_v[pl.ds(at, keys)]

    for j in range(span // wide):
        cols = slice(j * wide, (j + 1) * wide)
        pair = None
        for i in range(j * wide // ATTEND_ROWS, blocks):
            more = meet(i, k_t[0, :, cols], v_t[0, :, cols], j * wide, None if j == 0 else True)
            pair = more if pair is None else (pair[0] + more[0], pair[1] + more[1])
        store(0, cols, pair)

    @pl.loop(1, index[0] + 1)
    def _(r):
        for j in range(span // wide):
            cols = slice(j * wide, (j + 1) * wide)
            pair = None
            for i in range(blocks):
                more = meet(i, k_t[r, :, cols], v_t[r, :, cols], None, True)
                pair = more if pair is None else (pair[0] + more[0], pair[1] + more[1])
            store(r, cols, pair)

    @pl.loop(index[0] + 1, k_t.shape[0])
    def _(r):
        for out in outs:
            own = pl.ds(pl.multiple_of(r * 2 * keys, 2 * keys), 2 * keys)
            out[own] = jnp.zeros((2 * keys, span), B16)


def attend_back(index, queries, keys_t, values_t, grad, lse, delta):
    span, groups = queries.shape[0], keys_t.shape[0]
    near = lax.axis_size("near")
    shape = jax.ShapeDtypeStruct
    part = shape((groups * 2 * HEAD_DIM // near, span), B16)
    wide = pltpu.VMEM((HEAD_DIM, min(ATTEND_KEYS, span)), B16)
    grad_q, *parts = whole_call(
        attend_back_kernel,
        (shape(queries.shape, F32), *[part] * near),
        [wide, wide],
        index,
        queries,
        queries.T,
        grad,
        grad.T,
        keys_t,
        values_t,
        lse,
        delta,
    )
    return grad_q, parts


def in_two(x):
    high = x.astype(B16)
    return high, (x - high.astype(F32)).astype(B16)


def dot_half(low, x, dims=((1,), (0,))):
    high, rest = in_two(x)
    return dot(low, high, dims) + dot(low, rest, dims)


def dot_fine(left, right, dims=((1,), (0,))):
    high, rest = in_two(left)
    other, more = in_two(right)
    return dot(high, other, dims) + (dot(high, more, dims) + dot(rest, other, dims))


def spread(per_head, of_head):
    return dot_exact(per_head, of_head, ((0,), (0,)))


def head_decay(cum, cum_t, h):
    length = cum.shape[0]
    rows = lax.broadcasted_iota(jnp.int32, (length, length), 0)
    cols = lax.broadcasted_iota(jnp.int32, (length, length), 1)
    gap = cum[:, h : h + 1] - cum_t[h : h + 1, :]
    return jnp.exp(jnp.where(cols <= rows, gap, MASKED))


def in_head(shape, h, channels):
    lane = lax.broadcasted_iota(jnp.int32, shape, 1)
    return (lane >= h * channels) & (lane < (h + 1) * channels)


def scan_kernel(heads, x, dt, cum, cum_t, b_t, c_t, of_head, y, ends, state):
    @pl.when(pl.program_id(0) == 0)
    def _():
        state[...] = jnp.zeros_like(state)

    channels = x.shape[1] // heads
    per = HEAD_DIM // channels
    owner = of_head[...]
    cums, cums_t = cum[...], cum_t[...]
    scaled = x[...] * spread(dt[...], owner)
    inner = dot_tn(c_t[...], b_t[...])
    wide = spread(cums_t, owner)
    end = wide[-1:]
    carried = dot_half(c_t[...], state[...], ((0,), (0,))) * jnp.exp(wide)
    for at in range(heads // per):
        lanes = slice(at * HEAD_DIM, (at + 1) * HEAD_DIM)
        block = scaled[:, lanes]
        within = None
        for k in range(per):
            mixing = head_decay(cums, cums_t, at * per + k) * inner
            part = dot_fine(mixing, block)
            mine = in_head(part.shape, k, channels)
            within = part if within is None else jnp.where(mine, part, within)
        y[:, lanes] = within + carried[:, lanes]
    state[...] = jnp.exp(end) * state[...] + dot_half(b_t[...], scaled * jnp.exp(end - wide))
    ends[0] = state[...]


class ChunkSpecs:
    def __init__(self, rows, chunks, turned):
        self.rows, self.chunks = rows, chunks
        self.chunk = (lambda c: chunks - 1 - c) if turned else (lambda c: c)

    def by_row(self, width):
        return pl.BlockSpec((self.rows, width), lambda c: (self.chunk(c), 0))

    def by_col(self, height):
        return pl.BlockSpec((height, self.rows), lambda c: (0, self.chunk(c)))

    def stacked(self, array, more=0):
        shape = (1, *array.shape[1:])
        return pl.BlockSpec(shape, lambda c: (jnp.maximum(self.chunk(c) + more, 0), 0, 0))

    def whole(self, array):
        return pl.BlockSpec(array.shape, lambda c: (0,) * len(array.shape))


def chunk_call(kernel, chunks, in_specs, out_specs, out_shape, scratch, *operands):
    return pl.pallas_call(
        kernel,
        grid=(chunks,),
        in_specs=in_specs,
        out_specs=out_specs,
        out_shape=out_shape,
        scratch_shapes=scratch,
        cost_estimate=pl.CostEstimate(flops=0, bytes_accessed=0, transcendentals=0),
        compiler_params=pltpu.CompilerParams(vmem_limit_bytes=VMEM_LIMIT),
    )(*operands)


def scan_forward(heads, x, dt, cum, cum_t, b_t, c_t, of_head, rows):
    span, inner = x.shape
    chunks, padded = span // rows, dt.shape[0]
    at = ChunkSpecs(rows, chunks, False)
    ends = jax.ShapeDtypeStruct((chunks, STATE, inner), F32)
    return chunk_call(
        functools.partial(scan_kernel, heads),
        chunks,
        [
            at.by_row(inner),
            at.by_col(padded),
            at.by_row(padded),
            at.by_col(padded),
            at.by_col(STATE),
            at.by_col(STATE),
            at.whole(of_head),
        ],
        [at.by_row(inner), at.stacked(ends)],
        [jax.ShapeDtypeStruct((span, inner), F32), ends],
        [pltpu.VMEM((STATE, inner), F32)],
        x,
        dt,
        cum,
        cum_t,
        b_t,
        c_t,
        of_head,
    )


def within_kernel(heads, x, dt, cum, cum_t, b_t, c_t, of_head, ends, through, entering, grad, *outs):
    within, grad_bt, grad_ct = outs
    channels = x.shape[1] // heads
    per = HEAD_DIM // channels
    owner = of_head[...]
    cums, cums_t = cum[...], cum_t[...]
    scaled = x[...] * spread(dt[...], owner)
    inner = dot_tn(c_t[...], b_t[...])
    back = grad[...]
    faded = back * jnp.exp(spread(cums_t, owner))
    grad_inner = jnp.zeros_like(inner)
    for at in range(heads // per):
        lanes = slice(at * HEAD_DIM, (at + 1) * HEAD_DIM)
        total = None
        for k in range(per):
            decay = head_decay(cums, cums_t, at * per + k)
            part = dot_fine(decay * inner, back[:, lanes], ((0,), (0,)))
            mine = in_head(part.shape, k, channels)
            total = part if total is None else jnp.where(mine, part, total)
            only = jnp.where(mine, back[:, lanes], 0.0)
            grad_inner += dot_fine(only, scaled[:, lanes], ((1,), (1,))) * decay
        within[:, lanes] = total
    state_in = through[0] * entering[...]
    state_in = state_in + jnp.where(pl.program_id(0) == 0, 0.0, ends[0])
    grad_ct[...] = (
        dot_half(b_t[...], grad_inner, ((1,), (1,))) + dot_fine(state_in, faded, ((1,), (1,)))
    ).astype(B16)
    grad_bt[...] = dot_half(c_t[...], grad_inner)


def scan_within(heads, x, dt, cum, cum_t, b_t, c_t, of_head, ends, through, entering, grad, rows):
    span, inner = x.shape
    chunks, padded = span // rows, dt.shape[0]
    at = ChunkSpecs(rows, chunks, False)
    shape = jax.ShapeDtypeStruct
    return chunk_call(
        functools.partial(within_kernel, heads),
        chunks,
        [
            at.by_row(inner),
            at.by_col(padded),
            at.by_row(padded),
            at.by_col(padded),
            at.by_col(STATE),
            at.by_col(STATE),
            at.whole(of_head),
            at.stacked(ends, -1),
            at.stacked(through),
            at.whole(entering),
            at.by_row(inner),
        ],
        [at.by_row(inner), at.by_col(STATE), at.by_col(STATE)],
        [shape((span, inner), F32), shape((STATE, span), F32), shape((STATE, span), B16)],
        [],
        x,
        dt,
        cum,
        cum_t,
        b_t,
        c_t,
        of_head,
        ends,
        through,
        entering,
        grad,
    )


def across_kernel(
    x,
    x_pre,
    dt,
    cum_t,
    b_t,
    c_t,
    of_head,
    skip,
    ends,
    through,
    entering,
    y,
    grad,
    within,
    bt_part,
    leaving,
    grad_xpre,
    grad_bt,
    grad_logs,
    grad_dt,
    grad_skip,
    grad_state,
):
    @pl.when(pl.program_id(0) == 0)
    def _():
        grad_state[...] = leaving[...]
        grad_skip[...] = jnp.zeros_like(grad_skip)

    owner = of_head[...]
    low_owner = owner.astype(B16)
    times = spread(dt[...], owner)
    values = x[...]
    scaled = values * times
    wide = spread(cum_t[...], owner)
    end = wide[-1:]
    tail = jnp.exp(end - wide)
    back = grad[...]
    to_state = grad_state[...]
    grad_scaled = within[...] + tail * dot_half(b_t[...], to_state, ((0,), (0,)))
    grad_bt[...] = (bt_part[...] + dot_fine(to_state, scaled * tail, ((1,), (1,)))).astype(B16)
    grad_xpre[...] = (grad_scaled * times + skip[...] * back) * silu_slope(x_pre[...])
    grad_skip[...] += jnp.sum(back * values, 0, keepdims=True)
    state_out = ends[0] + through[0] * entering[...]
    at_end = jnp.sum(state_out * to_state, 0, keepdims=True)
    change = back * y[...] - grad_scaled * scaled
    rows = lax.broadcasted_iota(jnp.int32, change.shape, 0)
    change = change + jnp.where(rows == change.shape[0] - 1, at_end, 0.0)
    per_head = dot_half(low_owner, change, ((1,), (1,)))
    length = change.shape[0]
    later = lax.broadcasted_iota(jnp.int32, (length, length), 0) >= lax.broadcasted_iota(
        jnp.int32, (length, length), 1
    )
    grad_logs[...] = dot_exact(per_head, later.astype(F32))
    grad_dt[...] = dot_half(low_owner, grad_scaled * values, ((1,), (1,)))
    faded = back * jnp.exp(wide)
    grad_state[...] = jnp.exp(end) * to_state + dot_half(c_t[...], faded)


def scan_across(
    x,
    x_pre,
    dt,
    cum_t,
    b_t,
    c_t,
    of_head,
    skip,
    ends,
    through,
    entering,
    y,
    grad,
    within,
    bt_part,
    leaving,
    rows,
):
    span, inner = x.shape
    chunks, padded = span // rows, dt.shape[0]
    at = ChunkSpecs(rows, chunks, True)
    shape = jax.ShapeDtypeStruct
    return chunk_call(
        across_kernel,
        chunks,
        [
            at.by_row(inner),
            at.by_row(inner),
            at.by_col(padded),
            at.by_col(padded),
            at.by_col(STATE),
            at.by_col(STATE),
            at.whole(of_head),
            at.whole(skip),
            at.stacked(ends),
            at.stacked(through, 1),
            at.whole(entering),
            at.by_row(inner),
            at.by_row(inner),
            at.by_row(inner),
            at.by_col(STATE),
            at.whole(leaving),
        ],
        [
            at.by_row(inner),
            at.by_col(STATE),
            at.by_col(padded),
            at.by_col(padded),
            at.whole(skip),
        ],
        [
            shape((span, inner), F32),
            shape((STATE, span), B16),
            shape((padded, span), F32),
            shape((padded, span), F32),
            shape(skip.shape, F32),
        ],
        [pltpu.VMEM((STATE, inner), F32)],
        x,
        x_pre,
        dt,
        cum_t,
        b_t,
        c_t,
        of_head,
        skip,
        ends,
        through,
        entering,
        y,
        grad,
        within,
        bt_part,
        leaving,
    )


def flat(x):
    return with_layout_constraint(x, Layout(tuple(range(x.ndim))))


def cotangent_half(cotangent):
    return own_half(cotangent).astype(F32)


def home_kernel(runs, index, *refs):
    blocks, outs = refs[: -len(runs)], refs[-len(runs) :]
    for k, block in enumerate(blocks):
        at = 0
        for out, (width, across) in zip(outs, runs):
            piece = block[:, at : at + width].astype(F32)
            at += width
            place = pl.ds(pl.multiple_of(index[k] * width, width), width)
            if across:
                out[:, place] = piece
            else:
                out[place] = piece.T


def homed(blocks, *runs):
    count, piece = len(blocks), blocks[0].shape[0]
    shapes = [(piece, count * w) if across else (count * w, piece) for w, across in runs]
    shapes = [jax.ShapeDtypeStruct(shape, F32) for shape in shapes]
    index = jnp.stack(near_places()).astype(jnp.int32)
    return whole_call(functools.partial(home_kernel, runs), shapes, [], index, *blocks)


def per_device(
    tokens,
    cotangent,
    g1,
    w_q,
    w_k,
    w_v,
    w_o,
    w_z,
    w_x,
    w_bc,
    w_dt,
    conv_bc,
    conv_bc_bias,
    w_out,
    g2,
    w_gate,
    w_up,
    w_down,
    conv_x,
    conv_x_bias,
    dt_bias,
    a_log,
    d_skip,
):
    near, groups = lax.axis_size("near"), lax.axis_size("group")
    here, group, core = (lax.axis_index(a) for a in ("near", "group", "head"))
    rows, width = tokens.shape
    span = near * rows
    piece = w_q.shape[0]
    devices = near * groups
    key_cols = HEAD_DIM // near
    half_cols = key_cols // 2
    heads = w_dt.shape[1] // near
    padded = heads + -heads % 8
    inner, q_cols, ff = w_z.shape[1] // near, w_q.shape[1] // near, w_gate.shape[1] // near
    o_rows = w_o.shape[0] // near
    at_q = 2 * inner // q_cols

    def columns(w):
        return w.reshape(w.shape[0], near, -1).transpose(1, 0, 2)

    def share(x, dim):
        size = x.shape[dim] // near
        return lax.dynamic_slice_in_dim(x, here * size, size, dim)

    def by_head(x):
        return jnp.pad(share(x, 0).astype(F32), (0, padded - heads))[:, None]

    k_cols = w_k.reshape(piece, 2, near, half_cols).transpose(2, 0, 1, 3)
    w_bc_mine = lax.dynamic_slice_in_dim(w_bc, core * STATE, STATE, 1)
    pack1 = [columns(w_x), k_cols.reshape(near, piece, key_cols), columns(w_v)]
    pack1 = jnp.concatenate([*pack1, columns(w_bc_mine)], 2)
    extra = jnp.concatenate([g1, g2, conv_bc.reshape(-1), conv_bc_bias])
    n_small, n_dt = extra.shape[0], heads * piece
    extra = jnp.broadcast_to(extra, (near, n_small))
    extra = jnp.concatenate([extra, w_dt.T.reshape(near, n_dt)], 1)
    extra = jnp.pad(extra, ((0, 0), (0, -extra.shape[1] % (8 * pack1.shape[2]))))
    pack1 = jnp.concatenate([pack1, extra.reshape(near, -1, pack1.shape[2])], 1)
    full1 = jnp.broadcast_to(pack1, (groups, *pack1.shape)).reshape(devices, *pack1.shape[1:])
    full1 = trade_all(full1)
    token_parts = sent_tokens(own_half(tokens))
    pack2 = [columns(w_z), columns(w_out.T), columns(w_q), columns(w_o.T)]
    pack2 = jnp.concatenate(pack2, 2)
    pack3 = jnp.concatenate([columns(w_gate), columns(w_up), columns(w_down.T)], 2)
    sent2 = sent_near(pack2)
    positions = (group * span + jnp.arange(span)).astype(F32)
    half = HEAD_DIM // 2
    freqs = ROPE_BASE ** (-jnp.arange(half, dtype=F32) / half)
    angle = positions[:, None] * freqs[None, :]
    cos_q, sin_q = jnp.cos(angle), jnp.sin(angle)
    cos_k, sin_k = (share(x, 1).T for x in (cos_q, sin_q))
    of_head = jnp.arange(inner)[None, :] // (inner // heads) == jnp.arange(padded)[:, None]
    of_head = of_head.astype(F32)
    decay_rate, head_bias = jnp.exp(by_head(a_log)), by_head(dt_bias)
    skip = spread(by_head(d_skip), of_head)
    triangle = jnp.triu(jnp.ones((rows, rows), F32))
    taps_x = share(conv_x, 1).astype(F32)[:, None, :]
    bias_x = share(conv_x_bias, 0).astype(F32)[None, :]
    my_tokens = own_half(tokens).astype(F32)
    early = (cos_q, sin_q, cos_k, sin_k, of_head, decay_rate, head_bias, skip, triangle)
    early = (*early, taps_x, bias_x, my_tokens, pack3)
    full1, early = lax.optimization_barrier((full1, early))
    cos_q, sin_q, cos_k, sin_k, of_head, decay_rate, head_bias, skip, triangle = early[:9]
    taps_x, bias_x, my_tokens, pack3 = early[9:]

    extra = full1[:, piece:].reshape(devices, -1)
    smalls = extra[:, :n_small].astype(F32)
    gain1 = smalls[:, :piece].reshape(-1)
    gain2 = smalls[:, piece : 2 * piece].reshape(-1)
    full_dt = extra[:, n_small : n_small + n_dt].reshape(devices, heads, piece)
    full_dt = full_dt.transpose(1, 0, 2).reshape(heads, width)
    full_dt = jnp.pad(full_dt, ((0, padded - heads), (0, 0)))
    taps_bc = smalls[:, 2 * piece : -conv_bc_bias.shape[0]].reshape(devices, CONV, -1)
    taps_bc = taps_bc.transpose(1, 0, 2).reshape(CONV, 2, near, -1)
    taps_bc = taps_bc[:, core, here][:, :, None]
    bias_bc = smalls[:, -conv_bc_bias.shape[0] :].reshape(2, near, -1)[core, here][:, None]
    full1 = full1[:, :piece].reshape(width, -1)
    full_x, full_kvbc = full1[:, :inner], full1[:, inner:]
    n1 = placed_tokens(token_parts, gain1)
    grad_parts = sent_tokens(after(own_half(cotangent), n1))

    kvbc = dot(full_kvbc, n1, ((0,), (1,)))
    k_first, k_second = rotate_pair(kvbc[:half_cols], kvbc[half_cols:key_cols], cos_k, sin_k)
    kv = jnp.concatenate([k_first, k_second, kvbc[key_cols : 2 * key_cols]], 0).astype(B16)
    kv = flat(kv)
    kv_parts = [kv] + [step_group(kv, r) for r in range(1, groups)]
    bc_proj = flat(kvbc[2 * key_cols :])
    bc_edge = step_group(bc_proj[:, span - CONV + 1 :], 1)
    sent2, n1, kv = lax.optimization_barrier((sent2, n1, kv))
    full2 = placed(near_places(), sent2).reshape(near * piece, -1)
    n1_x, full2 = lax.optimization_barrier((n1, full2))
    full2 = lax.all_gather(full2, "group", axis=0, tiled=True)

    x_proj = dot(n1_x, full_x)
    x_edge = step_group(x_proj[span - CONV + 1 :], 1)
    sent3 = sent_near(after(pack3, x_proj))

    bc_pre = conv(bc_proj, bc_edge, taps_bc, bias_bc, 1)
    bc_mine = gather_near(flat(jax.nn.silu(bc_pre).astype(B16))).reshape(STATE, span)
    bc_other = swap_cores(bc_mine)
    first = core == 0
    b_t, c_t = jnp.where(first, bc_mine, bc_other), jnp.where(first, bc_other, bc_mine)

    dt_pre = dot_nt(full_dt, n1) + head_bias
    dt = jax.nn.softplus(dt_pre)
    logs = -dt * decay_rate
    cum_t = dot_exact(logs.reshape(padded * near, rows), triangle).reshape(padded, near, rows)
    chunk_total = cum_t[:, :, -1]
    before = jnp.cumsum(chunk_total, 1) - chunk_total
    group_total = jnp.sum(chunk_total, 1, keepdims=True)
    fade = jnp.exp(spread((cum_t + before[:, :, None]).reshape(padded, span), of_head))
    cum_t = cum_t.reshape(padded, span)
    cum = cum_t.T
    group_decay = jnp.exp(spread(group_total, of_head))

    x_pre = conv(x_proj, x_edge, taps_x, bias_x, 0)
    xc = jax.nn.silu(x_pre)
    kv_parts = jnp.concatenate(kv_parts, 0)
    xc = after(xc, kv_parts, *grad_parts)
    sent3, xc = lax.optimization_barrier((sent3, xc))
    full3 = placed(near_places(), sent3).reshape(near * piece, -1)
    xc, full3 = lax.optimization_barrier((xc, full3))
    full3 = lax.all_gather(full3, "group", axis=0, tiled=True)
    kv_parts = [to_near(kv_parts, k) if k else kv_parts for k in range(near)]
    outputs, ends = scan_forward(heads, xc, dt, cum, cum_t, b_t, c_t, of_head, rows)
    through = jnp.concatenate([jnp.zeros_like(group_total), jnp.cumsum(chunk_total, 1)], 1)
    through = jnp.exp(spread(through, of_head))[:, None]

    def state_rows(state):
        pad = jnp.broadcast_to(group_decay, (16, inner))
        return jnp.concatenate([state, pad], 0).astype(B16)

    def sent_states(state, direction):
        return [step_group(state, direction * r) for r in range(1, groups)]

    def chained(parts):
        total = jnp.zeros((STATE, inner), F32)
        for part in reversed(parts):
            part = part.astype(F32)
            total = part[STATE : STATE + 1] * total + part[:STATE]
        return total

    entering = sent_states(state_rows(ends[-1]), 1)
    full_z, full_out_t = full2[:, :inner], full2[:, inner : 2 * inner]
    full_q, full_o_t = full2[:, 2 * inner : 2 * inner + q_cols], full2[:, 2 * inner + q_cols :]
    full_gu, full_down_t = full3[:, : 2 * ff], full3[:, 2 * ff :]
    q_proj = dot(n1, full_q)
    queries = jnp.concatenate(rotate_pair(q_proj[:, :half], q_proj[:, half:], cos_q, sin_q), 1)
    queries = queries.astype(B16)
    z_proj = dot(n1, full_z)
    index = jnp.stack([group, *near_places()]).astype(jnp.int32)
    attended32, lse, keys_t, values_t = attend(index, queries, kv_parts)
    attended = attended32.astype(B16)
    entering = chained(after(entering, attended, z_proj))

    outputs = outputs + fade * dot_tn(c_t, entering.astype(B16))
    y = outputs + skip * xc
    gated = (y * jax.nn.silu(z_proj)).astype(B16)

    pairs = [(gated, (full2, 1)), (attended, (full2, at_q + 1))]
    blocks = partial_tokens(width, pairs)
    all_cotangent = placed_tokens(after(grad_parts, blocks))
    mixed, all_cotangent = scatter_tokens(blocks, alongside=all_cotangent)
    hidden = my_tokens + mixed
    normed2, unit2, factor2 = normalize(hidden, gain2)
    n2 = gather_tokens(normed2.astype(B16))
    both = dot(n2, full_gu)
    gate, up = both[:, :ff], both[:, ff:]
    sigma = jax.nn.sigmoid(gate)
    act = (gate * sigma * up).astype(B16)
    grad_act = dot(all_cotangent, full_down_t)
    grad_gate = grad_act * up * sigma * (1.0 + gate * (1.0 - sigma))
    grad_gu = jnp.concatenate([grad_gate, grad_act * gate * sigma], 1).astype(B16)

    def sum_groups(grad):
        own = lax.psum_scatter(grad, "group", scatter_dimension=0, tiled=True)
        return own.reshape(near, piece, -1)

    partial2 = partial_tokens(width, [(grad_gu, (full3, 0))])
    grads3 = dot_tn(n2, grad_gu).astype(B16)
    grad_n2, (grads3, feed) = scatter_tokens(
        partial2, alongside=(grads3, summed_dots(width, (act, (full3, 2))))
    )
    home3 = sum_groups(grads3)

    grad_norm2, grad_g2 = norm_back(grad_n2, unit2, factor2, gain2)
    grad_hidden = cotangent_half(cotangent) + grad_norm2
    grad_mixed = gather_tokens(grad_hidden.astype(B16))

    grad_gated = dot(grad_mixed, full_out_t).astype(B16).astype(F32)
    sig_z = jax.nn.sigmoid(z_proj)
    grad_y = grad_gated * z_proj * sig_z
    grad_z = (grad_gated * y * sig_z * (1.0 + z_proj * (1.0 - sig_z))).astype(B16)
    read = state_rows(dot(c_t, (grad_y * fade).astype(B16)))
    read_parts = sent_states(read, -1)

    grad_mixed = after(grad_mixed, read)
    grad_attended = dot(grad_mixed, full_o_t).astype(B16)
    delta = jnp.sum(grad_attended.astype(F32) * attended32, 1, keepdims=True)
    grad_q, kv_parts = attend_back(
        index, queries, keys_t, values_t, grad_attended, lse, delta
    )
    kv_parts = [to_near(p, k) if k else p for k, p in enumerate(kv_parts)]
    grad_q = grad_q * HEAD_DIM**-0.5
    grad_q = jnp.concatenate(rotate_pair(grad_q[:, :half], grad_q[:, half:], cos_q, -sin_q), 1)
    grad_zq = jnp.concatenate([grad_z, grad_q.astype(B16)], 1)
    mixer_out = jnp.concatenate([gated, attended], 1)
    read_parts, grad_zq = lax.optimization_barrier((read_parts, grad_zq))
    grads2 = joined_grads((all_cotangent, act), (grad_mixed, mixer_out), (n1, grad_zq))
    home2 = sum_groups(grads2)

    kv_parts, grads2 = lax.optimization_barrier((kv_parts, grads2))
    kv_parts = flat(added(kv_parts))
    kv_sent = kv_parts.astype(B16)
    kv_rows = 2 * key_cols
    grad_kv = [kv_parts[:kv_rows]]
    for r in range(1, groups):
        grad_kv.append(step_group(kv_sent[r * kv_rows : (r + 1) * kv_rows], -r))
    feed = met_tokens(*after(feed, kv_sent))

    feed, grad_y_scan = lax.optimization_barrier((feed, grad_y))
    within, bt_part, grad_ct = scan_within(
        heads, xc, dt, cum, cum_t, b_t, c_t, of_head, ends, through, entering, grad_y_scan, rows
    )
    feed = [to_near(b, k) if k else b for k, b in enumerate(feed)]
    home3 = sent_near(after(home3, kv_sent))
    read_parts, within, home3, feed = lax.optimization_barrier((read_parts, within, home3, feed))
    leaving = chained(read_parts)
    grad_xpre, grad_bt, grad_logs, grad_dt, grad_skip = scan_across(
        xc,
        x_pre,
        dt,
        cum_t,
        b_t,
        c_t,
        of_head,
        skip,
        ends,
        through,
        entering,
        outputs,
        grad_y,
        within,
        bt_part,
        leaving,
        rows,
    )
    kept = jnp.where(first, grad_bt, grad_ct)
    given = swap_cores(jnp.where(first, grad_ct, grad_bt))
    kept = (kept.astype(F32) + given.astype(F32)).astype(B16)
    grad_bc = flat(added(sent_near(kept.reshape(near, -1, span))))

    grad_bcpre = grad_bc * silu_slope(bc_pre)
    next_x = step_group(grad_xpre[: CONV - 1], -1)
    next_bc = step_group(grad_bcpre[:, : CONV - 1], -1)
    grad_x, grad_tapx, grad_biasx = conv_back(grad_xpre, next_x, x_proj, x_edge, taps_x, 0)
    grad_bcp, grad_tapbc, grad_biasbc = conv_back(
        grad_bcpre, next_bc, bc_proj, bc_edge, taps_bc, 1
    )
    grad_kv = added(after(grad_kv, grad_xpre))
    gk_first, gk_second = rotate_pair(
        grad_kv[:half_cols], grad_kv[half_cols:key_cols], cos_k, -sin_k
    )
    grad_kvbc = jnp.concatenate([gk_first, gk_second, grad_kv[key_cols:], grad_bcp], 0)
    grad_first = jnp.concatenate([grad_x.astype(B16), flat(grad_kvbc.astype(B16)).T], 1)

    grad_dt = grad_dt - grad_logs * decay_rate
    grad_dt_pre = grad_dt * jax.nn.sigmoid(dt_pre)
    grad_dt_low = grad_dt_pre.astype(B16)
    grad_skip = dot_exact(of_head, grad_skip, ((1,), (1,)))[:heads, 0]
    grad_alog = jnp.sum(grad_logs * logs, 1)[:heads]
    grad_dtbias = jnp.sum(grad_dt_pre, 1)[:heads]

    grads1 = dot_tn(n1, grad_first).astype(B16)
    grad_first, grads1 = lax.optimization_barrier((grad_first, grads1))
    grad_wdt = dot(grad_dt_low, n1).reshape(padded, devices, piece).transpose(1, 0, 2)
    pairs = [
        (grad_zq[:, :inner], (full2, 0)),
        (grad_zq[:, inner:], (full2, at_q)),
        (grad_first, (full1, 0)),
        (grad_dt_low.T, full_dt),
    ]
    partial1 = partial_tokens(width, pairs)
    output = (hidden + added(after(feed, partial1))).astype(B16)
    output = both_halves(output, swap_cores(output), 0)
    outs3 = homed(after(home3, partial1), (ff, True), (ff, True))
    grad_n1, (sum_wgate, sum_wup, output) = scatter_tokens(partial1, alongside=(*outs3, output))
    _, unit1, factor1 = normalize(my_tokens, gain1)
    grad_norm1, grad_g1 = norm_back(grad_n1, unit1, factor1, gain1)
    grad_tokens = grad_hidden + grad_norm1

    grad_tokens = both_halves(grad_tokens, swap_cores(grad_tokens), 0)

    crossing = jnp.concatenate([grad_g1, grad_g2, grad_tapbc.reshape(-1), grad_biasbc])
    other = swap_cores(crossing)
    gains = 2 * width
    mine = [grad_tapx.reshape(-1), grad_biasx, grad_dtbias, grad_alog, grad_skip]
    mine = [*mine, both_halves(crossing[gains:], other[gains:], 0)]
    ends, at = [], 0
    for g in mine[:-1]:
        at += g.shape[0]
        ends.append(at)
    packed = jnp.concatenate(mine)
    size = packed.shape[0]
    packed = jnp.broadcast_to(packed, (devices, size))
    own_parts = [crossing[:width] + other[:width], crossing[width:gains] + other[width:gains]]
    own_parts = [grad_wdt.reshape(devices, -1), *(p.reshape(devices, -1) for p in own_parts)]
    packed = jnp.concatenate([*own_parts, packed], 1)
    packed = jnp.pad(packed, ((0, 0), (0, -packed.shape[1] % (8 * HEAD_DIM))))
    packed = trade_all(packed.reshape(devices, -1, HEAD_DIM))
    home1 = grads1.reshape(groups, near * piece, -1)
    home1 = [lax.dynamic_index_in_dim(home1, (group + r) % groups, 0, False) for r in range(groups)]
    home1 = [around(b, r) if r else b for r, b in enumerate(home1)]
    home2 = sent_near(after(home2, grad_n1))
    home1, home2 = lax.optimization_barrier((home1, home2))
    home1 = sent_near(added(home1).astype(B16).reshape(near, piece, -1))
    packed, home1 = lax.optimization_barrier((packed, home1))
    packed = packed.reshape(devices, -1)
    n_dt = padded * piece
    sum_wdt = jnp.sum(packed[:, :n_dt].reshape(groups, near, padded, piece), 0)
    sum_wdt = sum_wdt[:, :heads].reshape(-1, piece).T
    own_sums = jnp.sum(packed[:, n_dt : n_dt + 2 * piece], 0)
    packed = packed[:, n_dt + 2 * piece :][:, :size]

    sum_wdown, sum_wout, sum_wo, sum_wz, sum_wq = homed(
        home2, (ff, False), (inner, False), (o_rows, False), (inner, True), (q_cols, True)
    )
    (sum_wx,) = homed(home1, (inner, True))
    home_small = placed(near_places(), [b[:, inner:] for b in home1]).astype(F32)
    home_k, home_v, home_bc = jnp.split(home_small, [key_cols, 2 * key_cols], 2)
    sum_wv = home_v.transpose(1, 0, 2).reshape(piece, -1)
    sum_wk = home_k.reshape(near, piece, 2, half_cols).transpose(1, 2, 0, 3)
    sum_wk = sum_wk.reshape(piece, -1)
    bc_mine = home_bc.transpose(1, 0, 2).reshape(piece, -1)
    sum_wbc = both_halves(bc_mine, swap_cores(bc_mine), 1)

    every = jnp.split(packed, ends, 1)
    place = group * near + here

    def by_near(x):
        return jnp.sum(x.reshape(groups, near, -1), 0)

    sum_g1, sum_g2 = own_sums[:piece], own_sums[piece:]
    sum_convx = by_near(every[0]).reshape(near, CONV, -1).transpose(1, 0, 2).reshape(CONV, -1)
    sum_convxb, sum_dtbias, sum_alog, sum_dskip = (by_near(x).reshape(-1) for x in every[1:5])
    sum_bc = by_near(every[5]).reshape(near, 2, CONV + 1, -1).transpose(2, 1, 0, 3)
    sum_bc = sum_bc.reshape(CONV + 1, -1)
    bc_cols = conv_bc.shape[1]
    sum_bc = lax.dynamic_slice_in_dim(sum_bc, place * bc_cols, bc_cols, 1)
    return (
        output,
        grad_tokens,
        sum_g1,
        sum_wq,
        sum_wk,
        sum_wv,
        sum_wo,
        sum_wz,
        sum_wx,
        sum_wbc,
        sum_wdt,
        sum_bc[:CONV],
        sum_bc[CONV],
        sum_wout,
        sum_g2,
        sum_wgate,
        sum_wup,
        sum_wdown,
        sum_convx,
        sum_convxb,
        sum_dtbias,
        sum_alog,
        sum_dskip,
    )


def solution(mesh):
    seq, cores = mesh.shape["seq"], mesh.shape["head"]
    near = math.gcd(seq, 4)
    split = Mesh(mesh.devices.reshape(seq // near, near, cores), ("group", "near", "head"))
    seq = ("group", "near")
    row_split = P(seq, "head")
    col_split = P("head", seq)
    weights = (
        P(seq),
        row_split,
        row_split,
        row_split,
        col_split,
        row_split,
        row_split,
        P(seq, None),
        row_split,
        P(None, seq),
        P(seq),
        col_split,
        P(seq),
        row_split,
        row_split,
        col_split,
        P(None, "head"),
        P("head"),
        P("head"),
        P("head"),
        P("head"),
    )
    tokens = P(seq, None)
    return jax.shard_map(
        per_device,
        mesh=split,
        in_specs=(tokens, tokens, *weights),
        out_specs=(tokens, tokens, *weights),
        check_vma=False,
    )
```

```python
import functools
import math

import jax
import jax.numpy as jnp
from jax import lax
from jax.experimental import pallas as pl
from jax.experimental.layout import Layout, with_layout_constraint
from jax.experimental.pallas import tpu as pltpu
from jax.sharding import Mesh, PartitionSpec as P

HEAD_DIM = 128
STATE = 256
CONV = 4
EPS = 1e-05
ROPE_BASE = 100000000000.0
MASKED = -1e30
HIGHEST = lax.Precision.HIGHEST
F32 = jnp.float32
B16 = jnp.bfloat16
ATTEND_ROWS = 256
ATTEND_KEYS = 512
VMEM_LIMIT = 40 << 20


def after(x, *earlier):
    return lax.optimization_barrier((x, earlier))[0]


def swap_cores(x):
    return lax.ppermute(x, "head", [(0, 1), (1, 0)])


def to_near(x, k):
    return lax.ppermute(x, "near", [(i, i ^ k) for i in range(lax.axis_size("near"))])


def around(x, distance):
    count = lax.axis_size("group")
    return lax.ppermute(x, "group", [(i, (i + distance) % count) for i in range(count)])


def step_group(x, distance):
    count = lax.axis_size("group")
    route = [(i, i + distance) for i in range(count) if 0 <= i + distance < count]
    return lax.ppermute(x, "group", route)


def place_kernel(count, index, *refs):
    for k, block in enumerate(refs[:count]):
        at = 0
        for out in refs[count:]:
            cols = slice(at, at + out.shape[-1])
            out[index[k]] = block[..., cols]
            at = cols.stop


def placed(index, blocks, widths=None):
    block = blocks[0]
    shapes = [
        jax.ShapeDtypeStruct((len(blocks), *block.shape[:-1], w), block.dtype)
        for w in widths or block.shape[-1:]
    ]
    kernel = functools.partial(place_kernel, len(blocks))
    out = whole_call(kernel, shapes, [], jnp.stack(index).astype(jnp.int32), *blocks)
    return out if widths else out[0]


def near_places():
    here = lax.axis_index("near")
    return [here ^ k for k in range(lax.axis_size("near"))]


def sent_near(x):
    blocks = [lax.dynamic_index_in_dim(x, at, 0, False) for at in near_places()]
    return [to_near(b, k) if k else b for k, b in enumerate(blocks)]


def trade_near(x):
    return placed(near_places(), sent_near(x))


def added(blocks):
    total = blocks[0].astype(F32)
    for block in blocks[1:]:
        total = total + block.astype(F32)
    return total


def gather_near(x):
    places = near_places()
    return placed(places, [x] + [to_near(x, k) for k in range(1, len(places))])


def trade_all(x):
    return lax.all_to_all(x, ("group", "near"), 0, 0, tiled=True)


def both_halves(mine, other, dim):
    first = lax.axis_index("head") == 0
    return jnp.concatenate([jnp.where(first, mine, other), jnp.where(first, other, mine)], dim)


def own_half(x):
    half = x.shape[0] // 2
    return lax.dynamic_slice_in_dim(x, lax.axis_index("head") * half, half, 0)


def normalized(value, gain):
    value = value.astype(F32)
    power = jnp.mean(value * value, 1, keepdims=True)
    return (value * lax.rsqrt(power + EPS) * gain).astype(B16)


def tokens_kernel(index, *refs):
    *refs, out = refs
    count = len(refs) // 2
    for k in range(count):
        for side in range(2):
            out[index[k], index[count + side]] = refs[k + side * count][...]


def normed_kernel(index, *refs):
    *refs, gain, out, halo = refs
    count, rows = len(refs) // 2, out.shape[2]
    for k in range(count):
        for side in range(2):
            value = refs[k + side * count][:rows]
            out[index[k], index[count + side]] = normalized(value, gain[...])

        @pl.when(index[k] == count - 1)
        def _():
            halo[...] = normalized(refs[k][rows:], gain[...])


def sent_tokens(mine):
    got = [mine] + [to_near(mine, k) for k in range(1, lax.axis_size("near"))]
    return [*got, *map(swap_cores, got)]


def tokens_index():
    core = lax.axis_index("head")
    return jnp.stack([*near_places(), core, 1 - core]).astype(jnp.int32)


def placed_tokens(parts):
    rows, width = parts[0].shape
    shape = jax.ShapeDtypeStruct((len(parts) // 2, 2, rows, width), parts[0].dtype)
    return whole_call(tokens_kernel, shape, [], tokens_index(), *parts).reshape(-1, width)


def normed_tokens(parts, gain, more):
    rows, width = parts[0].shape[0] - more, parts[0].shape[1]
    shapes = [
        jax.ShapeDtypeStruct((len(parts) // 2, 2, rows, width), B16),
        jax.ShapeDtypeStruct((more, width), B16),
    ]
    out, halo = whole_call(normed_kernel, shapes, [], tokens_index(), *parts, gain[None, :])
    return out.reshape(-1, width), halo


def gather_tokens(mine):
    return placed_tokens(sent_tokens(mine))


def dots_kernel(turned, core, *refs):
    *refs, give, keep = refs
    pairs = len(turned)
    for out, side in (give, 1 - core[0]), (keep, core[0]):
        lefts = []
        for left in refs[:pairs]:
            blocks = [left[j, side] for j in range(left.shape[0])]
            lefts.append(jnp.concatenate(blocks, 0))
        width = out.shape[1]
        tile = min(width, 512)
        for n in range(width // tile):
            cols = slice(n * tile, (n + 1) * tile)
            total = None
            for left, right, turn in zip(lefts, refs[pairs:], turned):
                part = dot_nt(left, right[cols]) if turn else dot(left, right[:, cols])
                total = part if total is None else total + part
            out[:, cols] = total.astype(B16)


def summed_dots(width, *pairs):
    lefts, rights, specs, turned, work = [], [], [], [], 0
    near = lax.axis_size("near")
    for left, right in pairs:
        span, depth = left.shape
        lefts.append(left.reshape(near, 2, span // near // 2, depth))
        turned.append(isinstance(right, tuple))
        array, at = right if turned[-1] else (right, 0)
        shape = (width, depth) if turned[-1] else array.shape
        specs.append(pl.BlockSpec(shape, lambda i, at=at: (0, at)))
        rights.append(array)
        work += 2 * span * width * depth
    smem = pl.BlockSpec(memory_space=pltpu.SMEM)
    wholes = [pl.BlockSpec(a.shape, lambda i: (0, 0, 0, 0)) for a in lefts]
    shape = (lefts[0].shape[0] * lefts[0].shape[2], width)
    return pl.pallas_call(
        functools.partial(dots_kernel, turned),
        grid=(1,),
        in_specs=[smem, *wholes, *specs],
        out_specs=[pl.BlockSpec(shape, lambda i: (0, 0))] * 2,
        out_shape=[jax.ShapeDtypeStruct(shape, B16)] * 2,
        cost_estimate=pl.CostEstimate(flops=0, bytes_accessed=0, transcendentals=0),
        compiler_params=pltpu.CompilerParams(vmem_limit_bytes=VMEM_LIMIT),
    )(lax.axis_index("head").astype(jnp.int32).reshape(1), *lefts, *rights)


def grads_kernel(count, *refs):
    *refs, out = refs
    at = 0
    for left, right in zip(refs[:count], refs[count:]):
        cols = slice(at, at + right.shape[1])
        out[:, cols] = dot_tn(left[...], right[...]).astype(B16)
        at = cols.stop


def joined_grads(*pairs):
    lefts, rights = zip(*pairs)
    span, width = lefts[0].shape
    total = sum(r.shape[1] for r in rights)
    tile = min(width, 512)
    return pl.pallas_call(
        functools.partial(grads_kernel, len(pairs)),
        grid=(width // tile,),
        in_specs=[pl.BlockSpec((span, tile), lambda i: (0, i))] * len(pairs)
        + [pl.BlockSpec(r.shape, lambda i: (0, 0)) for r in rights],
        out_specs=pl.BlockSpec((tile, total), lambda i: (i, 0)),
        out_shape=jax.ShapeDtypeStruct((width, total), B16),
        cost_estimate=pl.CostEstimate(flops=0, bytes_accessed=0, transcendentals=0),
        compiler_params=pltpu.CompilerParams(vmem_limit_bytes=VMEM_LIMIT),
    )(*lefts, *rights)


def meet_kernel(index, keep, got, *outs):
    rows = outs[0].shape[0]
    for k, out in enumerate(outs):
        part = pl.ds(pl.multiple_of(index[k] * rows, rows), rows)
        out[...] = (keep[part].astype(F32) + got[part].astype(F32)).astype(B16)


def partial_tokens(width, pairs):
    return met_tokens(*summed_dots(width, *pairs))


def met_tokens(give, keep):
    places = near_places()
    got = swap_cores(give)
    rows, width = keep.shape[0] // len(places), keep.shape[1]
    shapes = [jax.ShapeDtypeStruct((rows, width), B16)] * len(places)
    index = jnp.stack(places).astype(jnp.int32)
    return whole_call(meet_kernel, shapes, [], index, keep, got)


def scatter_tokens(blocks, alongside=None):
    blocks = [to_near(b, k) if k else b for k, b in enumerate(blocks)]
    if alongside is not None:
        blocks, alongside = lax.optimization_barrier((blocks, alongside))
    return added(blocks), alongside


def dot(left, right, dims=((1,), (0,))):
    return lax.dot_general(left, right, (dims, ((), ())), preferred_element_type=F32)


def dot_nt(left, right):
    return dot(left, right, ((1,), (1,)))


def dot_tn(left, right):
    return dot(left, right, ((0,), (0,)))


def dot_exact(left, right, dims=((1,), (0,))):
    return lax.dot_general(
        left, right, (dims, ((), ())), precision=HIGHEST, preferred_element_type=F32
    )


def normalize(values, gain):
    factor = lax.rsqrt(jnp.mean(values * values, -1, keepdims=True) + EPS)
    unit = values * factor
    return unit * gain, unit, factor


def norm_back(grad_out, unit, factor, gain):
    grad_unit = grad_out * gain[None, :]
    grad_in = factor * (grad_unit - unit * jnp.mean(grad_unit * unit, -1, keepdims=True))
    return grad_in, jnp.sum(grad_out * unit, 0)


def rotate_pair(first, second, cosine, sine):
    return first * cosine - second * sine, second * cosine + first * sine


def conv(inputs, edge, weight, bias, dim):
    length = inputs.shape[dim]
    padded = jnp.concatenate([edge, inputs], dim)
    total = bias
    for tap in range(CONV):
        total = total + weight[tap] * lax.slice_in_dim(padded, tap, tap + length, axis=dim)
    return total


def conv_back(grad, grad_edge, weight, dim):
    length = grad.shape[dim]
    late = jnp.concatenate([grad, grad_edge], dim)
    total = 0.0
    for tap in range(CONV):
        back = CONV - 1 - tap
        total = total + weight[tap] * lax.slice_in_dim(late, back, back + length, axis=dim)
    return total


def taps_back(grad, inputs, edge, dim):
    length = inputs.shape[dim]
    padded = jnp.concatenate([edge, inputs], dim)
    taps = []
    for tap in range(CONV):
        taps.append(jnp.sum(grad * lax.slice_in_dim(padded, tap, tap + length, axis=dim), dim))
    return jnp.stack(taps), jnp.sum(grad, dim)


def silu_slope(v):
    s = jax.nn.sigmoid(v)
    return s * (1.0 + v * (1.0 - s))


def row_block(i):
    return slice(i * ATTEND_ROWS, (i + 1) * ATTEND_ROWS)


def attend_kernel(index, q, *refs):
    *parts, out, lse, k_t, v_t, total, top, mass = refs
    span = q.shape[0]
    wide = min(ATTEND_KEYS, span)
    keys = HEAD_DIM // len(parts)
    half = keys // 2

    @pl.loop(0, index[0] + 1)
    def _(r):
        for k, part in enumerate(parts):
            at = pl.multiple_of(index[k + 1] * half, half)
            own = pl.multiple_of(r * 2 * keys, 2 * keys)
            k_t[r, pl.ds(at, half)] = part[pl.ds(own, half)]
            k_t[r, pl.ds(at + HEAD_DIM // 2, half)] = part[pl.ds(own + half, half)]
            at = pl.multiple_of(index[k + 1] * keys, keys)
            v_t[r, pl.ds(at, keys)] = part[pl.ds(own + keys, keys)]

    @pl.loop(index[0] + 1, k_t.shape[0])
    def _(r):
        k_t[r] = jnp.zeros(k_t.shape[1:], B16)
        v_t[r] = jnp.zeros(v_t.shape[1:], B16)

    def meet(i, keys_t, values_t, first):
        scores = dot(q[row_block(i)], keys_t) * HEAD_DIM**-0.5
        if first:
            rows = i * ATTEND_ROWS + lax.broadcasted_iota(jnp.int32, scores.shape, 0)
            cols = lax.broadcasted_iota(jnp.int32, scores.shape, 1)
            scores = jnp.where(cols <= rows, scores, MASKED)
        peak = jnp.max(scores, 1, keepdims=True)
        if not first:
            old = top[row_block(i)]
            peak = jnp.maximum(old, peak)
            fade = jnp.exp(old - peak)
        probs = jnp.exp(scores - peak)
        weight = jnp.sum(probs, 1, keepdims=True)
        read = dot_nt(probs.astype(B16), values_t)
        if not first:
            weight = weight + fade * mass[row_block(i)]
            read = read + fade * total[row_block(i)]
        top[row_block(i)] = peak
        mass[row_block(i)] = weight
        total[row_block(i)] = read

    for i in range(span // ATTEND_ROWS):
        keys = (i + 1) * ATTEND_ROWS
        meet(i, k_t[0, :, :keys], v_t[0, :, :keys], True)

    @pl.loop(1, index[0] + 1)
    def _(r):
        for j in range(span // wide):
            keys_t = k_t[r, :, j * wide : (j + 1) * wide]
            values_t = v_t[r, :, j * wide : (j + 1) * wide]
            for i in range(span // ATTEND_ROWS):
                meet(i, keys_t, values_t, False)

    out[...] = total[...] / mass[...]
    lse[...] = top[...] + jnp.log(mass[...])


def whole_call(kernel, out_shape, scratch, index, *operands):
    def whole(array):
        return pl.BlockSpec(array.shape, lambda i: (0,) * len(array.shape))

    return pl.pallas_call(
        kernel,
        grid=(1,),
        out_shape=out_shape,
        in_specs=[pl.BlockSpec(memory_space=pltpu.SMEM), *map(whole, operands)],
        out_specs=jax.tree.map(whole, out_shape),
        scratch_shapes=scratch,
        cost_estimate=pl.CostEstimate(flops=0, bytes_accessed=0, transcendentals=0),
        compiler_params=pltpu.CompilerParams(vmem_limit_bytes=VMEM_LIMIT),
    )(index, *operands)


def attend(index, queries, parts):
    span, groups = queries.shape[0], lax.axis_size("group")
    shape = jax.ShapeDtypeStruct
    turned = shape((groups, HEAD_DIM, span), B16)
    column = pltpu.VMEM((span, 1), F32)
    return whole_call(
        attend_kernel,
        (shape((span, HEAD_DIM), F32), shape((span, 1), F32), turned, turned),
        [pltpu.VMEM((span, HEAD_DIM), F32), column, column],
        index,
        queries,
        *parts,
    )


def attend_back_kernel(index, q, q_t, d, d_t, k_t, v_t, lse, delta, grad_q, *refs):
    *outs, sum_k, sum_v = refs
    span = q.shape[0]
    keys = HEAD_DIM // len(outs)
    half = keys // 2
    wide = min(ATTEND_KEYS, span)
    blocks = span // ATTEND_ROWS

    def meet(i, keys_t, values_t, offset, total_q):
        part = row_block(i)
        scores = dot(q[part], keys_t) * HEAD_DIM**-0.5
        if offset is not None:
            rows = i * ATTEND_ROWS + lax.broadcasted_iota(jnp.int32, scores.shape, 0)
            cols = offset + lax.broadcasted_iota(jnp.int32, scores.shape, 1)
            scores = jnp.where(cols <= rows, scores, MASKED)
        probs = jnp.exp(scores - lse[part])
        grad_scores = (probs * (dot(d[part], values_t) - delta[part])).astype(B16)
        update = dot_nt(grad_scores, keys_t)
        grad_q[part] = update if total_q is None else grad_q[part] + update
        return dot(q_t[:, part], grad_scores), dot(d_t[:, part], probs.astype(B16))

    def store(r, cols, pair):
        sum_k[...] = (pair[0] * HEAD_DIM**-0.5).astype(B16)
        sum_v[...] = pair[1].astype(B16)
        for k, out in enumerate(outs):
            at = pl.multiple_of(index[k + 1] * half, half)
            own = r * 2 * keys if isinstance(r, int) else pl.multiple_of(r * 2 * keys, 2 * keys)
            out[pl.ds(own, half), cols] = sum_k[pl.ds(at, half)]
            out[pl.ds(own + half, half), cols] = sum_k[pl.ds(at + HEAD_DIM // 2, half)]
            at = pl.multiple_of(index[k + 1] * keys, keys)
            out[pl.ds(own + keys, keys), cols] = sum_v[pl.ds(at, keys)]

    for j in range(span // wide):
        cols = slice(j * wide, (j + 1) * wide)
        pair = None
        for i in range(j * wide // ATTEND_ROWS, blocks):
            more = meet(i, k_t[0, :, cols], v_t[0, :, cols], j * wide, None if j == 0 else True)
            pair = more if pair is None else (pair[0] + more[0], pair[1] + more[1])
        store(0, cols, pair)

    @pl.loop(1, index[0] + 1)
    def _(r):
        for j in range(span // wide):
            cols = slice(j * wide, (j + 1) * wide)
            pair = None
            for i in range(blocks):
                more = meet(i, k_t[r, :, cols], v_t[r, :, cols], None, True)
                pair = more if pair is None else (pair[0] + more[0], pair[1] + more[1])
            store(r, cols, pair)

    @pl.loop(index[0] + 1, k_t.shape[0])
    def _(r):
        for out in outs:
            own = pl.ds(pl.multiple_of(r * 2 * keys, 2 * keys), 2 * keys)
            out[own] = jnp.zeros((2 * keys, span), B16)


def attend_back(index, queries, keys_t, values_t, grad, lse, delta):
    span, groups = queries.shape[0], keys_t.shape[0]
    near = lax.axis_size("near")
    shape = jax.ShapeDtypeStruct
    part = shape((groups * 2 * HEAD_DIM // near, span), B16)
    wide = pltpu.VMEM((HEAD_DIM, min(ATTEND_KEYS, span)), B16)
    grad_q, *parts = whole_call(
        attend_back_kernel,
        (shape(queries.shape, F32), *[part] * near),
        [wide, wide],
        index,
        queries,
        queries.T,
        grad,
        grad.T,
        keys_t,
        values_t,
        lse,
        delta,
    )
    return grad_q, parts


def in_two(x):
    high = x.astype(B16)
    return high, (x - high.astype(F32)).astype(B16)


def dot_half(low, x, dims=((1,), (0,))):
    high, rest = in_two(x)
    return dot(low, high, dims) + dot(low, rest, dims)


def dot_fine(left, right, dims=((1,), (0,))):
    high, rest = in_two(left)
    other, more = in_two(right)
    return dot(high, other, dims) + (dot(high, more, dims) + dot(rest, other, dims))


def spread(per_head, of_head):
    return dot_exact(per_head, of_head, ((0,), (0,)))


def head_decay(cum, cum_t, h):
    length = cum.shape[0]
    rows = lax.broadcasted_iota(jnp.int32, (length, length), 0)
    cols = lax.broadcasted_iota(jnp.int32, (length, length), 1)
    gap = cum[:, h : h + 1] - cum_t[h : h + 1, :]
    return jnp.exp(jnp.where(cols <= rows, gap, MASKED))


def in_head(shape, h, channels):
    lane = lax.broadcasted_iota(jnp.int32, shape, 1)
    return (lane >= h * channels) & (lane < (h + 1) * channels)


def scan_kernel(heads, x, dt, cum, cum_t, b_t, c_t, of_head, y, ends, state):
    @pl.when(pl.program_id(0) == 0)
    def _():
        state[...] = jnp.zeros_like(state)

    channels = x.shape[1] // heads
    per = HEAD_DIM // channels
    owner = of_head[...]
    cums, cums_t = cum[...], cum_t[...]
    scaled = x[...] * spread(dt[...], owner)
    inner = dot_tn(c_t[...], b_t[...])
    wide = spread(cums_t, owner)
    end = wide[-1:]
    carried = dot_half(c_t[...], state[...], ((0,), (0,))) * jnp.exp(wide)
    for at in range(heads // per):
        lanes = slice(at * HEAD_DIM, (at + 1) * HEAD_DIM)
        block = scaled[:, lanes]
        within = None
        for k in range(per):
            mixing = head_decay(cums, cums_t, at * per + k) * inner
            part = dot_fine(mixing, block)
            mine = in_head(part.shape, k, channels)
            within = part if within is None else jnp.where(mine, part, within)
        y[:, lanes] = within + carried[:, lanes]
    state[...] = jnp.exp(end) * state[...] + dot_half(b_t[...], scaled * jnp.exp(end - wide))
    ends[0] = state[...]


class ChunkSpecs:
    def __init__(self, rows, chunks, turned):
        self.rows, self.chunks = rows, chunks
        self.chunk = (lambda c: chunks - 1 - c) if turned else (lambda c: c)

    def by_row(self, width):
        return pl.BlockSpec((self.rows, width), lambda c: (self.chunk(c), 0))

    def by_col(self, height):
        return pl.BlockSpec((height, self.rows), lambda c: (0, self.chunk(c)))

    def stacked(self, array, more=0):
        shape = (1, *array.shape[1:])
        return pl.BlockSpec(shape, lambda c: (jnp.maximum(self.chunk(c) + more, 0), 0, 0))

    def whole(self, array):
        return pl.BlockSpec(array.shape, lambda c: (0,) * len(array.shape))


def chunk_call(kernel, chunks, in_specs, out_specs, out_shape, scratch, *operands):
    return pl.pallas_call(
        kernel,
        grid=(chunks,),
        in_specs=in_specs,
        out_specs=out_specs,
        out_shape=out_shape,
        scratch_shapes=scratch,
        cost_estimate=pl.CostEstimate(flops=0, bytes_accessed=0, transcendentals=0),
        compiler_params=pltpu.CompilerParams(vmem_limit_bytes=VMEM_LIMIT),
    )(*operands)


def scan_forward(heads, x, dt, cum, cum_t, b_t, c_t, of_head, rows):
    span, inner = x.shape
    chunks, padded = span // rows, dt.shape[0]
    at = ChunkSpecs(rows, chunks, False)
    ends = jax.ShapeDtypeStruct((chunks, STATE, inner), F32)
    return chunk_call(
        functools.partial(scan_kernel, heads),
        chunks,
        [
            at.by_row(inner),
            at.by_col(padded),
            at.by_row(padded),
            at.by_col(padded),
            at.by_col(STATE),
            at.by_col(STATE),
            at.whole(of_head),
        ],
        [at.by_row(inner), at.stacked(ends)],
        [jax.ShapeDtypeStruct((span, inner), F32), ends],
        [pltpu.VMEM((STATE, inner), F32)],
        x,
        dt,
        cum,
        cum_t,
        b_t,
        c_t,
        of_head,
    )


def within_kernel(heads, x, dt, cum, cum_t, b_t, c_t, of_head, ends, through, entering, grad, *outs):
    within, grad_bt, grad_ct = outs
    channels = x.shape[1] // heads
    per = HEAD_DIM // channels
    owner = of_head[...]
    cums, cums_t = cum[...], cum_t[...]
    scaled = x[...] * spread(dt[...], owner)
    inner = dot_tn(c_t[...], b_t[...])
    back = grad[...]
    faded = back * jnp.exp(spread(cums_t, owner))
    grad_inner = jnp.zeros_like(inner)
    for at in range(heads // per):
        lanes = slice(at * HEAD_DIM, (at + 1) * HEAD_DIM)
        total = None
        for k in range(per):
            decay = head_decay(cums, cums_t, at * per + k)
            part = dot_fine(decay * inner, back[:, lanes], ((0,), (0,)))
            mine = in_head(part.shape, k, channels)
            total = part if total is None else jnp.where(mine, part, total)
            only = jnp.where(mine, back[:, lanes], 0.0)
            grad_inner += dot_fine(only, scaled[:, lanes], ((1,), (1,))) * decay
        within[:, lanes] = total
    state_in = through[0] * entering[...]
    state_in = state_in + jnp.where(pl.program_id(0) == 0, 0.0, ends[0])
    grad_ct[...] = (
        dot_half(b_t[...], grad_inner, ((1,), (1,))) + dot_fine(state_in, faded, ((1,), (1,)))
    ).astype(B16)
    grad_bt[...] = dot_half(c_t[...], grad_inner)


def scan_within(heads, x, dt, cum, cum_t, b_t, c_t, of_head, ends, through, entering, grad, rows):
    span, inner = x.shape
    chunks, padded = span // rows, dt.shape[0]
    at = ChunkSpecs(rows, chunks, False)
    shape = jax.ShapeDtypeStruct
    return chunk_call(
        functools.partial(within_kernel, heads),
        chunks,
        [
            at.by_row(inner),
            at.by_col(padded),
            at.by_row(padded),
            at.by_col(padded),
            at.by_col(STATE),
            at.by_col(STATE),
            at.whole(of_head),
            at.stacked(ends, -1),
            at.stacked(through),
            at.whole(entering),
            at.by_row(inner),
        ],
        [at.by_row(inner), at.by_col(STATE), at.by_col(STATE)],
        [shape((span, inner), F32), shape((STATE, span), F32), shape((STATE, span), B16)],
        [],
        x,
        dt,
        cum,
        cum_t,
        b_t,
        c_t,
        of_head,
        ends,
        through,
        entering,
        grad,
    )


def across_kernel(
    x,
    x_pre,
    dt,
    cum_t,
    b_t,
    c_t,
    of_head,
    skip,
    ends,
    through,
    entering,
    y,
    grad,
    within,
    bt_part,
    leaving,
    grad_xpre,
    grad_bt,
    grad_logs,
    grad_dt,
    grad_skip,
    grad_state,
):
    @pl.when(pl.program_id(0) == 0)
    def _():
        grad_state[...] = leaving[...]
        grad_skip[...] = jnp.zeros_like(grad_skip)

    owner = of_head[...]
    low_owner = owner.astype(B16)
    times = spread(dt[...], owner)
    values = x[...]
    scaled = values * times
    wide = spread(cum_t[...], owner)
    end = wide[-1:]
    tail = jnp.exp(end - wide)
    back = grad[...]
    to_state = grad_state[...]
    grad_scaled = within[...] + tail * dot_half(b_t[...], to_state, ((0,), (0,)))
    grad_bt[...] = (bt_part[...] + dot_fine(to_state, scaled * tail, ((1,), (1,)))).astype(B16)
    grad_xpre[...] = (grad_scaled * times + skip[...] * back) * silu_slope(x_pre[...])
    grad_skip[...] += jnp.sum(back * values, 0, keepdims=True)
    state_out = ends[0] + through[0] * entering[...]
    at_end = jnp.sum(state_out * to_state, 0, keepdims=True)
    change = back * y[...] - grad_scaled * scaled
    rows = lax.broadcasted_iota(jnp.int32, change.shape, 0)
    change = change + jnp.where(rows == change.shape[0] - 1, at_end, 0.0)
    per_head = dot_half(low_owner, change, ((1,), (1,)))
    length = change.shape[0]
    later = lax.broadcasted_iota(jnp.int32, (length, length), 0) >= lax.broadcasted_iota(
        jnp.int32, (length, length), 1
    )
    grad_logs[...] = dot_exact(per_head, later.astype(F32))
    grad_dt[...] = dot_half(low_owner, grad_scaled * values, ((1,), (1,)))
    faded = back * jnp.exp(wide)
    grad_state[...] = jnp.exp(end) * to_state + dot_half(c_t[...], faded)


def scan_across(
    x,
    x_pre,
    dt,
    cum_t,
    b_t,
    c_t,
    of_head,
    skip,
    ends,
    through,
    entering,
    y,
    grad,
    within,
    bt_part,
    leaving,
    rows,
):
    span, inner = x.shape
    chunks, padded = span // rows, dt.shape[0]
    at = ChunkSpecs(rows, chunks, True)
    shape = jax.ShapeDtypeStruct
    return chunk_call(
        across_kernel,
        chunks,
        [
            at.by_row(inner),
            at.by_row(inner),
            at.by_col(padded),
            at.by_col(padded),
            at.by_col(STATE),
            at.by_col(STATE),
            at.whole(of_head),
            at.whole(skip),
            at.stacked(ends),
            at.stacked(through, 1),
            at.whole(entering),
            at.by_row(inner),
            at.by_row(inner),
            at.by_row(inner),
            at.by_col(STATE),
            at.whole(leaving),
        ],
        [
            at.by_row(inner),
            at.by_col(STATE),
            at.by_col(padded),
            at.by_col(padded),
            at.whole(skip),
        ],
        [
            shape((span, inner), F32),
            shape((STATE, span), B16),
            shape((padded, span), F32),
            shape((padded, span), F32),
            shape(skip.shape, F32),
        ],
        [pltpu.VMEM((STATE, inner), F32)],
        x,
        x_pre,
        dt,
        cum_t,
        b_t,
        c_t,
        of_head,
        skip,
        ends,
        through,
        entering,
        y,
        grad,
        within,
        bt_part,
        leaving,
    )


def flat(x):
    return with_layout_constraint(x, Layout(tuple(range(x.ndim))))


def cotangent_half(cotangent):
    return own_half(cotangent).astype(F32)


def home_kernel(runs, index, *refs):
    blocks, outs = refs[: -len(runs)], refs[-len(runs) :]
    for k, block in enumerate(blocks):
        at = 0
        for out, (width, across) in zip(outs, runs):
            piece = block[:, at : at + width].astype(F32)
            at += width
            place = pl.ds(pl.multiple_of(index[k] * width, width), width)
            if across:
                out[:, place] = piece
            else:
                out[place] = piece.T


def homed(blocks, *runs):
    count, piece = len(blocks), blocks[0].shape[0]
    shapes = [(piece, count * w) if across else (count * w, piece) for w, across in runs]
    shapes = [jax.ShapeDtypeStruct(shape, F32) for shape in shapes]
    index = jnp.stack(near_places()).astype(jnp.int32)
    return whole_call(functools.partial(home_kernel, runs), shapes, [], index, *blocks)


def per_device(
    tokens,
    cotangent,
    g1,
    w_q,
    w_k,
    w_v,
    w_o,
    w_z,
    w_x,
    w_bc,
    w_dt,
    conv_bc,
    conv_bc_bias,
    w_out,
    g2,
    w_gate,
    w_up,
    w_down,
    conv_x,
    conv_x_bias,
    dt_bias,
    a_log,
    d_skip,
):
    near, groups = lax.axis_size("near"), lax.axis_size("group")
    here, group, core = (lax.axis_index(a) for a in ("near", "group", "head"))
    rows, width = tokens.shape
    span = near * rows
    piece = w_q.shape[0]
    devices = near * groups
    key_cols = HEAD_DIM // near
    half_cols = key_cols // 2
    heads = w_dt.shape[1] // near
    padded = heads + -heads % 8
    inner, q_cols, ff = w_z.shape[1] // near, w_q.shape[1] // near, w_gate.shape[1] // near
    o_rows = w_o.shape[0] // near
    at_q = 2 * inner // q_cols

    def columns(w):
        return w.reshape(w.shape[0], near, -1).transpose(1, 0, 2)

    def share(x, dim):
        size = x.shape[dim] // near
        return lax.dynamic_slice_in_dim(x, here * size, size, dim)

    def by_head(x):
        return jnp.pad(share(x, 0).astype(F32), (0, padded - heads))[:, None]

    k_cols = w_k.reshape(piece, 2, near, half_cols).transpose(2, 0, 1, 3)
    w_bc_mine = lax.dynamic_slice_in_dim(w_bc, core * STATE, STATE, 1)
    pack1 = [columns(w_x), k_cols.reshape(near, piece, key_cols), columns(w_v)]
    pack1 = jnp.concatenate([*pack1, columns(w_bc_mine)], 2)
    extra = jnp.concatenate([g1, g2, conv_bc.reshape(-1), conv_bc_bias])
    n_small, n_dt = extra.shape[0], heads * piece
    extra = jnp.broadcast_to(extra, (near, n_small))
    extra = jnp.concatenate([extra, w_dt.T.reshape(near, n_dt)], 1)
    extra = jnp.pad(extra, ((0, 0), (0, -extra.shape[1] % (8 * pack1.shape[2]))))
    pack1 = jnp.concatenate([pack1, extra.reshape(near, -1, pack1.shape[2])], 1)
    halo = step_group(tokens[rows - 16 :], 1)
    pack1 = after(pack1, halo)
    full1 = jnp.broadcast_to(pack1, (groups, *pack1.shape)).reshape(devices, *pack1.shape[1:])
    full1 = trade_all(full1)
    token_parts = sent_tokens(jnp.concatenate([own_half(tokens), halo], 0))
    pack2 = [columns(w_z), columns(w_out.T), columns(w_q), columns(w_o.T)]
    pack2 = jnp.concatenate(pack2, 2)
    pack3 = jnp.concatenate([columns(w_gate), columns(w_up), columns(w_down.T)], 2)
    pack2, *token_parts[:near] = lax.optimization_barrier((pack2, *token_parts[:near]))
    sent2 = sent_near(pack2)
    positions = (group * span + jnp.arange(span)).astype(F32)
    half = HEAD_DIM // 2
    freqs = ROPE_BASE ** (-jnp.arange(half, dtype=F32) / half)
    angle = positions[:, None] * freqs[None, :]
    cos_q, sin_q = jnp.cos(angle), jnp.sin(angle)
    cos_k, sin_k = (share(x, 1).T for x in (cos_q, sin_q))
    of_head = jnp.arange(inner)[None, :] // (inner // heads) == jnp.arange(padded)[:, None]
    of_head = of_head.astype(F32)
    decay_rate, head_bias = jnp.exp(by_head(a_log)), by_head(dt_bias)
    skip = spread(by_head(d_skip), of_head)
    triangle = jnp.triu(jnp.ones((rows, rows), F32))
    taps_x = share(conv_x, 1).astype(F32)[:, None, :]
    bias_x = share(conv_x_bias, 0).astype(F32)[None, :]
    my_tokens = own_half(tokens).astype(F32)
    early = (cos_q, sin_q, cos_k, sin_k, of_head, decay_rate, head_bias, skip, triangle)
    early = (*early, taps_x, bias_x, my_tokens, pack3)
    full1, early = lax.optimization_barrier((full1, early))
    cos_q, sin_q, cos_k, sin_k, of_head, decay_rate, head_bias, skip, triangle = early[:9]
    taps_x, bias_x, my_tokens, pack3 = early[9:]

    extra = full1[:, piece:].reshape(devices, -1)
    smalls = extra[:, :n_small].astype(F32)
    gain1 = smalls[:, :piece].reshape(-1)
    gain2 = smalls[:, piece : 2 * piece].reshape(-1)
    full_dt = extra[:, n_small : n_small + n_dt].reshape(devices, heads, piece)
    full_dt = full_dt.transpose(1, 0, 2).reshape(heads, width)
    full_dt = jnp.pad(full_dt, ((0, padded - heads), (0, 0)))
    taps_bc = smalls[:, 2 * piece : -conv_bc_bias.shape[0]].reshape(devices, CONV, -1)
    taps_bc = taps_bc.transpose(1, 0, 2).reshape(CONV, 2, near, -1)
    taps_bc = taps_bc[:, core, here][:, :, None]
    bias_bc = smalls[:, -conv_bc_bias.shape[0] :].reshape(2, near, -1)[core, here][:, None]
    full1 = full1[:, :piece].reshape(width, -1)
    full_x, full_kvbc = full1[:, :inner], full1[:, inner:]
    n1, halo = normed_tokens(token_parts, gain1, 16)
    edge = dot(halo, full1)[17 - CONV :]
    x_edge, bc_edge = edge[:, :inner], edge[:, inner + 2 * key_cols :].T
    grad_parts = sent_tokens(after(own_half(cotangent), n1))

    kvbc = dot(full_kvbc, n1, ((0,), (1,)))
    k_first, k_second = rotate_pair(kvbc[:half_cols], kvbc[half_cols:key_cols], cos_k, sin_k)
    kv = jnp.concatenate([k_first, k_second, kvbc[key_cols : 2 * key_cols]], 0).astype(B16)
    kv = flat(kv)
    kv_parts = [kv] + [step_group(kv, r) for r in range(1, groups)]
    bc_proj = flat(kvbc[2 * key_cols :])
    sent2, n1, kv = lax.optimization_barrier((sent2, n1, kv))
    full2 = placed(near_places(), sent2).reshape(near * piece, -1)
    n1_x, full2 = lax.optimization_barrier((n1, full2))
    full2 = lax.all_gather(full2, "group", axis=0, tiled=True)

    x_proj = dot(n1_x, full_x)
    sent3 = sent_near(after(pack3, x_proj))

    bc_pre = conv(bc_proj, bc_edge, taps_bc, bias_bc, 1)
    bc_mine = gather_near(flat(jax.nn.silu(bc_pre).astype(B16))).reshape(STATE, span)
    bc_other = swap_cores(bc_mine)
    first = core == 0
    b_t, c_t = jnp.where(first, bc_mine, bc_other), jnp.where(first, bc_other, bc_mine)

    dt_pre = dot_nt(full_dt, n1) + head_bias
    dt = jax.nn.softplus(dt_pre)
    logs = -dt * decay_rate
    cum_t = dot_exact(logs.reshape(padded * near, rows), triangle).reshape(padded, near, rows)
    chunk_total = cum_t[:, :, -1]
    before = jnp.cumsum(chunk_total, 1) - chunk_total
    group_total = jnp.sum(chunk_total, 1, keepdims=True)
    fade = jnp.exp(spread((cum_t + before[:, :, None]).reshape(padded, span), of_head))
    cum_t = cum_t.reshape(padded, span)
    cum = cum_t.T
    group_decay = jnp.exp(spread(group_total, of_head))

    x_pre = conv(x_proj, x_edge, taps_x, bias_x, 0)
    xc = jax.nn.silu(x_pre)
    kv_parts = jnp.concatenate(kv_parts, 0)
    xc = after(xc, kv_parts, *grad_parts)
    sent3, xc = lax.optimization_barrier((sent3, xc))
    full3 = placed(near_places(), sent3).reshape(near * piece, -1)
    xc, full3 = lax.optimization_barrier((xc, full3))
    full3 = lax.all_gather(full3, "group", axis=0, tiled=True)
    kv_parts = [to_near(kv_parts, k) if k else kv_parts for k in range(near)]
    outputs, ends = scan_forward(heads, xc, dt, cum, cum_t, b_t, c_t, of_head, rows)
    through = jnp.concatenate([jnp.zeros_like(group_total), jnp.cumsum(chunk_total, 1)], 1)
    through = jnp.exp(spread(through, of_head))[:, None]

    def state_rows(state):
        pad = jnp.broadcast_to(group_decay, (16, inner))
        return jnp.concatenate([state, pad], 0).astype(B16)

    def sent_states(state, direction):
        return [step_group(state, direction * r) for r in range(1, groups)]

    def chained(parts):
        total = jnp.zeros((STATE, inner), F32)
        for part in reversed(parts):
            part = part.astype(F32)
            total = part[STATE : STATE + 1] * total + part[:STATE]
        return total

    entering = sent_states(state_rows(ends[-1]), 1)
    full_z, full_out_t = full2[:, :inner], full2[:, inner : 2 * inner]
    full_q, full_o_t = full2[:, 2 * inner : 2 * inner + q_cols], full2[:, 2 * inner + q_cols :]
    full_gu, full_down_t = full3[:, : 2 * ff], full3[:, 2 * ff :]
    q_proj = dot(n1, full_q)
    queries = jnp.concatenate(rotate_pair(q_proj[:, :half], q_proj[:, half:], cos_q, sin_q), 1)
    queries = queries.astype(B16)
    z_proj = dot(n1, full_z)
    index = jnp.stack([group, *near_places()]).astype(jnp.int32)
    attended32, lse, keys_t, values_t = attend(index, queries, kv_parts)
    attended = attended32.astype(B16)
    entering = chained(after(entering, attended, z_proj))

    outputs = outputs + fade * dot_tn(c_t, entering.astype(B16))
    y = outputs + skip * xc
    gated = (y * jax.nn.silu(z_proj)).astype(B16)

    pairs = [(gated, (full2, 1)), (attended, (full2, at_q + 1))]
    blocks = partial_tokens(width, pairs)
    all_cotangent = placed_tokens(after(grad_parts, blocks))
    mixed, all_cotangent = scatter_tokens(blocks, alongside=all_cotangent)
    hidden = my_tokens + mixed
    normed2, unit2, factor2 = normalize(hidden, gain2)
    n2 = gather_tokens(normed2.astype(B16))
    both = dot(n2, full_gu)
    gate, up = both[:, :ff], both[:, ff:]
    sigma = jax.nn.sigmoid(gate)
    act = (gate * sigma * up).astype(B16)
    grad_act = dot(all_cotangent, full_down_t)
    grad_gate = grad_act * up * sigma * (1.0 + gate * (1.0 - sigma))
    grad_gu = jnp.concatenate([grad_gate, grad_act * gate * sigma], 1).astype(B16)

    def sum_groups(grad):
        own = lax.psum_scatter(grad, "group", scatter_dimension=0, tiled=True)
        return own.reshape(near, piece, -1)

    partial2 = partial_tokens(width, [(grad_gu, (full3, 0))])
    grads3 = dot_tn(n2, grad_gu).astype(B16)
    grad_n2, (grads3, feed) = scatter_tokens(
        partial2, alongside=(grads3, summed_dots(width, (act, (full3, 2))))
    )
    home3 = sum_groups(grads3)

    grad_norm2, grad_g2 = norm_back(grad_n2, unit2, factor2, gain2)
    grad_hidden = cotangent_half(cotangent) + grad_norm2
    grad_mixed = gather_tokens(grad_hidden.astype(B16))

    grad_gated = dot(grad_mixed, full_out_t).astype(B16).astype(F32)
    sig_z = jax.nn.sigmoid(z_proj)
    grad_y = grad_gated * z_proj * sig_z
    grad_z = (grad_gated * y * sig_z * (1.0 + z_proj * (1.0 - sig_z))).astype(B16)
    read = state_rows(dot(c_t, (grad_y * fade).astype(B16)))
    read_parts = sent_states(read, -1)

    grad_mixed = after(grad_mixed, read)
    grad_attended = dot(grad_mixed, full_o_t).astype(B16)
    delta = jnp.sum(grad_attended.astype(F32) * attended32, 1, keepdims=True)
    grad_q, kv_parts = attend_back(
        index, queries, keys_t, values_t, grad_attended, lse, delta
    )
    kv_parts = [to_near(p, k) if k else p for k, p in enumerate(kv_parts)]
    grad_q = grad_q * HEAD_DIM**-0.5
    grad_q = jnp.concatenate(rotate_pair(grad_q[:, :half], grad_q[:, half:], cos_q, -sin_q), 1)
    grad_zq = jnp.concatenate([grad_z, grad_q.astype(B16)], 1)
    mixer_out = jnp.concatenate([gated, attended], 1)
    read_parts, grad_zq = lax.optimization_barrier((read_parts, grad_zq))
    grads2 = joined_grads((all_cotangent, act), (grad_mixed, mixer_out), (n1, grad_zq))
    home2 = sum_groups(grads2)

    kv_parts, grads2 = lax.optimization_barrier((kv_parts, grads2))
    kv_parts = flat(added(kv_parts))
    kv_sent = kv_parts.astype(B16)
    kv_rows = 2 * key_cols
    grad_kv = [kv_parts[:kv_rows]]
    for r in range(1, groups):
        grad_kv.append(step_group(kv_sent[r * kv_rows : (r + 1) * kv_rows], -r))
    feed = met_tokens(*after(feed, kv_sent))

    feed, grad_y_scan = lax.optimization_barrier((feed, grad_y))
    within, bt_part, grad_ct = scan_within(
        heads, xc, dt, cum, cum_t, b_t, c_t, of_head, ends, through, entering, grad_y_scan, rows
    )
    feed = [to_near(b, k) if k else b for k, b in enumerate(feed)]
    home3 = sent_near(after(home3, kv_sent))
    read_parts, within, home3, feed = lax.optimization_barrier((read_parts, within, home3, feed))
    leaving = chained(read_parts)
    grad_xpre, grad_bt, grad_logs, grad_dt, grad_skip = scan_across(
        xc,
        x_pre,
        dt,
        cum_t,
        b_t,
        c_t,
        of_head,
        skip,
        ends,
        through,
        entering,
        outputs,
        grad_y,
        within,
        bt_part,
        leaving,
        rows,
    )
    kept = jnp.where(first, grad_bt, grad_ct)
    given = swap_cores(jnp.where(first, grad_ct, grad_bt))
    kept = (kept.astype(F32) + given.astype(F32)).astype(B16)
    grad_bc = flat(added(sent_near(kept.reshape(near, -1, span))))

    grad_bcpre = grad_bc * silu_slope(bc_pre)
    next_x = step_group(grad_xpre[: CONV - 1], -1)
    next_bc = step_group(grad_bcpre[:, : CONV - 1], -1)
    grad_x = conv_back(grad_xpre, next_x, taps_x, 0)
    grad_bcp = conv_back(grad_bcpre, next_bc, taps_bc, 1)
    grad_kv = added(after(grad_kv, grad_xpre))
    gk_first, gk_second = rotate_pair(
        grad_kv[:half_cols], grad_kv[half_cols:key_cols], cos_k, -sin_k
    )
    grad_kvbc = jnp.concatenate([gk_first, gk_second, grad_kv[key_cols:], grad_bcp], 0)
    grad_first = jnp.concatenate([grad_x.astype(B16), flat(grad_kvbc.astype(B16)).T], 1)

    grad_dt = grad_dt - grad_logs * decay_rate
    grad_dt_pre = grad_dt * jax.nn.sigmoid(dt_pre)
    grad_dt_low = grad_dt_pre.astype(B16)
    grad_skip = dot_exact(of_head, grad_skip, ((1,), (1,)))[:heads, 0]
    grad_alog = jnp.sum(grad_logs * logs, 1)[:heads]
    grad_dtbias = jnp.sum(grad_dt_pre, 1)[:heads]

    grads1 = dot_tn(n1, grad_first).astype(B16)
    grad_first, grads1 = lax.optimization_barrier((grad_first, grads1))
    grad_wdt = dot(grad_dt_low, n1).reshape(padded, devices, piece).transpose(1, 0, 2)
    pairs = [
        (grad_zq[:, :inner], (full2, 0)),
        (grad_zq[:, inner:], (full2, at_q)),
        (grad_first, (full1, 0)),
        (grad_dt_low.T, full_dt),
    ]
    partial1 = partial_tokens(width, pairs)
    grad_xpre, grad_bcpre = after((grad_xpre, grad_bcpre), partial1)
    grad_tapx, grad_biasx = taps_back(grad_xpre, x_proj, x_edge, 0)
    grad_tapbc, grad_biasbc = taps_back(grad_bcpre, bc_proj, bc_edge, 1)
    output = (hidden + added(after(feed, partial1))).astype(B16)
    output = both_halves(output, swap_cores(output), 0)
    outs3 = homed(after(home3, partial1), (ff, True), (ff, True))
    taps = grad_tapx, grad_biasx, grad_tapbc, grad_biasbc
    grad_n1, (sum_wgate, sum_wup, output, taps) = scatter_tokens(
        partial1, alongside=(*outs3, output, taps)
    )
    grad_tapx, grad_biasx, grad_tapbc, grad_biasbc = taps
    _, unit1, factor1 = normalize(my_tokens, gain1)
    grad_norm1, grad_g1 = norm_back(grad_n1, unit1, factor1, gain1)
    grad_tokens = grad_hidden + grad_norm1

    grad_tokens = both_halves(grad_tokens, swap_cores(grad_tokens), 0)

    crossing = jnp.concatenate([grad_g1, grad_g2, grad_tapbc.reshape(-1), grad_biasbc])
    other = swap_cores(crossing)
    gains = 2 * width
    mine = [grad_tapx.reshape(-1), grad_biasx, grad_dtbias, grad_alog, grad_skip]
    mine = [*mine, both_halves(crossing[gains:], other[gains:], 0)]
    ends, at = [], 0
    for g in mine[:-1]:
        at += g.shape[0]
        ends.append(at)
    packed = jnp.concatenate(mine)
    size = packed.shape[0]
    packed = jnp.broadcast_to(packed, (devices, size))
    own_parts = [crossing[:width] + other[:width], crossing[width:gains] + other[width:gains]]
    own_parts = [grad_wdt.reshape(devices, -1), *(p.reshape(devices, -1) for p in own_parts)]
    packed = jnp.concatenate([*own_parts, packed], 1)
    packed = jnp.pad(packed, ((0, 0), (0, -packed.shape[1] % (8 * HEAD_DIM))))
    packed = trade_all(packed.reshape(devices, -1, HEAD_DIM))
    home1 = grads1.reshape(groups, near * piece, -1)
    home1 = [lax.dynamic_index_in_dim(home1, (group + r) % groups, 0, False) for r in range(groups)]
    home1 = [around(b, r) if r else b for r, b in enumerate(home1)]
    home2 = sent_near(after(home2, grad_n1))
    home1, home2 = lax.optimization_barrier((home1, home2))
    home1 = sent_near(added(home1).astype(B16).reshape(near, piece, -1))
    packed, home1 = lax.optimization_barrier((packed, home1))
    packed = packed.reshape(devices, -1)
    n_dt = padded * piece
    sum_wdt = jnp.sum(packed[:, :n_dt].reshape(groups, near, padded, piece), 0)
    sum_wdt = sum_wdt[:, :heads].reshape(-1, piece).T
    own_sums = jnp.sum(packed[:, n_dt : n_dt + 2 * piece], 0)
    packed = packed[:, n_dt + 2 * piece :][:, :size]

    sum_wdown, sum_wout, sum_wo, sum_wz, sum_wq = homed(
        home2, (ff, False), (inner, False), (o_rows, False), (inner, True), (q_cols, True)
    )
    (sum_wx,) = homed(home1, (inner, True))
    home_small = placed(near_places(), [b[:, inner:] for b in home1]).astype(F32)
    home_k, home_v, home_bc = jnp.split(home_small, [key_cols, 2 * key_cols], 2)
    sum_wv = home_v.transpose(1, 0, 2).reshape(piece, -1)
    sum_wk = home_k.reshape(near, piece, 2, half_cols).transpose(1, 2, 0, 3)
    sum_wk = sum_wk.reshape(piece, -1)
    bc_mine = home_bc.transpose(1, 0, 2).reshape(piece, -1)
    sum_wbc = both_halves(bc_mine, swap_cores(bc_mine), 1)

    every = jnp.split(packed, ends, 1)
    place = group * near + here

    def by_near(x):
        return jnp.sum(x.reshape(groups, near, -1), 0)

    sum_g1, sum_g2 = own_sums[:piece], own_sums[piece:]
    sum_convx = by_near(every[0]).reshape(near, CONV, -1).transpose(1, 0, 2).reshape(CONV, -1)
    sum_convxb, sum_dtbias, sum_alog, sum_dskip = (by_near(x).reshape(-1) for x in every[1:5])
    sum_bc = by_near(every[5]).reshape(near, 2, CONV + 1, -1).transpose(2, 1, 0, 3)
    sum_bc = sum_bc.reshape(CONV + 1, -1)
    bc_cols = conv_bc.shape[1]
    sum_bc = lax.dynamic_slice_in_dim(sum_bc, place * bc_cols, bc_cols, 1)
    return (
        output,
        grad_tokens,
        sum_g1,
        sum_wq,
        sum_wk,
        sum_wv,
        sum_wo,
        sum_wz,
        sum_wx,
        sum_wbc,
        sum_wdt,
        sum_bc[:CONV],
        sum_bc[CONV],
        sum_wout,
        sum_g2,
        sum_wgate,
        sum_wup,
        sum_wdown,
        sum_convx,
        sum_convxb,
        sum_dtbias,
        sum_alog,
        sum_dskip,
    )


def solution(mesh):
    seq, cores = mesh.shape["seq"], mesh.shape["head"]
    near = math.gcd(seq, 4)
    split = Mesh(mesh.devices.reshape(seq // near, near, cores), ("group", "near", "head"))
    seq = ("group", "near")
    row_split = P(seq, "head")
    col_split = P("head", seq)
    weights = (
        P(seq),
        row_split,
        row_split,
        row_split,
        col_split,
        row_split,
        row_split,
        P(seq, None),
        row_split,
        P(None, seq),
        P(seq),
        col_split,
        P(seq),
        row_split,
        row_split,
        col_split,
        P(None, "head"),
        P("head"),
        P("head"),
        P("head"),
        P("head"),
    )
    tokens = P(seq, None)
    return jax.shard_map(
        per_device,
        mesh=split,
        in_specs=(tokens, tokens, *weights),
        out_specs=(tokens, tokens, *weights),
        check_vma=False,
    )
```

```python
import functools
import math

import jax
import jax.numpy as jnp
from jax import lax
from jax.experimental import pallas as pl
from jax.experimental.layout import Layout, with_layout_constraint
from jax.experimental.pallas import tpu as pltpu
from jax.sharding import Mesh, PartitionSpec as P

HEAD_DIM = 128
STATE = 256
CONV = 4
EPS = 1e-05
ROPE_BASE = 100000000000.0
MASKED = -1e30
HIGHEST = lax.Precision.HIGHEST
F32 = jnp.float32
B16 = jnp.bfloat16
ATTEND_ROWS = 256
ATTEND_KEYS = 1024
VMEM_LIMIT = 40 << 20


def after(x, *earlier):
    return lax.optimization_barrier((x, earlier))[0]


def swap_cores(x):
    return lax.ppermute(x, "head", [(0, 1), (1, 0)])


def to_near(x, k):
    return lax.ppermute(x, "near", [(i, i ^ k) for i in range(lax.axis_size("near"))])


def around(x, distance):
    count = lax.axis_size("group")
    return lax.ppermute(x, "group", [(i, (i + distance) % count) for i in range(count)])


def step_group(x, distance):
    count = lax.axis_size("group")
    route = [(i, i + distance) for i in range(count) if 0 <= i + distance < count]
    return lax.ppermute(x, "group", route)


def place_kernel(count, index, *refs):
    for k, block in enumerate(refs[:count]):
        at = 0
        for out in refs[count:]:
            cols = slice(at, at + out.shape[-1])
            out[index[k]] = block[..., cols]
            at = cols.stop


def placed(index, blocks, widths=None):
    block = blocks[0]
    shapes = [
        jax.ShapeDtypeStruct((len(blocks), *block.shape[:-1], w), block.dtype)
        for w in widths or block.shape[-1:]
    ]
    kernel = functools.partial(place_kernel, len(blocks))
    out = whole_call(kernel, shapes, [], jnp.stack(index).astype(jnp.int32), *blocks)
    return out if widths else out[0]


def near_places():
    here = lax.axis_index("near")
    return [here ^ k for k in range(lax.axis_size("near"))]


def sent_near(x):
    blocks = [lax.dynamic_index_in_dim(x, at, 0, False) for at in near_places()]
    return [to_near(b, k) if k else b for k, b in enumerate(blocks)]


def trade_near(x):
    return placed(near_places(), sent_near(x))


def added(blocks):
    total = blocks[0].astype(F32)
    for block in blocks[1:]:
        total = total + block.astype(F32)
    return total


def gather_near(x):
    places = near_places()
    return placed(places, [x] + [to_near(x, k) for k in range(1, len(places))])


def trade_all(x):
    return lax.all_to_all(x, ("group", "near"), 0, 0, tiled=True)


def both_halves(mine, other, dim):
    first = lax.axis_index("head") == 0
    return jnp.concatenate([jnp.where(first, mine, other), jnp.where(first, other, mine)], dim)


def own_half(x):
    half = x.shape[0] // 2
    return lax.dynamic_slice_in_dim(x, lax.axis_index("head") * half, half, 0)


def normalized(value, gain):
    value = value.astype(F32)
    power = jnp.mean(value * value, 1, keepdims=True)
    return (value * lax.rsqrt(power + EPS) * gain).astype(B16)


def tokens_kernel(index, *refs):
    *refs, out = refs
    count = len(refs) // 2
    for k in range(count):
        for side in range(2):
            out[index[k], index[count + side]] = refs[k + side * count][...]


def normed_kernel(index, *refs):
    *refs, gain, out, halo = refs
    count, rows = len(refs) // 2, out.shape[2]
    for k in range(count):
        for side in range(2):
            value = refs[k + side * count][:rows]
            out[index[k], index[count + side]] = normalized(value, gain[...])

        @pl.when(index[k] == count - 1)
        def _():
            halo[...] = normalized(refs[k][rows:], gain[...])


def sent_tokens(mine):
    got = [mine] + [to_near(mine, k) for k in range(1, lax.axis_size("near"))]
    return [*got, *map(swap_cores, got)]


def tokens_index():
    core = lax.axis_index("head")
    return jnp.stack([*near_places(), core, 1 - core]).astype(jnp.int32)


def placed_tokens(parts):
    rows, width = parts[0].shape
    shape = jax.ShapeDtypeStruct((len(parts) // 2, 2, rows, width), parts[0].dtype)
    return whole_call(tokens_kernel, shape, [], tokens_index(), *parts).reshape(-1, width)


def normed_tokens(parts, gain, more):
    rows, width = parts[0].shape[0] - more, parts[0].shape[1]
    shapes = [
        jax.ShapeDtypeStruct((len(parts) // 2, 2, rows, width), B16),
        jax.ShapeDtypeStruct((more, width), B16),
    ]
    out, halo = whole_call(normed_kernel, shapes, [], tokens_index(), *parts, gain[None, :])
    return out.reshape(-1, width), halo


def gather_tokens(mine):
    return placed_tokens(sent_tokens(mine))


def dots_kernel(turned, core, *refs):
    *refs, give, keep = refs
    pairs = len(turned)
    for out, side in (give, 1 - core[0]), (keep, core[0]):
        lefts = []
        for left in refs[:pairs]:
            blocks = [left[j, side] for j in range(left.shape[0])]
            lefts.append(jnp.concatenate(blocks, 0))
        width = out.shape[1]
        tile = min(width, 512)
        for n in range(width // tile):
            cols = slice(n * tile, (n + 1) * tile)
            total = None
            for left, right, turn in zip(lefts, refs[pairs:], turned):
                part = dot_nt(left, right[cols]) if turn else dot(left, right[:, cols])
                total = part if total is None else total + part
            out[:, cols] = total.astype(B16)


def summed_dots(width, *pairs):
    lefts, rights, specs, turned, work = [], [], [], [], 0
    near = lax.axis_size("near")
    for left, right in pairs:
        span, depth = left.shape
        lefts.append(left.reshape(near, 2, span // near // 2, depth))
        turned.append(isinstance(right, tuple))
        array, at = right if turned[-1] else (right, 0)
        shape = (width, depth) if turned[-1] else array.shape
        specs.append(pl.BlockSpec(shape, lambda i, at=at: (0, at)))
        rights.append(array)
        work += 2 * span * width * depth
    smem = pl.BlockSpec(memory_space=pltpu.SMEM)
    wholes = [pl.BlockSpec(a.shape, lambda i: (0, 0, 0, 0)) for a in lefts]
    shape = (lefts[0].shape[0] * lefts[0].shape[2], width)
    return pl.pallas_call(
        functools.partial(dots_kernel, turned),
        grid=(1,),
        in_specs=[smem, *wholes, *specs],
        out_specs=[pl.BlockSpec(shape, lambda i: (0, 0))] * 2,
        out_shape=[jax.ShapeDtypeStruct(shape, B16)] * 2,
        cost_estimate=pl.CostEstimate(flops=0, bytes_accessed=0, transcendentals=0),
        compiler_params=pltpu.CompilerParams(vmem_limit_bytes=VMEM_LIMIT),
    )(lax.axis_index("head").astype(jnp.int32).reshape(1), *lefts, *rights)


def grads_kernel(count, *refs):
    *refs, out = refs
    at = 0
    for left, right in zip(refs[:count], refs[count:]):
        cols = slice(at, at + right.shape[1])
        out[:, cols] = dot_tn(left[...], right[...]).astype(B16)
        at = cols.stop


def joined_grads(*pairs):
    lefts, rights = zip(*pairs)
    span, width = lefts[0].shape
    total = sum(r.shape[1] for r in rights)
    tile = min(width, 512)
    return pl.pallas_call(
        functools.partial(grads_kernel, len(pairs)),
        grid=(width // tile,),
        in_specs=[pl.BlockSpec((span, tile), lambda i: (0, i))] * len(pairs)
        + [pl.BlockSpec(r.shape, lambda i: (0, 0)) for r in rights],
        out_specs=pl.BlockSpec((tile, total), lambda i: (i, 0)),
        out_shape=jax.ShapeDtypeStruct((width, total), B16),
        cost_estimate=pl.CostEstimate(flops=0, bytes_accessed=0, transcendentals=0),
        compiler_params=pltpu.CompilerParams(vmem_limit_bytes=VMEM_LIMIT),
    )(*lefts, *rights)


def meet_kernel(index, keep, got, *outs):
    rows = outs[0].shape[0]
    for k, out in enumerate(outs):
        part = pl.ds(pl.multiple_of(index[k] * rows, rows), rows)
        out[...] = (keep[part].astype(F32) + got[part].astype(F32)).astype(B16)


def partial_tokens(width, pairs):
    return met_tokens(*summed_dots(width, *pairs))


def met_tokens(give, keep):
    places = near_places()
    got = swap_cores(give)
    rows, width = keep.shape[0] // len(places), keep.shape[1]
    shapes = [jax.ShapeDtypeStruct((rows, width), B16)] * len(places)
    index = jnp.stack(places).astype(jnp.int32)
    return whole_call(meet_kernel, shapes, [], index, keep, got)


def scatter_tokens(blocks, alongside=None):
    blocks = [to_near(b, k) if k else b for k, b in enumerate(blocks)]
    if alongside is not None:
        blocks, alongside = lax.optimization_barrier((blocks, alongside))
    return added(blocks), alongside


def dot(left, right, dims=((1,), (0,))):
    return lax.dot_general(left, right, (dims, ((), ())), preferred_element_type=F32)


def dot_nt(left, right):
    return dot(left, right, ((1,), (1,)))


def dot_tn(left, right):
    return dot(left, right, ((0,), (0,)))


def dot_exact(left, right, dims=((1,), (0,))):
    return lax.dot_general(
        left, right, (dims, ((), ())), precision=HIGHEST, preferred_element_type=F32
    )


def normalize(values, gain):
    factor = lax.rsqrt(jnp.mean(values * values, -1, keepdims=True) + EPS)
    unit = values * factor
    return unit * gain, unit, factor


def norm_back(grad_out, unit, factor, gain):
    grad_unit = grad_out * gain[None, :]
    grad_in = factor * (grad_unit - unit * jnp.mean(grad_unit * unit, -1, keepdims=True))
    return grad_in, jnp.sum(grad_out * unit, 0)


def rotate_pair(first, second, cosine, sine):
    return first * cosine - second * sine, second * cosine + first * sine


def conv(inputs, edge, weight, bias, dim):
    length = inputs.shape[dim]
    padded = jnp.concatenate([edge, inputs], dim)
    total = bias
    for tap in range(CONV):
        total = total + weight[tap] * lax.slice_in_dim(padded, tap, tap + length, axis=dim)
    return total


def conv_back(grad, grad_edge, weight, dim):
    length = grad.shape[dim]
    late = jnp.concatenate([grad, grad_edge], dim)
    total = 0.0
    for tap in range(CONV):
        back = CONV - 1 - tap
        total = total + weight[tap] * lax.slice_in_dim(late, back, back + length, axis=dim)
    return total


def taps_back(grad, inputs, edge, dim):
    length = inputs.shape[dim]
    padded = jnp.concatenate([edge, inputs], dim)
    taps = []
    for tap in range(CONV):
        taps.append(jnp.sum(grad * lax.slice_in_dim(padded, tap, tap + length, axis=dim), dim))
    return jnp.stack(taps), jnp.sum(grad, dim)


def silu_slope(v):
    s = jax.nn.sigmoid(v)
    return s * (1.0 + v * (1.0 - s))


def row_block(i):
    return slice(i * ATTEND_ROWS, (i + 1) * ATTEND_ROWS)


def attend_kernel(index, q, *refs):
    *parts, out, lse, k_t, v_t, total, top, mass = refs
    span = q.shape[0]
    wide = min(ATTEND_KEYS, span)
    keys = HEAD_DIM // len(parts)
    half = keys // 2

    @pl.loop(0, index[0] + 1)
    def _(r):
        for k, part in enumerate(parts):
            at = pl.multiple_of(index[k + 1] * half, half)
            own = pl.multiple_of(r * 2 * keys, 2 * keys)
            k_t[r, pl.ds(at, half)] = part[pl.ds(own, half)]
            k_t[r, pl.ds(at + HEAD_DIM // 2, half)] = part[pl.ds(own + half, half)]
            at = pl.multiple_of(index[k + 1] * keys, keys)
            v_t[r, pl.ds(at, keys)] = part[pl.ds(own + keys, keys)]

    @pl.loop(index[0] + 1, k_t.shape[0])
    def _(r):
        k_t[r] = jnp.zeros(k_t.shape[1:], B16)
        v_t[r] = jnp.zeros(v_t.shape[1:], B16)

    def meet(i, keys_t, values_t, first):
        scores = dot(q[row_block(i)], keys_t) * HEAD_DIM**-0.5
        if first:
            rows = i * ATTEND_ROWS + lax.broadcasted_iota(jnp.int32, scores.shape, 0)
            cols = lax.broadcasted_iota(jnp.int32, scores.shape, 1)
            scores = jnp.where(cols <= rows, scores, MASKED)
        peak = jnp.max(scores, 1, keepdims=True)
        if not first:
            old = top[row_block(i)]
            peak = jnp.maximum(old, peak)
            fade = jnp.exp(old - peak)
        probs = jnp.exp(scores - peak)
        weight = jnp.sum(probs, 1, keepdims=True)
        read = dot_nt(probs.astype(B16), values_t)
        if not first:
            weight = weight + fade * mass[row_block(i)]
            read = read + fade * total[row_block(i)]
        top[row_block(i)] = peak
        mass[row_block(i)] = weight
        total[row_block(i)] = read

    for i in range(span // ATTEND_ROWS):
        keys = (i + 1) * ATTEND_ROWS
        meet(i, k_t[0, :, :keys], v_t[0, :, :keys], True)

    @pl.loop(1, index[0] + 1)
    def _(r):
        for j in range(span // wide):
            keys_t = k_t[r, :, j * wide : (j + 1) * wide]
            values_t = v_t[r, :, j * wide : (j + 1) * wide]
            for i in range(span // ATTEND_ROWS):
                meet(i, keys_t, values_t, False)

    out[...] = total[...] / mass[...]
    lse[...] = top[...] + jnp.log(mass[...])


def whole_call(kernel, out_shape, scratch, index, *operands):
    def whole(array):
        return pl.BlockSpec(array.shape, lambda i: (0,) * len(array.shape))

    return pl.pallas_call(
        kernel,
        grid=(1,),
        out_shape=out_shape,
        in_specs=[pl.BlockSpec(memory_space=pltpu.SMEM), *map(whole, operands)],
        out_specs=jax.tree.map(whole, out_shape),
        scratch_shapes=scratch,
        cost_estimate=pl.CostEstimate(flops=0, bytes_accessed=0, transcendentals=0),
        compiler_params=pltpu.CompilerParams(vmem_limit_bytes=VMEM_LIMIT),
    )(index, *operands)


def attend(index, queries, parts):
    span, groups = queries.shape[0], lax.axis_size("group")
    shape = jax.ShapeDtypeStruct
    turned = shape((groups, HEAD_DIM, span), B16)
    column = pltpu.VMEM((span, 1), F32)
    return whole_call(
        attend_kernel,
        (shape((span, HEAD_DIM), F32), shape((span, 1), F32), turned, turned),
        [pltpu.VMEM((span, HEAD_DIM), F32), column, column],
        index,
        queries,
        *parts,
    )


def attend_back_kernel(index, q, q_t, d, d_t, k_t, v_t, lse, delta, grad_q, *refs):
    *outs, sum_k, sum_v = refs
    span = q.shape[0]
    keys = HEAD_DIM // len(outs)
    half = keys // 2
    wide = min(ATTEND_KEYS, span)
    blocks = span // ATTEND_ROWS

    def meet(i, keys_t, values_t, offset, total_q):
        part = row_block(i)
        scores = dot(q[part], keys_t) * HEAD_DIM**-0.5
        if offset is not None:
            rows = i * ATTEND_ROWS + lax.broadcasted_iota(jnp.int32, scores.shape, 0)
            cols = offset + lax.broadcasted_iota(jnp.int32, scores.shape, 1)
            scores = jnp.where(cols <= rows, scores, MASKED)
        probs = jnp.exp(scores - lse[part])
        grad_scores = (probs * (dot(d[part], values_t) - delta[part])).astype(B16)
        update = dot_nt(grad_scores, keys_t)
        grad_q[part] = update if total_q is None else grad_q[part] + update
        return dot(q_t[:, part], grad_scores), dot(d_t[:, part], probs.astype(B16))

    def store(r, cols, pair):
        sum_k[...] = (pair[0] * HEAD_DIM**-0.5).astype(B16)
        sum_v[...] = pair[1].astype(B16)
        for k, out in enumerate(outs):
            at = pl.multiple_of(index[k + 1] * half, half)
            own = r * 2 * keys if isinstance(r, int) else pl.multiple_of(r * 2 * keys, 2 * keys)
            out[pl.ds(own, half), cols] = sum_k[pl.ds(at, half)]
            out[pl.ds(own + half, half), cols] = sum_k[pl.ds(at + HEAD_DIM // 2, half)]
            at = pl.multiple_of(index[k + 1] * keys, keys)
            out[pl.ds(own + keys, keys), cols] = sum_v[pl.ds(at, keys)]

    for j in range(span // wide):
        cols = slice(j * wide, (j + 1) * wide)
        pair = None
        for i in range(j * wide // ATTEND_ROWS, blocks):
            more = meet(i, k_t[0, :, cols], v_t[0, :, cols], j * wide, None if j == 0 else True)
            pair = more if pair is None else (pair[0] + more[0], pair[1] + more[1])
        store(0, cols, pair)

    @pl.loop(1, index[0] + 1)
    def _(r):
        for j in range(span // wide):
            cols = slice(j * wide, (j + 1) * wide)
            pair = None
            for i in range(blocks):
                more = meet(i, k_t[r, :, cols], v_t[r, :, cols], None, True)
                pair = more if pair is None else (pair[0] + more[0], pair[1] + more[1])
            store(r, cols, pair)

    @pl.loop(index[0] + 1, k_t.shape[0])
    def _(r):
        for out in outs:
            own = pl.ds(pl.multiple_of(r * 2 * keys, 2 * keys), 2 * keys)
            out[own] = jnp.zeros((2 * keys, span), B16)


def attend_back(index, queries, keys_t, values_t, grad, lse, delta):
    span, groups = queries.shape[0], keys_t.shape[0]
    near = lax.axis_size("near")
    shape = jax.ShapeDtypeStruct
    part = shape((groups * 2 * HEAD_DIM // near, span), B16)
    wide = pltpu.VMEM((HEAD_DIM, min(ATTEND_KEYS, span)), B16)
    grad_q, *parts = whole_call(
        attend_back_kernel,
        (shape(queries.shape, F32), *[part] * near),
        [wide, wide],
        index,
        queries,
        queries.T,
        grad,
        grad.T,
        keys_t,
        values_t,
        lse,
        delta,
    )
    return grad_q, parts


def in_two(x):
    high = x.astype(B16)
    return high, (x - high.astype(F32)).astype(B16)


def dot_half(low, x, dims=((1,), (0,))):
    high, rest = in_two(x)
    return dot(low, high, dims) + dot(low, rest, dims)


def dot_fine(left, right, dims=((1,), (0,))):
    high, rest = in_two(left)
    other, more = in_two(right)
    return dot(high, other, dims) + (dot(high, more, dims) + dot(rest, other, dims))


def spread(per_head, of_head):
    return dot_exact(per_head, of_head, ((0,), (0,)))


def head_decay(cum, cum_t, h):
    length = cum.shape[0]
    rows = lax.broadcasted_iota(jnp.int32, (length, length), 0)
    cols = lax.broadcasted_iota(jnp.int32, (length, length), 1)
    gap = cum[:, h : h + 1] - cum_t[h : h + 1, :]
    return jnp.exp(jnp.where(cols <= rows, gap, MASKED))


def in_head(shape, h, channels):
    lane = lax.broadcasted_iota(jnp.int32, shape, 1)
    return (lane >= h * channels) & (lane < (h + 1) * channels)


def scan_kernel(heads, x, dt, cum, cum_t, b_t, c_t, of_head, y, ends, state):
    @pl.when(pl.program_id(0) == 0)
    def _():
        state[...] = jnp.zeros_like(state)

    channels = x.shape[1] // heads
    per = HEAD_DIM // channels
    owner = of_head[...]
    cums, cums_t = cum[...], cum_t[...]
    scaled = x[...] * spread(dt[...], owner)
    inner = dot_tn(c_t[...], b_t[...])
    wide = spread(cums_t, owner)
    end = wide[-1:]
    carried = dot_half(c_t[...], state[...], ((0,), (0,))) * jnp.exp(wide)
    for at in range(heads // per):
        lanes = slice(at * HEAD_DIM, (at + 1) * HEAD_DIM)
        block = scaled[:, lanes]
        within = None
        for k in range(per):
            mixing = head_decay(cums, cums_t, at * per + k) * inner
            part = dot_fine(mixing, block)
            mine = in_head(part.shape, k, channels)
            within = part if within is None else jnp.where(mine, part, within)
        y[:, lanes] = within + carried[:, lanes]
    state[...] = jnp.exp(end) * state[...] + dot_half(b_t[...], scaled * jnp.exp(end - wide))
    ends[0] = state[...]


class ChunkSpecs:
    def __init__(self, rows, chunks, turned):
        self.rows, self.chunks = rows, chunks
        self.chunk = (lambda c: chunks - 1 - c) if turned else (lambda c: c)

    def by_row(self, width):
        return pl.BlockSpec((self.rows, width), lambda c: (self.chunk(c), 0))

    def by_col(self, height):
        return pl.BlockSpec((height, self.rows), lambda c: (0, self.chunk(c)))

    def stacked(self, array, more=0):
        shape = (1, *array.shape[1:])
        return pl.BlockSpec(shape, lambda c: (jnp.maximum(self.chunk(c) + more, 0), 0, 0))

    def whole(self, array):
        return pl.BlockSpec(array.shape, lambda c: (0,) * len(array.shape))


def chunk_call(kernel, chunks, in_specs, out_specs, out_shape, scratch, *operands):
    return pl.pallas_call(
        kernel,
        grid=(chunks,),
        in_specs=in_specs,
        out_specs=out_specs,
        out_shape=out_shape,
        scratch_shapes=scratch,
        cost_estimate=pl.CostEstimate(flops=0, bytes_accessed=0, transcendentals=0),
        compiler_params=pltpu.CompilerParams(vmem_limit_bytes=VMEM_LIMIT),
    )(*operands)


def scan_forward(heads, x, dt, cum, cum_t, b_t, c_t, of_head, rows):
    span, inner = x.shape
    chunks, padded = span // rows, dt.shape[0]
    at = ChunkSpecs(rows, chunks, False)
    ends = jax.ShapeDtypeStruct((chunks, STATE, inner), F32)
    return chunk_call(
        functools.partial(scan_kernel, heads),
        chunks,
        [
            at.by_row(inner),
            at.by_col(padded),
            at.by_row(padded),
            at.by_col(padded),
            at.by_col(STATE),
            at.by_col(STATE),
            at.whole(of_head),
        ],
        [at.by_row(inner), at.stacked(ends)],
        [jax.ShapeDtypeStruct((span, inner), F32), ends],
        [pltpu.VMEM((STATE, inner), F32)],
        x,
        dt,
        cum,
        cum_t,
        b_t,
        c_t,
        of_head,
    )


def within_kernel(heads, x, dt, cum, cum_t, b_t, c_t, of_head, ends, through, entering, grad, *outs):
    within, grad_bt, grad_ct = outs
    channels = x.shape[1] // heads
    per = HEAD_DIM // channels
    owner = of_head[...]
    cums, cums_t = cum[...], cum_t[...]
    scaled = x[...] * spread(dt[...], owner)
    inner = dot_tn(c_t[...], b_t[...])
    back = grad[...]
    faded = back * jnp.exp(spread(cums_t, owner))
    grad_inner = jnp.zeros_like(inner)
    for at in range(heads // per):
        lanes = slice(at * HEAD_DIM, (at + 1) * HEAD_DIM)
        total = None
        for k in range(per):
            decay = head_decay(cums, cums_t, at * per + k)
            part = dot_fine(decay * inner, back[:, lanes], ((0,), (0,)))
            mine = in_head(part.shape, k, channels)
            total = part if total is None else jnp.where(mine, part, total)
            only = jnp.where(mine, back[:, lanes], 0.0)
            grad_inner += dot_fine(only, scaled[:, lanes], ((1,), (1,))) * decay
        within[:, lanes] = total
    state_in = through[0] * entering[...]
    state_in = state_in + jnp.where(pl.program_id(0) == 0, 0.0, ends[0])
    grad_ct[...] = (
        dot_half(b_t[...], grad_inner, ((1,), (1,))) + dot_fine(state_in, faded, ((1,), (1,)))
    ).astype(B16)
    grad_bt[...] = dot_half(c_t[...], grad_inner)


def scan_within(heads, x, dt, cum, cum_t, b_t, c_t, of_head, ends, through, entering, grad, rows):
    span, inner = x.shape
    chunks, padded = span // rows, dt.shape[0]
    at = ChunkSpecs(rows, chunks, False)
    shape = jax.ShapeDtypeStruct
    return chunk_call(
        functools.partial(within_kernel, heads),
        chunks,
        [
            at.by_row(inner),
            at.by_col(padded),
            at.by_row(padded),
            at.by_col(padded),
            at.by_col(STATE),
            at.by_col(STATE),
            at.whole(of_head),
            at.stacked(ends, -1),
            at.stacked(through),
            at.whole(entering),
            at.by_row(inner),
        ],
        [at.by_row(inner), at.by_col(STATE), at.by_col(STATE)],
        [shape((span, inner), F32), shape((STATE, span), F32), shape((STATE, span), B16)],
        [],
        x,
        dt,
        cum,
        cum_t,
        b_t,
        c_t,
        of_head,
        ends,
        through,
        entering,
        grad,
    )


def across_kernel(
    x,
    x_pre,
    dt,
    cum_t,
    b_t,
    c_t,
    of_head,
    skip,
    ends,
    through,
    entering,
    y,
    grad,
    within,
    bt_part,
    leaving,
    grad_xpre,
    grad_bt,
    grad_logs,
    grad_dt,
    grad_skip,
    grad_state,
):
    @pl.when(pl.program_id(0) == 0)
    def _():
        grad_state[...] = leaving[...]
        grad_skip[...] = jnp.zeros_like(grad_skip)

    owner = of_head[...]
    low_owner = owner.astype(B16)
    times = spread(dt[...], owner)
    values = x[...]
    scaled = values * times
    wide = spread(cum_t[...], owner)
    end = wide[-1:]
    tail = jnp.exp(end - wide)
    back = grad[...]
    to_state = grad_state[...]
    grad_scaled = within[...] + tail * dot_half(b_t[...], to_state, ((0,), (0,)))
    grad_bt[...] = (bt_part[...] + dot_fine(to_state, scaled * tail, ((1,), (1,)))).astype(B16)
    grad_xpre[...] = (grad_scaled * times + skip[...] * back) * silu_slope(x_pre[...])
    grad_skip[...] += jnp.sum(back * values, 0, keepdims=True)
    state_out = ends[0] + through[0] * entering[...]
    at_end = jnp.sum(state_out * to_state, 0, keepdims=True)
    change = back * y[...] - grad_scaled * scaled
    rows = lax.broadcasted_iota(jnp.int32, change.shape, 0)
    change = change + jnp.where(rows == change.shape[0] - 1, at_end, 0.0)
    per_head = dot_half(low_owner, change, ((1,), (1,)))
    length = change.shape[0]
    later = lax.broadcasted_iota(jnp.int32, (length, length), 0) >= lax.broadcasted_iota(
        jnp.int32, (length, length), 1
    )
    grad_logs[...] = dot_exact(per_head, later.astype(F32))
    grad_dt[...] = dot_half(low_owner, grad_scaled * values, ((1,), (1,)))
    faded = back * jnp.exp(wide)
    grad_state[...] = jnp.exp(end) * to_state + dot_half(c_t[...], faded)


def scan_across(
    x,
    x_pre,
    dt,
    cum_t,
    b_t,
    c_t,
    of_head,
    skip,
    ends,
    through,
    entering,
    y,
    grad,
    within,
    bt_part,
    leaving,
    rows,
):
    span, inner = x.shape
    chunks, padded = span // rows, dt.shape[0]
    at = ChunkSpecs(rows, chunks, True)
    shape = jax.ShapeDtypeStruct
    return chunk_call(
        across_kernel,
        chunks,
        [
            at.by_row(inner),
            at.by_row(inner),
            at.by_col(padded),
            at.by_col(padded),
            at.by_col(STATE),
            at.by_col(STATE),
            at.whole(of_head),
            at.whole(skip),
            at.stacked(ends),
            at.stacked(through, 1),
            at.whole(entering),
            at.by_row(inner),
            at.by_row(inner),
            at.by_row(inner),
            at.by_col(STATE),
            at.whole(leaving),
        ],
        [
            at.by_row(inner),
            at.by_col(STATE),
            at.by_col(padded),
            at.by_col(padded),
            at.whole(skip),
        ],
        [
            shape((span, inner), F32),
            shape((STATE, span), B16),
            shape((padded, span), F32),
            shape((padded, span), F32),
            shape(skip.shape, F32),
        ],
        [pltpu.VMEM((STATE, inner), F32)],
        x,
        x_pre,
        dt,
        cum_t,
        b_t,
        c_t,
        of_head,
        skip,
        ends,
        through,
        entering,
        y,
        grad,
        within,
        bt_part,
        leaving,
    )


def flat(x):
    return with_layout_constraint(x, Layout(tuple(range(x.ndim))))


def cotangent_half(cotangent):
    return own_half(cotangent).astype(F32)


def home_kernel(runs, index, *refs):
    blocks, outs = refs[: -len(runs)], refs[-len(runs) :]
    for k, block in enumerate(blocks):
        at = 0
        for out, (width, across) in zip(outs, runs):
            piece = block[:, at : at + width].astype(F32)
            at += width
            place = pl.ds(pl.multiple_of(index[k] * width, width), width)
            if across:
                out[:, place] = piece
            else:
                out[place] = piece.T


def homed(blocks, *runs):
    count, piece = len(blocks), blocks[0].shape[0]
    shapes = [(piece, count * w) if across else (count * w, piece) for w, across in runs]
    shapes = [jax.ShapeDtypeStruct(shape, F32) for shape in shapes]
    index = jnp.stack(near_places()).astype(jnp.int32)
    return whole_call(functools.partial(home_kernel, runs), shapes, [], index, *blocks)


def per_device(
    tokens,
    cotangent,
    g1,
    w_q,
    w_k,
    w_v,
    w_o,
    w_z,
    w_x,
    w_bc,
    w_dt,
    conv_bc,
    conv_bc_bias,
    w_out,
    g2,
    w_gate,
    w_up,
    w_down,
    conv_x,
    conv_x_bias,
    dt_bias,
    a_log,
    d_skip,
):
    near, groups = lax.axis_size("near"), lax.axis_size("group")
    here, group, core = (lax.axis_index(a) for a in ("near", "group", "head"))
    rows, width = tokens.shape
    span = near * rows
    piece = w_q.shape[0]
    devices = near * groups
    key_cols = HEAD_DIM // near
    half_cols = key_cols // 2
    heads = w_dt.shape[1] // near
    padded = heads + -heads % 8
    inner, q_cols, ff = w_z.shape[1] // near, w_q.shape[1] // near, w_gate.shape[1] // near
    o_rows = w_o.shape[0] // near
    at_q = 2 * inner // q_cols

    def columns(w):
        return w.reshape(w.shape[0], near, -1).transpose(1, 0, 2)

    def share(x, dim):
        size = x.shape[dim] // near
        return lax.dynamic_slice_in_dim(x, here * size, size, dim)

    def by_head(x):
        return jnp.pad(share(x, 0).astype(F32), (0, padded - heads))[:, None]

    k_cols = w_k.reshape(piece, 2, near, half_cols).transpose(2, 0, 1, 3)
    w_bc_mine = lax.dynamic_slice_in_dim(w_bc, core * STATE, STATE, 1)
    pack1 = [columns(w_x), k_cols.reshape(near, piece, key_cols), columns(w_v)]
    pack1 = jnp.concatenate([*pack1, columns(w_bc_mine)], 2)
    extra = jnp.concatenate([g1, g2, conv_bc.reshape(-1), conv_bc_bias])
    n_small, n_dt = extra.shape[0], heads * piece
    extra = jnp.broadcast_to(extra, (near, n_small))
    extra = jnp.concatenate([extra, w_dt.T.reshape(near, n_dt)], 1)
    extra = jnp.pad(extra, ((0, 0), (0, -extra.shape[1] % (8 * pack1.shape[2]))))
    pack1 = jnp.concatenate([pack1, extra.reshape(near, -1, pack1.shape[2])], 1)
    halo = step_group(tokens[rows - 16 :], 1)
    pack1 = after(pack1, halo)
    full1 = jnp.broadcast_to(pack1, (groups, *pack1.shape)).reshape(devices, *pack1.shape[1:])
    full1 = trade_all(full1)
    token_parts = sent_tokens(jnp.concatenate([own_half(tokens), halo], 0))
    pack2 = [columns(w_z), columns(w_out.T), columns(w_q), columns(w_o.T)]
    pack2 = jnp.concatenate(pack2, 2)
    pack3 = jnp.concatenate([columns(w_gate), columns(w_up), columns(w_down.T)], 2)
    pack2, *token_parts[:near] = lax.optimization_barrier((pack2, *token_parts[:near]))
    sent2 = sent_near(pack2)
    positions = (group * span + jnp.arange(span)).astype(F32)
    half = HEAD_DIM // 2
    freqs = ROPE_BASE ** (-jnp.arange(half, dtype=F32) / half)
    angle = positions[:, None] * freqs[None, :]
    cos_q, sin_q = jnp.cos(angle), jnp.sin(angle)
    cos_k, sin_k = (share(x, 1).T for x in (cos_q, sin_q))
    of_head = jnp.arange(inner)[None, :] // (inner // heads) == jnp.arange(padded)[:, None]
    of_head = of_head.astype(F32)
    decay_rate, head_bias = jnp.exp(by_head(a_log)), by_head(dt_bias)
    skip = spread(by_head(d_skip), of_head)
    triangle = jnp.triu(jnp.ones((rows, rows), F32))
    taps_x = share(conv_x, 1).astype(F32)[:, None, :]
    bias_x = share(conv_x_bias, 0).astype(F32)[None, :]
    my_tokens = own_half(tokens).astype(F32)
    early = (cos_q, sin_q, cos_k, sin_k, of_head, decay_rate, head_bias, skip, triangle)
    early = (*early, taps_x, bias_x, my_tokens, pack3)
    full1, early = lax.optimization_barrier((full1, early))
    cos_q, sin_q, cos_k, sin_k, of_head, decay_rate, head_bias, skip, triangle = early[:9]
    taps_x, bias_x, my_tokens, pack3 = early[9:]

    extra = full1[:, piece:].reshape(devices, -1)
    smalls = extra[:, :n_small].astype(F32)
    gain1 = smalls[:, :piece].reshape(-1)
    gain2 = smalls[:, piece : 2 * piece].reshape(-1)
    full_dt = extra[:, n_small : n_small + n_dt].reshape(devices, heads, piece)
    full_dt = full_dt.transpose(1, 0, 2).reshape(heads, width)
    full_dt = jnp.pad(full_dt, ((0, padded - heads), (0, 0)))
    taps_bc = smalls[:, 2 * piece : -conv_bc_bias.shape[0]].reshape(devices, CONV, -1)
    taps_bc = taps_bc.transpose(1, 0, 2).reshape(CONV, 2, near, -1)
    taps_bc = taps_bc[:, core, here][:, :, None]
    bias_bc = smalls[:, -conv_bc_bias.shape[0] :].reshape(2, near, -1)[core, here][:, None]
    full1 = full1[:, :piece].reshape(width, -1)
    full_x, full_kvbc = full1[:, :inner], full1[:, inner:]
    n1, halo = normed_tokens(token_parts, gain1, 16)
    edge = dot(halo, full1)[17 - CONV :]
    x_edge, bc_edge = edge[:, :inner], edge[:, inner + 2 * key_cols :].T
    grad_parts = sent_tokens(after(own_half(cotangent), n1))

    kvbc = dot(full_kvbc, n1, ((0,), (1,)))
    k_first, k_second = rotate_pair(kvbc[:half_cols], kvbc[half_cols:key_cols], cos_k, sin_k)
    kv = jnp.concatenate([k_first, k_second, kvbc[key_cols : 2 * key_cols]], 0).astype(B16)
    kv = flat(kv)
    kv_parts = [kv] + [step_group(kv, r) for r in range(1, groups)]
    bc_proj = flat(kvbc[2 * key_cols :])
    sent2, n1, kv = lax.optimization_barrier((sent2, n1, kv))
    full2 = placed(near_places(), sent2).reshape(near * piece, -1)
    n1_x, full2 = lax.optimization_barrier((n1, full2))
    full2 = lax.all_gather(full2, "group", axis=0, tiled=True)

    x_proj = dot(n1_x, full_x)
    sent3 = sent_near(after(pack3, x_proj))

    bc_pre = conv(bc_proj, bc_edge, taps_bc, bias_bc, 1)
    bc_mine = gather_near(flat(jax.nn.silu(bc_pre).astype(B16))).reshape(STATE, span)
    bc_other = swap_cores(bc_mine)
    first = core == 0
    b_t, c_t = jnp.where(first, bc_mine, bc_other), jnp.where(first, bc_other, bc_mine)

    dt_pre = dot_nt(full_dt, n1) + head_bias
    dt = jax.nn.softplus(dt_pre)
    logs = -dt * decay_rate
    cum_t = dot_exact(logs.reshape(padded * near, rows), triangle).reshape(padded, near, rows)
    chunk_total = cum_t[:, :, -1]
    before = jnp.cumsum(chunk_total, 1) - chunk_total
    group_total = jnp.sum(chunk_total, 1, keepdims=True)
    fade = jnp.exp(spread((cum_t + before[:, :, None]).reshape(padded, span), of_head))
    cum_t = cum_t.reshape(padded, span)
    cum = cum_t.T
    group_decay = jnp.exp(spread(group_total, of_head))

    x_pre = conv(x_proj, x_edge, taps_x, bias_x, 0)
    xc = jax.nn.silu(x_pre)
    kv_parts = jnp.concatenate(kv_parts, 0)
    xc = after(xc, kv_parts, *grad_parts)
    sent3, xc = lax.optimization_barrier((sent3, xc))
    full3 = placed(near_places(), sent3).reshape(near * piece, -1)
    xc, full3 = lax.optimization_barrier((xc, full3))
    full3 = lax.all_gather(full3, "group", axis=0, tiled=True)
    kv_parts = [to_near(kv_parts, k) if k else kv_parts for k in range(near)]
    outputs, ends = scan_forward(heads, xc, dt, cum, cum_t, b_t, c_t, of_head, rows)
    through = jnp.concatenate([jnp.zeros_like(group_total), jnp.cumsum(chunk_total, 1)], 1)
    through = jnp.exp(spread(through, of_head))[:, None]

    def state_rows(state):
        pad = jnp.broadcast_to(group_decay, (16, inner))
        return jnp.concatenate([state, pad], 0).astype(B16)

    def sent_states(state, direction):
        return [step_group(state, direction * r) for r in range(1, groups)]

    def chained(parts):
        total = jnp.zeros((STATE, inner), F32)
        for part in reversed(parts):
            part = part.astype(F32)
            total = part[STATE : STATE + 1] * total + part[:STATE]
        return total

    entering = sent_states(state_rows(ends[-1]), 1)
    full_z, full_out_t = full2[:, :inner], full2[:, inner : 2 * inner]
    full_q, full_o_t = full2[:, 2 * inner : 2 * inner + q_cols], full2[:, 2 * inner + q_cols :]
    full_gu, full_down_t = full3[:, : 2 * ff], full3[:, 2 * ff :]
    q_proj = dot(n1, full_q)
    queries = jnp.concatenate(rotate_pair(q_proj[:, :half], q_proj[:, half:], cos_q, sin_q), 1)
    queries = queries.astype(B16)
    z_proj = dot(n1, full_z)
    index = jnp.stack([group, *near_places()]).astype(jnp.int32)
    attended32, lse, keys_t, values_t = attend(index, queries, kv_parts)
    attended = attended32.astype(B16)
    entering = chained(after(entering, attended, z_proj))

    outputs = outputs + fade * dot_tn(c_t, entering.astype(B16))
    y = outputs + skip * xc
    gated = (y * jax.nn.silu(z_proj)).astype(B16)

    pairs = [(gated, (full2, 1)), (attended, (full2, at_q + 1))]
    blocks = partial_tokens(width, pairs)
    all_cotangent = placed_tokens(after(grad_parts, blocks))
    mixed, all_cotangent = scatter_tokens(blocks, alongside=all_cotangent)
    hidden = my_tokens + mixed
    normed2, unit2, factor2 = normalize(hidden, gain2)
    n2 = gather_tokens(normed2.astype(B16))
    both = dot(n2, full_gu)
    gate, up = both[:, :ff], both[:, ff:]
    sigma = jax.nn.sigmoid(gate)
    act = (gate * sigma * up).astype(B16)
    grad_act = dot(all_cotangent, full_down_t)
    grad_gate = grad_act * up * sigma * (1.0 + gate * (1.0 - sigma))
    grad_gu = jnp.concatenate([grad_gate, grad_act * gate * sigma], 1).astype(B16)

    def sum_groups(grad):
        own = lax.psum_scatter(grad, "group", scatter_dimension=0, tiled=True)
        return own.reshape(near, piece, -1)

    partial2 = partial_tokens(width, [(grad_gu, (full3, 0))])
    grads3 = dot_tn(n2, grad_gu).astype(B16)
    grad_n2, (grads3, feed) = scatter_tokens(
        partial2, alongside=(grads3, summed_dots(width, (act, (full3, 2))))
    )
    home3 = sum_groups(grads3)

    grad_norm2, grad_g2 = norm_back(grad_n2, unit2, factor2, gain2)
    grad_hidden = cotangent_half(cotangent) + grad_norm2
    grad_mixed = gather_tokens(grad_hidden.astype(B16))

    grad_gated = dot(grad_mixed, full_out_t).astype(B16).astype(F32)
    sig_z = jax.nn.sigmoid(z_proj)
    grad_y = grad_gated * z_proj * sig_z
    grad_z = (grad_gated * y * sig_z * (1.0 + z_proj * (1.0 - sig_z))).astype(B16)
    read = state_rows(dot(c_t, (grad_y * fade).astype(B16)))
    read_parts = sent_states(read, -1)

    grad_mixed = after(grad_mixed, read)
    grad_attended = dot(grad_mixed, full_o_t).astype(B16)
    delta = jnp.sum(grad_attended.astype(F32) * attended32, 1, keepdims=True)
    grad_q, kv_parts = attend_back(
        index, queries, keys_t, values_t, grad_attended, lse, delta
    )
    kv_parts = [to_near(p, k) if k else p for k, p in enumerate(kv_parts)]
    grad_q = grad_q * HEAD_DIM**-0.5
    grad_q = jnp.concatenate(rotate_pair(grad_q[:, :half], grad_q[:, half:], cos_q, -sin_q), 1)
    grad_zq = jnp.concatenate([grad_z, grad_q.astype(B16)], 1)
    mixer_out = jnp.concatenate([gated, attended], 1)
    read_parts, grad_zq = lax.optimization_barrier((read_parts, grad_zq))
    grads2 = joined_grads((all_cotangent, act), (grad_mixed, mixer_out), (n1, grad_zq))
    home2 = sum_groups(grads2)

    kv_parts, grads2 = lax.optimization_barrier((kv_parts, grads2))
    kv_parts = flat(added(kv_parts))
    kv_sent = kv_parts.astype(B16)
    kv_rows = 2 * key_cols
    grad_kv = [kv_parts[:kv_rows]]
    for r in range(1, groups):
        grad_kv.append(step_group(kv_sent[r * kv_rows : (r + 1) * kv_rows], -r))
    feed = met_tokens(*after(feed, kv_sent))

    feed, grad_y_scan = lax.optimization_barrier((feed, grad_y))
    within, bt_part, grad_ct = scan_within(
        heads, xc, dt, cum, cum_t, b_t, c_t, of_head, ends, through, entering, grad_y_scan, rows
    )
    feed = [to_near(b, k) if k else b for k, b in enumerate(feed)]
    home3 = sent_near(after(home3, kv_sent))
    read_parts, within, home3, feed = lax.optimization_barrier((read_parts, within, home3, feed))
    leaving = chained(read_parts)
    grad_xpre, grad_bt, grad_logs, grad_dt, grad_skip = scan_across(
        xc,
        x_pre,
        dt,
        cum_t,
        b_t,
        c_t,
        of_head,
        skip,
        ends,
        through,
        entering,
        outputs,
        grad_y,
        within,
        bt_part,
        leaving,
        rows,
    )
    kept = jnp.where(first, grad_bt, grad_ct)
    given = swap_cores(jnp.where(first, grad_ct, grad_bt))
    kept = (kept.astype(F32) + given.astype(F32)).astype(B16)
    grad_bc = flat(added(sent_near(kept.reshape(near, -1, span))))

    grad_bcpre = grad_bc * silu_slope(bc_pre)
    next_x = step_group(grad_xpre[: CONV - 1], -1)
    next_bc = step_group(grad_bcpre[:, : CONV - 1], -1)
    grad_x = conv_back(grad_xpre, next_x, taps_x, 0)
    grad_bcp = conv_back(grad_bcpre, next_bc, taps_bc, 1)
    grad_kv = added(after(grad_kv, grad_xpre))
    gk_first, gk_second = rotate_pair(
        grad_kv[:half_cols], grad_kv[half_cols:key_cols], cos_k, -sin_k
    )
    grad_kvbc = jnp.concatenate([gk_first, gk_second, grad_kv[key_cols:], grad_bcp], 0)
    grad_first = jnp.concatenate([grad_x.astype(B16), flat(grad_kvbc.astype(B16)).T], 1)

    grad_dt = grad_dt - grad_logs * decay_rate
    grad_dt_pre = grad_dt * jax.nn.sigmoid(dt_pre)
    grad_dt_low = grad_dt_pre.astype(B16)
    grad_skip = dot_exact(of_head, grad_skip, ((1,), (1,)))[:heads, 0]
    grad_alog = jnp.sum(grad_logs * logs, 1)[:heads]
    grad_dtbias = jnp.sum(grad_dt_pre, 1)[:heads]

    grads1 = dot_tn(n1, grad_first).astype(B16)
    grad_first, grads1 = lax.optimization_barrier((grad_first, grads1))
    grad_wdt = dot(grad_dt_low, n1).reshape(padded, devices, piece).transpose(1, 0, 2)
    pairs = [
        (grad_zq[:, :inner], (full2, 0)),
        (grad_zq[:, inner:], (full2, at_q)),
        (grad_first, (full1, 0)),
        (grad_dt_low.T, full_dt),
    ]
    partial1 = partial_tokens(width, pairs)
    grad_xpre, grad_bcpre = after((grad_xpre, grad_bcpre), partial1)
    grad_tapx, grad_biasx = taps_back(grad_xpre, x_proj, x_edge, 0)
    grad_tapbc, grad_biasbc = taps_back(grad_bcpre, bc_proj, bc_edge, 1)
    output = (hidden + added(after(feed, partial1))).astype(B16)
    output = both_halves(output, swap_cores(output), 0)
    outs3 = homed(after(home3, partial1), (ff, True), (ff, True))
    taps = grad_tapx, grad_biasx, grad_tapbc, grad_biasbc
    grad_n1, (sum_wgate, sum_wup, output, taps) = scatter_tokens(
        partial1, alongside=(*outs3, output, taps)
    )
    grad_tapx, grad_biasx, grad_tapbc, grad_biasbc = taps
    _, unit1, factor1 = normalize(my_tokens, gain1)
    grad_norm1, grad_g1 = norm_back(grad_n1, unit1, factor1, gain1)
    grad_tokens = grad_hidden + grad_norm1

    grad_tokens = both_halves(grad_tokens, swap_cores(grad_tokens), 0)

    crossing = jnp.concatenate([grad_g1, grad_g2, grad_tapbc.reshape(-1), grad_biasbc])
    other = swap_cores(crossing)
    gains = 2 * width
    mine = [grad_tapx.reshape(-1), grad_biasx, grad_dtbias, grad_alog, grad_skip]
    mine = [*mine, both_halves(crossing[gains:], other[gains:], 0)]
    ends, at = [], 0
    for g in mine[:-1]:
        at += g.shape[0]
        ends.append(at)
    packed = jnp.concatenate(mine)
    size = packed.shape[0]
    packed = jnp.broadcast_to(packed, (devices, size))
    own_parts = [crossing[:width] + other[:width], crossing[width:gains] + other[width:gains]]
    own_parts = [grad_wdt.reshape(devices, -1), *(p.reshape(devices, -1) for p in own_parts)]
    packed = jnp.concatenate([*own_parts, packed], 1)
    packed = jnp.pad(packed, ((0, 0), (0, -packed.shape[1] % (8 * HEAD_DIM))))
    packed = trade_all(packed.reshape(devices, -1, HEAD_DIM))
    home1 = grads1.reshape(groups, near * piece, -1)
    home1 = [lax.dynamic_index_in_dim(home1, (group + r) % groups, 0, False) for r in range(groups)]
    home1 = [around(b, r) if r else b for r, b in enumerate(home1)]
    home2 = sent_near(after(home2, grad_n1))
    home1, home2 = lax.optimization_barrier((home1, home2))
    home1 = sent_near(added(home1).astype(B16).reshape(near, piece, -1))
    packed, home1 = lax.optimization_barrier((packed, home1))
    packed = packed.reshape(devices, -1)
    n_dt = padded * piece
    sum_wdt = jnp.sum(packed[:, :n_dt].reshape(groups, near, padded, piece), 0)
    sum_wdt = sum_wdt[:, :heads].reshape(-1, piece).T
    own_sums = jnp.sum(packed[:, n_dt : n_dt + 2 * piece], 0)
    packed = packed[:, n_dt + 2 * piece :][:, :size]

    sum_wdown, sum_wout, sum_wo, sum_wz, sum_wq = homed(
        home2, (ff, False), (inner, False), (o_rows, False), (inner, True), (q_cols, True)
    )
    (sum_wx,) = homed(home1, (inner, True))
    home_small = placed(near_places(), [b[:, inner:] for b in home1]).astype(F32)
    home_k, home_v, home_bc = jnp.split(home_small, [key_cols, 2 * key_cols], 2)
    sum_wv = home_v.transpose(1, 0, 2).reshape(piece, -1)
    sum_wk = home_k.reshape(near, piece, 2, half_cols).transpose(1, 2, 0, 3)
    sum_wk = sum_wk.reshape(piece, -1)
    bc_mine = home_bc.transpose(1, 0, 2).reshape(piece, -1)
    sum_wbc = both_halves(bc_mine, swap_cores(bc_mine), 1)

    every = jnp.split(packed, ends, 1)
    place = group * near + here

    def by_near(x):
        return jnp.sum(x.reshape(groups, near, -1), 0)

    sum_g1, sum_g2 = own_sums[:piece], own_sums[piece:]
    sum_convx = by_near(every[0]).reshape(near, CONV, -1).transpose(1, 0, 2).reshape(CONV, -1)
    sum_convxb, sum_dtbias, sum_alog, sum_dskip = (by_near(x).reshape(-1) for x in every[1:5])
    sum_bc = by_near(every[5]).reshape(near, 2, CONV + 1, -1).transpose(2, 1, 0, 3)
    sum_bc = sum_bc.reshape(CONV + 1, -1)
    bc_cols = conv_bc.shape[1]
    sum_bc = lax.dynamic_slice_in_dim(sum_bc, place * bc_cols, bc_cols, 1)
    return (
        output,
        grad_tokens,
        sum_g1,
        sum_wq,
        sum_wk,
        sum_wv,
        sum_wo,
        sum_wz,
        sum_wx,
        sum_wbc,
        sum_wdt,
        sum_bc[:CONV],
        sum_bc[CONV],
        sum_wout,
        sum_g2,
        sum_wgate,
        sum_wup,
        sum_wdown,
        sum_convx,
        sum_convxb,
        sum_dtbias,
        sum_alog,
        sum_dskip,
    )


def solution(mesh):
    seq, cores = mesh.shape["seq"], mesh.shape["head"]
    near = math.gcd(seq, 4)
    split = Mesh(mesh.devices.reshape(seq // near, near, cores), ("group", "near", "head"))
    seq = ("group", "near")
    row_split = P(seq, "head")
    col_split = P("head", seq)
    weights = (
        P(seq),
        row_split,
        row_split,
        row_split,
        col_split,
        row_split,
        row_split,
        P(seq, None),
        row_split,
        P(None, seq),
        P(seq),
        col_split,
        P(seq),
        row_split,
        row_split,
        col_split,
        P(None, "head"),
        P("head"),
        P("head"),
        P("head"),
        P("head"),
    )
    tokens = P(seq, None)
    return jax.shard_map(
        per_device,
        mesh=split,
        in_specs=(tokens, tokens, *weights),
        out_specs=(tokens, tokens, *weights),
        check_vma=False,
    )
```
